256 devices in a mesh: seq: 64 (over x, z, core), head: 4 (over y).
Axes of the slice: x: 4, y: 4, z: 8, core: 2. Of those that a mesh axis runs over, the one named last changes fastest.
Arguments:
- token_response: int32 [16384], P('seq'), may hold values from 0 to 1023, as said below
- prompt_owner: int32 [64], replicated, may hold values from 0 to 63, each once
- queries: bfloat16 [16384, 4096], P('seq', 'head'), may hold values from -8 to 8
- resp_keys: bfloat16 [16384, 512], P('seq', 'head'), may hold values from -6 to 6
- resp_values: bfloat16 [16384, 512], P('seq', 'head'), may hold values from -6 to 6
- prompt_kv: bfloat16 [64, 2, 512, 512], P('seq', None, None, 'head'), may hold values from -8 to 8
- out_weight: bfloat16 [4096, 2048], P('head'), may hold values from -0.5 to 0.5
- out_grad: bfloat16 [16384, 2048], P('seq', 'head'), may hold values from -1.5 to 1.5
Outputs:
- layer_out: bfloat16 [16384, 2048], P('seq', 'head')
- query_grad: bfloat16 [16384, 4096], P('seq', 'head')
- key_grad: bfloat16 [16384, 512], P('seq', 'head')
- value_grad: bfloat16 [16384, 512], P('seq', 'head')
- prompt_kv_grad: float32 [64, 2, 512, 512], P('seq', None, None, 'head')
The draws below stay inside these ranges and needn't reach their ends.
Inputs may be any that keep to these rules, and one draw needn't show every extreme that they name: `token_response`: never falls along the tokens; response r belongs to prompt r // 16, and every prompt has exactly 16 responses; all tokens of a response lie on one device; the rows k * 256 to (k + 1) * 256 - 1 belong to prompts k - 1, k and k + 1 only; in every draw some device holds tokens of three prompts and 30 responses.
All inputs are finite; a program needn't handle non-finite values.
Results may differ from the reference program's by a relative error of at most 0.03.
Values may be sent and summed in bfloat16 or wider, within the bound.
A program may use at most 64 MiB of HBM per device.

```python
import jax
import jax.numpy as jnp
from jax import lax

HID = 2048
QH = 32
KVH = 4
HD = 128
GROUP = 16
RESP_DEV = 256
PLEN = 512
DRIFT = 7
PROMPTS = 64
TOKENS = 16384


def draw_token_response(key, part):
    key = jax.random.fold_in(key, 5)
    offset_key, pick_key, jitter_key = jax.random.split(key, 3)
    devices = TOKENS // RESP_DEV
    offsets = jax.random.randint(offset_key, (devices + 1,), -DRIFT, DRIFT + 1)
    chosen = jax.random.randint(pick_key, (), 1, devices - 1)
    slot_index = jnp.arange(devices + 1)
    offsets = jnp.where(slot_index == chosen, -DRIFT, offsets)
    offsets = jnp.where(slot_index == chosen + 1, DRIFT, offsets)
    offsets = jnp.where((slot_index == 0) | (slot_index == devices), 0, offsets)
    starts = GROUP * slot_index + offsets
    counts = starts[1:] - starts[:-1]
    most_cuts = GROUP + 2 * DRIFT
    cut_index = jnp.arange(most_cuts)
    jitter = jax.random.randint(jitter_key, (devices, most_cuts), -1, 2)
    cut_rows = cut_index[None, :] * RESP_DEV // counts[:, None] + jitter
    active = (cut_index[None, :] >= 1) & (cut_index[None, :] < counts[:, None])
    local_rows = jnp.arange(RESP_DEV)
    passed = active[:, None, :] & (cut_rows[:, None, :] <= local_rows[None, :, None])
    number = jnp.sum(passed.astype(jnp.int32), axis=-1)
    return (starts[:-1, None] + number).reshape(-1).astype(jnp.int32)


def draw_queries(key, part):
    key = jax.random.fold_in(key, 7)
    normal_key = jax.random.fold_in(key, 0)
    return jnp.clip(1.5 * jax.random.normal(normal_key, (TOKENS, QH * HD), jnp.float32), -8.0, 8.0).astype(jnp.bfloat16)


def draw_prompt_kv(key, part):
    key = jax.random.fold_in(key, 9)
    return jnp.clip(jax.random.normal(key, (PROMPTS, 2, PLEN, KVH * HD), jnp.float32), -6.0, 6.0).astype(jnp.bfloat16)


def levels(own_key, shape, pieces, low, high):
    factor_of, own = 1.0, jax.random.fold_in(own_key, 6)
    for position, shards_of in pieces:
        steps = jnp.exp(jax.random.uniform(jax.random.fold_in(own, position), (shards_of,), jnp.float32, low / len(pieces), high / len(pieces)))
        factor_of = factor_of * jnp.repeat(steps, shape[position] // shards_of).reshape([-1 if axis == position else 1 for axis in range(len(shape))])
    return factor_of


def normal_values(rng, shape, scale, bound, shards=(), held_as=jnp.bfloat16):
    entries = jax.random.normal(rng, shape, jnp.float32) * scale
    if len(shards) > 0:
        entries = levels(rng, shape, shards, -0.22, 0.18) * entries
    return jnp.clip(entries, min=-bound, max=bound).astype(held_as)


def setup_inputs(seed: int = 0) -> dict:
    key_of = jax.random.split(jax.random.key(seed), 9)
    token_response = draw_token_response(jax.random.fold_in(key_of[8], 71), 0)
    prompt_owner = jax.random.permutation(key_of[1], PROMPTS).astype(jnp.int32)
    queries = draw_queries(jax.random.fold_in(key_of[8], 71), 0)
    resp_keys = normal_values(key_of[3], (TOKENS, KVH * HD), 1.0, 6.0, ((0, 64), (1, 4)))
    resp_values = normal_values(key_of[4], (TOKENS, KVH * HD), 1.0, 6.0, ((0, 64), (1, 4)))
    prompt_kv = draw_prompt_kv(jax.random.fold_in(key_of[8], 71), 0)
    out_weight = normal_values(key_of[6], (QH * HD, HID), HD ** -0.5, 0.5, ((0, 4),))
    out_grad = normal_values(key_of[7], (TOKENS, HID), 0.25, 1.5, ((0, 64), (1, 4)))
    return dict(token_response=token_response, prompt_owner=prompt_owner, queries=queries, resp_keys=resp_keys, resp_values=resp_values, prompt_kv=prompt_kv, out_weight=out_weight, out_grad=out_grad)


masked_fill = -1.0e30


def group_attention(query_group, grad_group, all_keys, all_values, visible, score_scale):
    scores = jnp.einsum("rhe,ke->hrk", query_group.astype(jnp.float32), all_keys.astype(jnp.float32)) * score_scale
    scores = jnp.where(visible[None], scores, masked_fill)
    highest = jnp.max(scores, axis=-1, keepdims=True)
    expanded = jnp.exp(scores - highest)
    weights = expanded / jnp.sum(expanded, axis=-1, keepdims=True)
    weights_low = weights.astype(jnp.bfloat16)
    attended = jnp.einsum("hrk,ke->rhe", weights_low.astype(jnp.float32), all_values.astype(jnp.float32)).astype(jnp.bfloat16)
    row_dots = jnp.sum(grad_group.astype(jnp.float32) * attended.astype(jnp.float32), axis=-1)
    value_dots = jnp.einsum("rhe,ke->hrk", grad_group.astype(jnp.float32), all_values.astype(jnp.float32))
    score_grad = (weights * (value_dots - jnp.transpose(row_dots)[:, :, None]) * score_scale).astype(jnp.bfloat16)
    query_grad = jnp.einsum("hrk,ke->rhe", score_grad.astype(jnp.float32), all_keys.astype(jnp.float32)).astype(jnp.bfloat16)
    key_grad = jnp.einsum("hrk,rhe->ke", score_grad.astype(jnp.float32), query_group.astype(jnp.float32))
    value_grad = jnp.einsum("hrk,rhe->ke", weights_low.astype(jnp.float32), grad_group.astype(jnp.float32))
    return attended, query_grad, key_grad, value_grad


def reference(token_response, prompt_owner, queries, resp_keys, resp_values, prompt_kv, out_weight, out_grad):
    devices = TOKENS // RESP_DEV
    per_group = QH // KVH
    score_scale = HD ** -0.5
    by_prompt = jnp.take(prompt_kv, prompt_owner, axis=0)
    blank_row = jnp.zeros((1,) + by_prompt.shape[1:], by_prompt.dtype)
    padded = jnp.concatenate([blank_row, by_prompt, blank_row], axis=0)

    def block_step(totals, inputs):
        block, tokens, block_queries, block_keys, block_values, block_grad = inputs
        prompt_slots = lax.dynamic_slice_in_dim(padded, block, 3, 0)
        prompt_of = tokens // GROUP
        slot_prompt = block - 1 + jnp.arange(3 * PLEN, dtype=jnp.int32) // PLEN
        local_rows = jnp.arange(RESP_DEV, dtype=jnp.int32)
        same_response = (tokens[:, None] == tokens[None, :]) & (local_rows[None, :] <= local_rows[:, None])
        visible = jnp.concatenate([prompt_of[:, None] == slot_prompt[None, :], same_response], axis=1)
        attn_grad = jnp.dot(block_grad, out_weight.T, preferred_element_type=jnp.float32).astype(jnp.bfloat16)
        attended_parts, query_parts, key_parts, value_parts, prompt_key_parts, prompt_value_parts = [], [], [], [], [], []
        for head_group in range(KVH):
            lower_col = head_group * HD
            all_keys = jnp.concatenate([prompt_slots[:, 0, :, lower_col:lower_col + HD].reshape(3 * PLEN, HD), block_keys[:, lower_col:lower_col + HD]], axis=0)
            all_values = jnp.concatenate([prompt_slots[:, 1, :, lower_col:lower_col + HD].reshape(3 * PLEN, HD), block_values[:, lower_col:lower_col + HD]], axis=0)
            feature_low = head_group * per_group * HD
            query_group = block_queries[:, feature_low:feature_low + per_group * HD].reshape(RESP_DEV, per_group, HD)
            grad_group = attn_grad[:, feature_low:feature_low + per_group * HD].reshape(RESP_DEV, per_group, HD)
            attended, query_grad, key_grad, value_grad = group_attention(query_group, grad_group, all_keys, all_values, visible, score_scale)
            attended_parts.append(attended.reshape(RESP_DEV, per_group * HD))
            query_parts.append(query_grad.reshape(RESP_DEV, per_group * HD))
            key_parts.append(key_grad[3 * PLEN:])
            value_parts.append(value_grad[3 * PLEN:])
            prompt_key_parts.append(key_grad[:3 * PLEN].reshape(3, PLEN, HD))
            prompt_value_parts.append(value_grad[:3 * PLEN].reshape(3, PLEN, HD))
        attended = jnp.concatenate(attended_parts, axis=1)
        layer_out = jnp.dot(attended, out_weight, preferred_element_type=jnp.float32).astype(jnp.bfloat16)
        query_grad = jnp.concatenate(query_parts, axis=1)
        key_grad = jnp.concatenate(key_parts, axis=1).astype(jnp.bfloat16)
        value_grad = jnp.concatenate(value_parts, axis=1).astype(jnp.bfloat16)
        slot_grads = jnp.stack([jnp.concatenate(prompt_key_parts, axis=-1), jnp.concatenate(prompt_value_parts, axis=-1)], axis=1)
        current = lax.dynamic_slice_in_dim(totals, block, 3, 0)
        totals = lax.dynamic_update_slice_in_dim(totals, current + slot_grads, block, 0)
        return totals, (layer_out, query_grad, key_grad, value_grad)

    totals = jnp.zeros((devices + 2, 2, PLEN, KVH * HD), jnp.float32)
    inputs = (jnp.arange(devices, dtype=jnp.int32), token_response.reshape(devices, RESP_DEV), queries.reshape(devices, RESP_DEV, QH * HD), resp_keys.reshape(devices, RESP_DEV, KVH * HD), resp_values.reshape(devices, RESP_DEV, KVH * HD), out_grad.reshape(devices, RESP_DEV, HID))
    totals, (layer_out, query_grad, key_grad, value_grad) = lax.scan(block_step, totals, inputs)
    prompt_grad = totals[1:devices + 1]
    prompt_kv_grad = jnp.zeros_like(prompt_grad).at[prompt_owner].set(prompt_grad)
    return (layer_out.reshape(TOKENS, HID), query_grad.reshape(TOKENS, QH * HD), key_grad.reshape(TOKENS, KVH * HD), value_grad.reshape(TOKENS, KVH * HD), prompt_kv_grad)
```

```python
import functools

import jax
import jax.numpy as jnp
from jax import lax
from jax.experimental import pallas as pl
from jax.experimental.pallas import tpu as pltpu
from jax.sharding import PartitionSpec as P

GROUP = 16
TILE = 32
LOG2E = 1.4426950408889634
F32, BF16 = jnp.float32, jnp.bfloat16
MESH = pl.DeviceIdType.MESH
VMEM_LIMIT = 48 * 2**20


def dot(a, b, ca, cb):
    return lax.dot_general(a, b, (((ca,), (cb,)), ((), ())), preferred_element_type=F32)


def at_seq(j):
    return (j, lax.axis_index("head"))


def at_head(j):
    return (lax.axis_index("seq"), j)


def enter(seq, heads):
    me, mine = lax.axis_index("seq"), lax.axis_index("head")
    barrier = pltpu.get_barrier_semaphore()

    def greet(i, _):
        pl.semaphore_signal(barrier, inc=1, device_id=at_seq(lax.rem(me + i, seq)), device_id_type=MESH)
        return 0

    lax.fori_loop(1, seq, greet, 0)
    for i in range(1, heads):
        pl.semaphore_signal(barrier, inc=1, device_id=at_head(lax.rem(mine + i, heads)), device_id_type=MESH)
    pl.semaphore_wait(barrier, seq - 1 + heads - 1)


def wait_bytes(ref, sem):
    pltpu.make_async_copy(ref, ref, sem).wait()


def gather_kernel(
    seq, heads, owner, kv, og, w_hbm, slots, ag, first, order, ogs, w, sem1, sem2, sem3, sem4, wsem
):
    me, mine = lax.axis_index("seq"), lax.axis_index("head")
    load_w = pltpu.make_async_copy(w_hbm, w, wsem)
    load_w.start()
    enter(seq, heads)
    width = og.shape[1]
    og_copies = []
    for i in range(1, heads):
        peer = lax.rem(mine + i, heads)
        copy = pltpu.make_async_remote_copy(
            og, ogs.at[mine], sem4.at[0, i], sem4.at[1, heads - i], device_id=at_head(peer), device_id_type=MESH
        )
        og_copies.append(copy)

    def spread(i, _):
        j = lax.rem(me + i, seq)
        pltpu.make_async_remote_copy(
            kv.at[j], first.at[me], sem1.at[0], sem1.at[1], device_id=at_seq(j), device_id_type=MESH
        ).start()
        return 0

    lax.fori_loop(1, seq, spread, 0)
    for copy in og_copies:
        copy.start()
    first[me] = kv[me]
    ogs[mine] = og[...]
    wait_bytes(first.at[pl.ds(0, seq - 1)], sem1.at[1])

    def deliver(i, _):
        p = lax.rem(me + i, seq)
        order[p] = first[owner[p]]
        pltpu.make_async_remote_copy(
            order.at[p], slots.at[1, me], sem2.at[0], sem2.at[1], device_id=at_seq(p), device_id_type=MESH
        ).start()
        return 0

    lax.fori_loop(1, seq, deliver, 0)
    slots[1, me] = first[owner[me]]
    for copy in og_copies:
        copy.wait()
    load_w.wait()
    block = 256

    def project(n, _):
        r = pl.multiple_of(n * block, block)
        total = dot(ogs[0], w[pl.ds(r, block), 0:width], 1, 1)
        for h in range(1, heads):
            total += dot(ogs[h], w[pl.ds(r, block), h * width : (h + 1) * width], 1, 1)
        ag[:, pl.ds(r, block)] = total.astype(BF16)
        return 0

    lax.fori_loop(0, w.shape[0] // block, project, 0)
    wait_bytes(slots.at[1, pl.ds(0, seq - 1)], sem2.at[1])
    up, down = lax.rem(me + 1, seq), lax.rem(me + seq - 1, seq)
    to_up = pltpu.make_async_remote_copy(
        slots.at[1], slots.at[0], sem3.at[0], sem3.at[1], device_id=at_seq(up), device_id_type=MESH
    )
    to_down = pltpu.make_async_remote_copy(
        slots.at[1], slots.at[2], sem3.at[2], sem3.at[3], device_id=at_seq(down), device_id_type=MESH
    )
    to_up.start()
    to_down.start()
    wait_bytes(first.at[pl.ds(0, seq - 1)], sem1.at[0])
    wait_bytes(order.at[pl.ds(0, seq - 1)], sem2.at[0])
    to_up.wait()
    to_down.wait()


def gather(owner, kv, og, w, seq, heads):
    vm = pl.BlockSpec(memory_space=pltpu.VMEM)
    pieces = kv.reshape(seq, -1, kv.shape[-1])
    rows, width = og.shape
    slots, ag = pl.pallas_call(
        functools.partial(gather_kernel, seq, heads),
        out_shape=(
            jax.ShapeDtypeStruct((3,) + pieces.shape, BF16),
            jax.ShapeDtypeStruct((rows, w.shape[0]), BF16),
        ),
        in_specs=[pl.BlockSpec(memory_space=pltpu.SMEM), vm, vm, pl.BlockSpec(memory_space=pl.ANY)],
        out_specs=(vm, vm),
        scratch_shapes=[
            pltpu.VMEM(pieces.shape, BF16),
            pltpu.VMEM(pieces.shape, BF16),
            pltpu.VMEM((heads, rows, width), BF16),
            pltpu.VMEM(w.shape, BF16),
            pltpu.SemaphoreType.DMA((2,)),
            pltpu.SemaphoreType.DMA((2,)),
            pltpu.SemaphoreType.DMA((4,)),
            pltpu.SemaphoreType.DMA((2, heads)),
            pltpu.SemaphoreType.DMA,
        ],
        compiler_params=pltpu.CompilerParams(
            collective_id=0, has_side_effects=True, vmem_limit_bytes=VMEM_LIMIT
        ),
        name="gather",
    )(owner, pieces, og, w)
    return slots.reshape((3,) + kv.shape[1:]), ag


def scatter_kernel(
    seq, heads, inverse, dslots, att, w_hbm, out, grad, near, summed, second, order, back, parts, got, w,
    sem1, sem2, sem3, sem4, wsem
):
    me, mine = lax.axis_index("seq"), lax.axis_index("head")
    load_w = pltpu.make_async_copy(w_hbm, w, wsem)
    load_w.start()
    enter(seq, heads)
    up, down = lax.rem(me + 1, seq), lax.rem(me + seq - 1, seq)
    groups = near.shape[1] // GROUPS
    near_copies = []
    for n in range(GROUPS):
        part = pl.ds(n * groups, groups)
        to_up = pltpu.make_async_remote_copy(
            dslots.at[2, part], near.at[0, part], sem1.at[0, n], sem1.at[1, n],
            device_id=at_seq(up), device_id_type=MESH,
        )
        to_down = pltpu.make_async_remote_copy(
            dslots.at[0, part], near.at[1, part], sem1.at[2, n], sem1.at[3, n],
            device_id=at_seq(down), device_id_type=MESH,
        )
        to_up.start()
        to_down.start()
        near_copies += [to_up, to_down]
    load_w.wait()
    width = out.shape[1]

    def project(i):
        peer = lax.rem(mine + i, heads)
        columns = pl.ds(pl.multiple_of(peer * width, width), width)
        return peer, dot(att[...], w[:, columns], 1, 0)

    out_copies = []

    def send_part(i):
        peer, part = project(i)
        parts[i] = part.astype(BF16)
        copy = pltpu.make_async_remote_copy(
            parts.at[i], got.at[i], sem4.at[0, i], sem4.at[1, i], device_id=at_head(peer), device_id_type=MESH
        )
        copy.start()
        out_copies.append(copy)

    send_part(1)
    first, last = me == 0, me == seq - 1
    for n in range(GROUPS):
        near_copies[2 * n].wait_recv()
        near_copies[2 * n + 1].wait_recv()
        part = pl.ds(n * groups, groups)
        low = jnp.where(first, 0.0, near[0, part].astype(F32))
        high = jnp.where(last, 0.0, near[1, part].astype(F32))
        summed[part] = (dslots[1, part].astype(F32) + low + high).astype(BF16)
    second[me] = summed[me]

    def spread(i, _):
        j = lax.rem(me + i, seq)
        pltpu.make_async_remote_copy(
            summed.at[j], second.at[me], sem2.at[0], sem2.at[1], device_id=at_seq(j), device_id_type=MESH
        ).start()
        return 0

    lax.fori_loop(1, seq, spread, 0)
    for i in range(2, heads):
        send_part(i)
    wait_bytes(second.at[pl.ds(0, seq - 1)], sem2.at[1])

    def deliver(i, _):
        o = lax.rem(me + i, seq)
        order[o] = second[inverse[o]]
        pltpu.make_async_remote_copy(
            order.at[o], back.at[me], sem3.at[0], sem3.at[1], device_id=at_seq(o), device_id_type=MESH
        ).start()
        return 0

    lax.fori_loop(1, seq, deliver, 0)
    back[me] = second[inverse[me]]
    total = project(0)[1]
    for copy in out_copies:
        copy.wait_recv()
    for i in range(1, heads):
        total += got[i].astype(F32)
    out[...] = total.astype(BF16)
    for copy in near_copies + out_copies:
        copy.wait_send()
    wait_bytes(second.at[pl.ds(0, seq - 1)], sem2.at[0])
    wait_bytes(order.at[pl.ds(0, seq - 1)], sem3.at[0])
    wait_bytes(back.at[pl.ds(0, seq - 1)], sem3.at[1])
    grad[...] = back[...].astype(F32)


GROUPS = 4


def scatter(inverse, dslots, att, w, seq, heads):
    vm = pl.BlockSpec(memory_space=pltpu.VMEM)
    pieces = dslots.reshape(3, seq, -1, dslots.shape[-1])
    shape = pieces.shape[1:]
    rows, width = att.shape[0], w.shape[1] // heads
    out, grad = pl.pallas_call(
        functools.partial(scatter_kernel, seq, heads),
        out_shape=(jax.ShapeDtypeStruct((rows, width), BF16), jax.ShapeDtypeStruct(shape, F32)),
        in_specs=[pl.BlockSpec(memory_space=pltpu.SMEM), vm, vm, pl.BlockSpec(memory_space=pl.ANY)],
        out_specs=(vm, vm),
        scratch_shapes=[
            pltpu.VMEM((2,) + shape, BF16),
            pltpu.VMEM(shape, BF16),
            pltpu.VMEM(shape, BF16),
            pltpu.VMEM(shape, BF16),
            pltpu.VMEM(shape, BF16),
            pltpu.VMEM((heads, rows, width), BF16),
            pltpu.VMEM((heads, rows, width), BF16),
            pltpu.VMEM(w.shape, BF16),
            pltpu.SemaphoreType.DMA((4, GROUPS)),
            pltpu.SemaphoreType.DMA((2,)),
            pltpu.SemaphoreType.DMA((2,)),
            pltpu.SemaphoreType.DMA((2, heads)),
            pltpu.SemaphoreType.DMA,
        ],
        compiler_params=pltpu.CompilerParams(
            collective_id=1, has_side_effects=True, vmem_limit_bytes=VMEM_LIMIT
        ),
        name="scatter",
    )(inverse, pieces, att, w)
    return out, grad.reshape((1,) + dslots.shape[1:])


def attention_kernel(bounds, lanes, q_ref, g_ref, slots, rk, rv, att, dq, drk, drv, dslots,
                     kt, vt, dk_acc, dv_acc, s_buf, d_buf):
    heads = q_ref.shape[1] // 128
    plen = slots.shape[2]
    rows = rk.shape[0]
    scale = 128 ** -0.5
    c = scale * LOG2E
    nt = q_ref.shape[0] // TILE
    R = TILE * heads
    for i in range(3):
        kt[i] = slots[i, 0].T
        vt[i] = slots[i, 1].T
    kt_r = rk[...].T
    vt_r = rv[...].T
    dk_acc[...] = jnp.zeros_like(dk_acc)
    dv_acc[...] = jnp.zeros_like(dv_acc)

    def tile_step(t, _):
        t0 = pl.multiple_of(t * TILE, TILE)
        q = jnp.concatenate([q_ref[pl.ds(t0, TILE), h * 128:(h + 1) * 128] for h in range(heads)], axis=0)
        g = jnp.concatenate([g_ref[pl.ds(t0, TILE), h * 128:(h + 1) * 128] for h in range(heads)], axis=0)
        start = lanes[0, t]
        slot_of = lanes[1, t]
        lane_tok = t0 + (lax.broadcasted_iota(jnp.int32, (1, R), 1) & (TILE - 1))
        lo = bounds[0, t]
        hi = bounds[1, t]

        def pair(p, _):
            member = slot_of == p
            key_id = lax.broadcasted_iota(jnp.int32, (rows, R), 0)
            vis = (key_id >= start) & (key_id <= lane_tok)
            sp = dot(slots[p, 0], q, 1, 1)
            sr = jnp.where(vis, dot(rk[...], q, 1, 1), -1e30)
            m = jnp.maximum(jnp.max(sp, axis=0, keepdims=True), jnp.max(sr, axis=0, keepdims=True))
            mc = m * c
            ep = jnp.exp2(sp * c - mc)
            er = jnp.exp2(sr * c - mc)
            l = jnp.sum(ep, axis=0, keepdims=True) + jnp.sum(er, axis=0, keepdims=True)
            inv = jnp.where(member, 1.0 / l, 0.0)
            wp = ep * inv
            wr = er * inv
            vp = dot(slots[p, 1], g, 1, 1)
            vr = dot(rv[...], g, 1, 1)
            rd = jnp.sum(wp * vp, axis=0, keepdims=True) + jnp.sum(wr * vr, axis=0, keepdims=True)
            wpl = wp.astype(BF16)
            wrl = wr.astype(BF16)
            gp = (wp * (vp - rd)).astype(BF16)
            gr = (wr * (vr - rd)).astype(BF16)
            ot = dot(vt[p], wpl, 1, 0) + dot(vt_r, wrl, 1, 0)
            qt = (dot(kt[p], gp, 1, 0) + dot(kt_r, gr, 1, 0)) * scale
            o = ot.T.astype(BF16)
            dqv = qt.T.astype(BF16)
            first = p == lo
            for h in range(heads):
                for ref, val in ((att, o), (dq, dqv)):
                    new = val[h * TILE:(h + 1) * TILE]
                    old = ref[pl.ds(t0, TILE), h * 128:(h + 1) * 128]
                    ref[pl.ds(t0, TILE), h * 128:(h + 1) * 128] = jnp.where(first, new, old + new)
            pr = pl.multiple_of(p * plen, plen)
            dv_acc[pl.ds(pr, plen)] += dot(wpl, g, 1, 0)
            dk_acc[pl.ds(pr, plen)] += dot(gp, q, 1, 0)
            dv_acc[3 * plen:] += dot(wrl, g, 1, 0)
            dk_acc[3 * plen:] += dot(gr, q, 1, 0)
            return 0
        lax.fori_loop(lo, hi + 1, pair, 0)
        return 0
    lax.fori_loop(0, nt, tile_step, 0)
    for i in range(3):
        dslots[i, 0] = (dk_acc[i * plen:(i + 1) * plen] * scale).astype(BF16)
        dslots[i, 1] = dv_acc[i * plen:(i + 1) * plen].astype(BF16)
    drk[...] = (dk_acc[3 * plen:] * scale).astype(BF16)
    drv[...] = dv_acc[3 * plen:].astype(BF16)

def attention(tokens, k, q, g, slots, rk, rv):
    rows, feat = q.shape
    plen = slots.shape[2]
    heads = feat // 128
    nt = rows // TILE
    R = TILE * heads
    idx = jnp.arange(rows, dtype=jnp.int32)
    start = jnp.sum((tokens[None, :] < tokens[:, None]).astype(jnp.int32), axis=1)
    slot = tokens // GROUP - (k - 1)
    lanes = jnp.stack([jnp.tile(start.reshape(nt, 1, TILE), (1, 1, heads)), jnp.tile(slot.reshape(nt, 1, TILE), (1, 1, heads))])
    sl = slot.reshape(nt, TILE)
    bounds = jnp.stack([sl[:, 0], sl[:, -1]])
    vm = pl.BlockSpec(memory_space=pltpu.VMEM)
    return pl.pallas_call(
        attention_kernel,
        out_shape=(jax.ShapeDtypeStruct(q.shape, BF16), jax.ShapeDtypeStruct(q.shape, BF16),
                   jax.ShapeDtypeStruct(rk.shape, BF16), jax.ShapeDtypeStruct(rv.shape, BF16),
                   jax.ShapeDtypeStruct(slots.shape, BF16)),
        in_specs=[pl.BlockSpec(memory_space=pltpu.SMEM)] + [vm] * 6,
        out_specs=(vm,) * 5,
        scratch_shapes=[pltpu.VMEM((3, 128, plen), BF16), pltpu.VMEM((3, 128, plen), BF16),
                        pltpu.VMEM((3 * plen + rows, 128), F32), pltpu.VMEM((3 * plen + rows, 128), F32),
                        pltpu.VMEM((8, 128), F32), pltpu.VMEM((8, 128), F32)],
        compiler_params=pltpu.CompilerParams(vmem_limit_bytes=48 * 2**20),
    )(bounds, lanes, q, g, slots, rk, rv)


def per_device(
    token_response, prompt_owner, queries, resp_keys, resp_values, prompt_kv, out_weight, out_grad
):
    seq, heads = lax.axis_size("seq"), lax.axis_size("head")
    inverse = jnp.argmax(prompt_owner[None, :] == jnp.arange(seq, dtype=jnp.int32)[:, None], axis=1).astype(
        jnp.int32
    )
    slots, attn_grad = gather(prompt_owner, prompt_kv, out_grad, out_weight, seq, heads)
    attended, query_grad, key_grad, value_grad, slot_grads = attention(
        token_response, lax.axis_index("seq"), queries, attn_grad, slots, resp_keys, resp_values
    )
    layer_out, prompt_kv_grad = scatter(inverse, slot_grads, attended, out_weight, seq, heads)
    return (layer_out, query_grad, key_grad, value_grad, prompt_kv_grad)


def solution(mesh):
    placed = (
        P("seq"),
        P(),
        P("seq", "head"),
        P("seq", "head"),
        P("seq", "head"),
        P("seq", None, None, "head"),
        P("head", None),
        P("seq", "head"),
    )
    return jax.shard_map(
        per_device,
        mesh=mesh,
        in_specs=placed,
        out_specs=(
            P("seq", "head"),
            P("seq", "head"),
            P("seq", "head"),
            P("seq", "head"),
            P("seq", None, None, "head"),
        ),
        check_vma=False,
    )
```

```python
import functools

import jax
import jax.numpy as jnp
from jax import lax
from jax.experimental import pallas as pl
from jax.experimental.pallas import tpu as pltpu
from jax.sharding import PartitionSpec as P

GROUP = 16
TILE = 32
LOG2E = 1.4426950408889634
F32, BF16 = jnp.float32, jnp.bfloat16
MESH = pl.DeviceIdType.MESH
VMEM_LIMIT = 48 * 2**20


def dot(a, b, ca, cb):
    return lax.dot_general(a, b, (((ca,), (cb,)), ((), ())), preferred_element_type=F32)


def at_seq(j):
    return (j, lax.axis_index("head"))


def at_head(j):
    return (lax.axis_index("seq"), j)


def greet(seq, heads):
    me, mine = lax.axis_index("seq"), lax.axis_index("head")
    barrier = pltpu.get_barrier_semaphore()

    def tell(i, _):
        pl.semaphore_signal(barrier, inc=1, device_id=at_seq(lax.rem(me + i, seq)), device_id_type=MESH)
        return 0

    lax.fori_loop(1, seq, tell, 0)
    for i in range(1, heads):
        pl.semaphore_signal(barrier, inc=1, device_id=at_head(lax.rem(mine + i, heads)), device_id_type=MESH)


def all_in(seq, heads):
    pl.semaphore_wait(pltpu.get_barrier_semaphore(), seq - 1 + heads - 1)


def each_peer(seq, visit):
    me = lax.axis_index("seq")
    core, chip, chips = lax.rem(me, 2), me // 2, seq // 2
    visit(me + 1 - 2 * core)
    for c in range(2):

        def go(t, _):
            visit(2 * lax.rem(chip + t, chips) + c)
            return 0

        lax.fori_loop(1, chips, go, 0)


def wait_bytes(ref, sem):
    pltpu.make_async_copy(ref, ref, sem).wait()


def gather_kernel(
    seq, heads, owner_hbm, kv, og, w_hbm, slots, ag, first, order, ogs, w, owner, sem1, sem2s, sem2, sem3, sem4, local
):
    me, mine = lax.axis_index("seq"), lax.axis_index("head")
    groups = max(2, seq // 8)
    per = seq // groups
    width = og.shape[1]
    load_owner = pltpu.make_async_copy(owner_hbm, owner, local.at[0])
    load_piece = pltpu.make_async_copy(kv.at[me], first.at[me], local.at[1])
    load_og = pltpu.make_async_copy(og, ogs.at[mine], local.at[2])
    load_w = pltpu.make_async_copy(w_hbm, w, local.at[3])
    for load in (load_owner, load_piece, load_og, load_w):
        load.start()
    greet(seq, heads)
    all_in(seq, heads)

    def spread(j):
        pltpu.make_async_remote_copy(
            kv.at[j], first.at[me], sem1.at[0], sem1.at[1], device_id=at_seq(j), device_id_type=MESH
        ).start()

    each_peer(seq, spread)
    og_copies = []
    for i in range(1, heads):
        copy = pltpu.make_async_remote_copy(
            og, ogs.at[mine], sem4.at[0, i], sem4.at[1, heads - i],
            device_id=at_head(lax.rem(mine + i, heads)), device_id_type=MESH,
        )
        copy.start()
        og_copies.append(copy)
    load_owner.wait()
    load_piece.wait()
    wait_bytes(first.at[pl.ds(0, seq - 1)], sem1.at[1])
    group = me // per

    def deliver(p):
        order[p] = first[owner[p]]
        pltpu.make_async_remote_copy(
            order.at[p], slots.at[1, me], sem2s, sem2.at[group], device_id=at_seq(p), device_id_type=MESH
        ).start()

    each_peer(seq, deliver)
    slots[1, me] = first[owner[me]]
    load_og.wait()
    load_w.wait()
    for copy in og_copies:
        copy.wait_recv()
    block = 256

    def project(n, _):
        r = pl.multiple_of(n * block, block)
        total = dot(ogs[0], w[pl.ds(r, block), 0:width], 1, 1)
        for h in range(1, heads):
            total += dot(ogs[h], w[pl.ds(r, block), h * width : (h + 1) * width], 1, 1)
        ag[:, pl.ds(r, block)] = total.astype(BF16)
        return 0

    lax.fori_loop(0, w.shape[0] // block, project, 0)
    up, down = lax.rem(me + 1, seq), lax.rem(me + seq - 1, seq)
    for n in range(groups):
        g = lax.rem(group + 2 * groups - 1 - n, groups)
        arrived = per if n < groups - 1 else per - 1
        wait_bytes(slots.at[1, pl.ds(0, arrived)], sem2.at[g])
        part = pl.ds(g * per, per)
        pltpu.make_async_remote_copy(
            slots.at[1, part], slots.at[0, part], sem3.at[0], sem3.at[1], device_id=at_seq(up), device_id_type=MESH
        ).start()
        pltpu.make_async_remote_copy(
            slots.at[1, part], slots.at[2, part], sem3.at[2], sem3.at[3], device_id=at_seq(down), device_id_type=MESH
        ).start()
    wait_bytes(first.at[pl.ds(0, seq - 1)], sem1.at[0])
    wait_bytes(order.at[pl.ds(0, seq - 1)], sem2s)
    for copy in og_copies:
        copy.wait_send()
    wait_bytes(slots.at[1], sem3.at[0])
    wait_bytes(slots.at[1], sem3.at[2])
    wait_bytes(slots.at[0], sem3.at[1])
    wait_bytes(slots.at[2], sem3.at[3])


def gather(owner, kv, og, w, seq, heads):
    vm = pl.BlockSpec(memory_space=pltpu.VMEM)
    hbm = pl.BlockSpec(memory_space=pltpu.HBM)
    pieces = kv.reshape(seq, -1, kv.shape[-1])
    rows, width = og.shape
    slots, ag = pl.pallas_call(
        functools.partial(gather_kernel, seq, heads),
        out_shape=(
            jax.ShapeDtypeStruct((3,) + pieces.shape, BF16),
            jax.ShapeDtypeStruct((rows, w.shape[0]), BF16),
        ),
        in_specs=[hbm, hbm, hbm, hbm],
        out_specs=(vm, vm),
        scratch_shapes=[
            pltpu.VMEM(pieces.shape, BF16),
            pltpu.VMEM(pieces.shape, BF16),
            pltpu.VMEM((heads, rows, width), BF16),
            pltpu.VMEM(w.shape, BF16),
            pltpu.SMEM(owner.shape, jnp.int32),
            pltpu.SemaphoreType.DMA((2,)),
            pltpu.SemaphoreType.DMA,
            pltpu.SemaphoreType.DMA((max(2, seq // 8),)),
            pltpu.SemaphoreType.DMA((4,)),
            pltpu.SemaphoreType.DMA((2, heads)),
            pltpu.SemaphoreType.DMA((4,)),
        ],
        compiler_params=pltpu.CompilerParams(
            collective_id=0, has_side_effects=True, vmem_limit_bytes=VMEM_LIMIT
        ),
        name="gather",
    )(owner, pieces, og, w)
    return slots.reshape((3,) + kv.shape[1:]), ag


def scatter_kernel(
    seq, heads, owner_hbm, dslots, att, w_hbm, out, grad, near, summed, second, order, back, parts, got, w, own_part,
    owner, inverse_row, inverse, sem1s, sem1, sem2, sem3, sem4, local,
):
    me, mine = lax.axis_index("seq"), lax.axis_index("head")
    groups = max(2, seq // 8)
    per = seq // groups
    width = out.shape[1]
    load_owner = pltpu.make_async_copy(owner_hbm, owner, local.at[0])
    load_w = pltpu.make_async_copy(w_hbm, w, local.at[1])
    load_w.start()
    load_owner.start()
    greet(seq, heads)
    load_w.wait()

    def project(i):
        peer = lax.rem(mine + i, heads)
        return dot(att[...], w[:, pl.ds(pl.multiple_of(peer * width, width), width)], 1, 0)

    def send_part(i):
        copy = pltpu.make_async_remote_copy(
            parts.at[i], got.at[i], sem4.at[0, i], sem4.at[1, i],
            device_id=at_head(lax.rem(mine + i, heads)), device_id_type=MESH,
        )
        copy.start()
        return copy

    parts[1] = project(1).astype(BF16)
    all_in(seq, heads)
    up, down = lax.rem(me + 1, seq), lax.rem(me + seq - 1, seq)
    group = me // per
    for n in range(groups):
        g = lax.rem(group + n, groups)
        part = pl.ds(g * per, per)
        pltpu.make_async_remote_copy(
            dslots.at[2, part], near.at[0, part], sem1s.at[0], sem1.at[0, g], device_id=at_seq(up), device_id_type=MESH
        ).start()
        pltpu.make_async_remote_copy(
            dslots.at[0, part], near.at[1, part], sem1s.at[1], sem1.at[1, g], device_id=at_seq(down), device_id_type=MESH
        ).start()
    copies = [send_part(1)]
    for i in range(2, heads):
        parts[i] = project(i).astype(BF16)
        copies.append(send_part(i))
    at_start, at_end = me == 0, me == seq - 1
    for n in range(groups):
        g = lax.rem(group + n, groups)
        part = pl.ds(g * per, per)
        wait_bytes(near.at[0, part], sem1.at[0, g])
        wait_bytes(near.at[1, part], sem1.at[1, g])
        low = jnp.where(at_start, 0.0, near[0, part].astype(F32))
        high = jnp.where(at_end, 0.0, near[1, part].astype(F32))
        summed[part] = (dslots[1, part].astype(F32) + low + high).astype(BF16)
        for i in range(per):
            j = g * per + i

            @pl.when(j != me)
            def _():
                pltpu.make_async_remote_copy(
                    summed.at[j], second.at[me], sem2.at[0], sem2.at[1], device_id=at_seq(j), device_id_type=MESH
                ).start()

    second[me] = summed[me]
    load_owner.wait()
    lane = lax.broadcasted_iota(jnp.int32, inverse_row.shape, 1)
    row = jnp.zeros(inverse_row.shape, jnp.int32)
    for p in range(seq):
        row = jnp.where(lane == owner[p], p, row)
    inverse_row[...] = row
    to_scalars = pltpu.make_async_copy(inverse_row, inverse, local.at[2])
    to_scalars.start()
    own_part[...] = project(0)
    to_scalars.wait()
    wait_bytes(second.at[pl.ds(0, seq - 1)], sem2.at[1])

    def deliver(o):
        order[o] = second[inverse[0, o]]
        pltpu.make_async_remote_copy(
            order.at[o], back.at[me], sem3.at[0], sem3.at[1], device_id=at_seq(o), device_id_type=MESH
        ).start()

    each_peer(seq, deliver)
    back[me] = second[inverse[0, me]]
    for copy in copies:
        copy.wait_recv()
    total = own_part[...]
    for i in range(1, heads):
        total += got[i].astype(F32)
    out[...] = total.astype(BF16)
    for copy in copies:
        copy.wait_send()
    wait_bytes(near.at[0], sem1s.at[0])
    wait_bytes(near.at[1], sem1s.at[1])
    wait_bytes(second.at[pl.ds(0, seq - 1)], sem2.at[0])
    wait_bytes(order.at[pl.ds(0, seq - 1)], sem3.at[0])
    wait_bytes(back.at[pl.ds(0, seq - 1)], sem3.at[1])
    grad[...] = back[...].astype(F32)


def scatter(owner, dslots, att, w, seq, heads):
    vm = pl.BlockSpec(memory_space=pltpu.VMEM)
    hbm = pl.BlockSpec(memory_space=pltpu.HBM)
    pieces = dslots.reshape(3, seq, -1, dslots.shape[-1])
    shape = pieces.shape[1:]
    rows, width = att.shape[0], w.shape[1] // heads
    lanes = -(-seq // 128) * 128
    out, grad = pl.pallas_call(
        functools.partial(scatter_kernel, seq, heads),
        out_shape=(jax.ShapeDtypeStruct((rows, width), BF16), jax.ShapeDtypeStruct(shape, F32)),
        in_specs=[hbm, vm, vm, hbm],
        out_specs=(vm, vm),
        scratch_shapes=[
            pltpu.VMEM((2,) + shape, BF16),
            pltpu.VMEM(shape, BF16),
            pltpu.VMEM(shape, BF16),
            pltpu.VMEM(shape, BF16),
            pltpu.VMEM(shape, BF16),
            pltpu.VMEM((heads, rows, width), BF16),
            pltpu.VMEM((heads, rows, width), BF16),
            pltpu.VMEM(w.shape, BF16),
            pltpu.VMEM((rows, width), F32),
            pltpu.SMEM(owner.shape, jnp.int32),
            pltpu.VMEM((1, lanes), jnp.int32),
            pltpu.SMEM((1, lanes), jnp.int32),
            pltpu.SemaphoreType.DMA((2,)),
            pltpu.SemaphoreType.DMA((2, max(2, seq // 8))),
            pltpu.SemaphoreType.DMA((2,)),
            pltpu.SemaphoreType.DMA((2,)),
            pltpu.SemaphoreType.DMA((2, heads)),
            pltpu.SemaphoreType.DMA((3,)),
        ],
        compiler_params=pltpu.CompilerParams(
            collective_id=1, has_side_effects=True, vmem_limit_bytes=VMEM_LIMIT
        ),
        name="scatter",
    )(owner, pieces, att, w)
    return out, grad.reshape((1,) + dslots.shape[1:])


def attention_kernel(bounds, lanes, q_ref, g_ref, slots, rk, rv, att, dq, drk, drv, dslots,
                     kt, vt, dk_acc, dv_acc, s_buf, d_buf):
    heads = q_ref.shape[1] // 128
    plen = slots.shape[2]
    rows = rk.shape[0]
    scale = 128 ** -0.5
    c = scale * LOG2E
    nt = q_ref.shape[0] // TILE
    R = TILE * heads
    for i in range(3):
        kt[i] = slots[i, 0].T
        vt[i] = slots[i, 1].T
    kt_r = rk[...].T
    vt_r = rv[...].T
    dk_acc[...] = jnp.zeros_like(dk_acc)
    dv_acc[...] = jnp.zeros_like(dv_acc)

    def tile_step(t, _):
        t0 = pl.multiple_of(t * TILE, TILE)
        q = jnp.concatenate([q_ref[pl.ds(t0, TILE), h * 128:(h + 1) * 128] for h in range(heads)], axis=0)
        g = jnp.concatenate([g_ref[pl.ds(t0, TILE), h * 128:(h + 1) * 128] for h in range(heads)], axis=0)
        start = lanes[0, t]
        slot_of = lanes[1, t]
        lane_tok = t0 + (lax.broadcasted_iota(jnp.int32, (1, R), 1) & (TILE - 1))
        lo = bounds[0, t]
        hi = bounds[1, t]

        def pair(p, _):
            member = slot_of == p
            key_id = lax.broadcasted_iota(jnp.int32, (rows, R), 0)
            vis = (key_id >= start) & (key_id <= lane_tok)
            sp = dot(slots[p, 0], q, 1, 1)
            sr = jnp.where(vis, dot(rk[...], q, 1, 1), -1e30)
            m = jnp.maximum(jnp.max(sp, axis=0, keepdims=True), jnp.max(sr, axis=0, keepdims=True))
            mc = m * c
            ep = jnp.exp2(sp * c - mc)
            er = jnp.exp2(sr * c - mc)
            l = jnp.sum(ep, axis=0, keepdims=True) + jnp.sum(er, axis=0, keepdims=True)
            inv = jnp.where(member, 1.0 / l, 0.0)
            wp = ep * inv
            wr = er * inv
            vp = dot(slots[p, 1], g, 1, 1)
            vr = dot(rv[...], g, 1, 1)
            rd = jnp.sum(wp * vp, axis=0, keepdims=True) + jnp.sum(wr * vr, axis=0, keepdims=True)
            wpl = wp.astype(BF16)
            wrl = wr.astype(BF16)
            gp = (wp * (vp - rd)).astype(BF16)
            gr = (wr * (vr - rd)).astype(BF16)
            ot = dot(vt[p], wpl, 1, 0) + dot(vt_r, wrl, 1, 0)
            qt = (dot(kt[p], gp, 1, 0) + dot(kt_r, gr, 1, 0)) * scale
            o = ot.T.astype(BF16)
            dqv = qt.T.astype(BF16)
            first = p == lo
            for h in range(heads):
                for ref, val in ((att, o), (dq, dqv)):
                    new = val[h * TILE:(h + 1) * TILE]
                    old = ref[pl.ds(t0, TILE), h * 128:(h + 1) * 128]
                    ref[pl.ds(t0, TILE), h * 128:(h + 1) * 128] = jnp.where(first, new, old + new)
            pr = pl.multiple_of(p * plen, plen)
            dv_acc[pl.ds(pr, plen)] += dot(wpl, g, 1, 0)
            dk_acc[pl.ds(pr, plen)] += dot(gp, q, 1, 0)
            dv_acc[3 * plen:] += dot(wrl, g, 1, 0)
            dk_acc[3 * plen:] += dot(gr, q, 1, 0)
            return 0
        lax.fori_loop(lo, hi + 1, pair, 0)
        return 0
    lax.fori_loop(0, nt, tile_step, 0)
    for i in range(3):
        dslots[i, 0] = (dk_acc[i * plen:(i + 1) * plen] * scale).astype(BF16)
        dslots[i, 1] = dv_acc[i * plen:(i + 1) * plen].astype(BF16)
    drk[...] = (dk_acc[3 * plen:] * scale).astype(BF16)
    drv[...] = dv_acc[3 * plen:].astype(BF16)

def attention(tokens, k, q, g, slots, rk, rv):
    rows, feat = q.shape
    plen = slots.shape[2]
    heads = feat // 128
    nt = rows // TILE
    R = TILE * heads
    idx = jnp.arange(rows, dtype=jnp.int32)
    start = jnp.sum((tokens[None, :] < tokens[:, None]).astype(jnp.int32), axis=1)
    slot = tokens // GROUP - (k - 1)
    lanes = jnp.stack([jnp.tile(start.reshape(nt, 1, TILE), (1, 1, heads)), jnp.tile(slot.reshape(nt, 1, TILE), (1, 1, heads))])
    sl = slot.reshape(nt, TILE)
    bounds = jnp.stack([sl[:, 0], sl[:, -1]])
    vm = pl.BlockSpec(memory_space=pltpu.VMEM)
    return pl.pallas_call(
        attention_kernel,
        out_shape=(jax.ShapeDtypeStruct(q.shape, BF16), jax.ShapeDtypeStruct(q.shape, BF16),
                   jax.ShapeDtypeStruct(rk.shape, BF16), jax.ShapeDtypeStruct(rv.shape, BF16),
                   jax.ShapeDtypeStruct(slots.shape, BF16)),
        in_specs=[pl.BlockSpec(memory_space=pltpu.SMEM)] + [vm] * 6,
        out_specs=(vm,) * 5,
        scratch_shapes=[pltpu.VMEM((3, 128, plen), BF16), pltpu.VMEM((3, 128, plen), BF16),
                        pltpu.VMEM((3 * plen + rows, 128), F32), pltpu.VMEM((3 * plen + rows, 128), F32),
                        pltpu.VMEM((8, 128), F32), pltpu.VMEM((8, 128), F32)],
        compiler_params=pltpu.CompilerParams(vmem_limit_bytes=48 * 2**20),
    )(bounds, lanes, q, g, slots, rk, rv)


def per_device(
    token_response, prompt_owner, queries, resp_keys, resp_values, prompt_kv, out_weight, out_grad
):
    seq, heads = lax.axis_size("seq"), lax.axis_size("head")
    slots, attn_grad = gather(prompt_owner, prompt_kv, out_grad, out_weight, seq, heads)
    attended, query_grad, key_grad, value_grad, slot_grads = attention(
        token_response, lax.axis_index("seq"), queries, attn_grad, slots, resp_keys, resp_values
    )
    layer_out, prompt_kv_grad = scatter(prompt_owner, slot_grads, attended, out_weight, seq, heads)
    return (layer_out, query_grad, key_grad, value_grad, prompt_kv_grad)


def solution(mesh):
    placed = (
        P("seq"),
        P(),
        P("seq", "head"),
        P("seq", "head"),
        P("seq", "head"),
        P("seq", None, None, "head"),
        P("head", None),
        P("seq", "head"),
    )
    return jax.shard_map(
        per_device,
        mesh=mesh,
        in_specs=placed,
        out_specs=(
            P("seq", "head"),
            P("seq", "head"),
            P("seq", "head"),
            P("seq", "head"),
            P("seq", None, None, "head"),
        ),
        check_vma=False,
    )
```

```python
import functools

import jax
import jax.numpy as jnp
from jax import lax
from jax.experimental import pallas as pl
from jax.experimental.pallas import tpu as pltpu
from jax.sharding import PartitionSpec as P

GROUP = 16
TILE = 32
LOG2E = 1.4426950408889634
F32, BF16 = jnp.float32, jnp.bfloat16
MESH = pl.DeviceIdType.MESH
VMEM_LIMIT = 48 * 2**20


def dot(a, b, ca, cb):
    return lax.dot_general(a, b, (((ca,), (cb,)), ((), ())), preferred_element_type=F32)


def at_seq(j):
    return (j, lax.axis_index("head"))


def at_head(j):
    return (lax.axis_index("seq"), j)


def greet(seq, heads):
    me, mine = lax.axis_index("seq"), lax.axis_index("head")
    barrier = pltpu.get_barrier_semaphore()

    def tell(i, _):
        pl.semaphore_signal(barrier, inc=1, device_id=at_seq(lax.rem(me + i, seq)), device_id_type=MESH)
        return 0

    lax.fori_loop(1, seq, tell, 0)
    for i in range(1, heads):
        pl.semaphore_signal(barrier, inc=1, device_id=at_head(lax.rem(mine + i, heads)), device_id_type=MESH)


def all_in(seq, heads):
    pl.semaphore_wait(pltpu.get_barrier_semaphore(), seq - 1 + heads - 1)


def each_peer(seq, visit):
    me = lax.axis_index("seq")
    core, chip, chips = lax.rem(me, 2), me // 2, seq // 2
    visit(me + 1 - 2 * core)
    for c in range(2):

        def go(t, _):
            visit(2 * lax.rem(chip + t, chips) + c)
            return 0

        lax.fori_loop(1, chips, go, 0)


def in_hbm(x):
    return pltpu.with_memory_space_constraint(x, pltpu.HBM)


def wait_bytes(ref, sem):
    pltpu.make_async_copy(ref, ref, sem).wait()


def gather_kernel(
    seq, heads, owner_hbm, kv, og, w_hbm, slots, ag, first, order, ogs, w, owner, sem1, sem2s, sem2, sem3, sem4, local
):
    me, mine = lax.axis_index("seq"), lax.axis_index("head")
    groups = max(2, seq // 8)
    per = seq // groups
    width = og.shape[1]
    load_owner = pltpu.make_async_copy(owner_hbm, owner, local.at[0])
    load_piece = pltpu.make_async_copy(kv.at[me], first.at[me], local.at[1])
    load_og = pltpu.make_async_copy(og, ogs.at[mine], local.at[2])
    load_w = pltpu.make_async_copy(w_hbm, w, local.at[3])
    for load in (load_owner, load_piece, load_og, load_w):
        load.start()
    greet(seq, heads)
    all_in(seq, heads)

    def spread(j):
        pltpu.make_async_remote_copy(
            kv.at[j], first.at[me], sem1.at[0], sem1.at[1], device_id=at_seq(j), device_id_type=MESH
        ).start()

    each_peer(seq, spread)
    og_copies = []
    for i in range(1, heads):
        copy = pltpu.make_async_remote_copy(
            og, ogs.at[mine], sem4.at[0, i], sem4.at[1, heads - i],
            device_id=at_head(lax.rem(mine + i, heads)), device_id_type=MESH,
        )
        copy.start()
        og_copies.append(copy)
    load_owner.wait()
    load_piece.wait()
    wait_bytes(first.at[pl.ds(0, seq - 1)], sem1.at[1])
    group = me // per

    def deliver(p):
        order[p] = first[owner[p]]
        pltpu.make_async_remote_copy(
            order.at[p], slots.at[1, me], sem2s, sem2.at[group], device_id=at_seq(p), device_id_type=MESH
        ).start()

    each_peer(seq, deliver)
    slots[1, me] = first[owner[me]]
    load_og.wait()
    load_w.wait()
    for copy in og_copies:
        copy.wait_recv()
    block = 256

    def project(n, _):
        r = pl.multiple_of(n * block, block)
        total = dot(ogs[0], w[pl.ds(r, block), 0:width], 1, 1)
        for h in range(1, heads):
            total += dot(ogs[h], w[pl.ds(r, block), h * width : (h + 1) * width], 1, 1)
        ag[:, pl.ds(r, block)] = total.astype(BF16)
        return 0

    lax.fori_loop(0, w.shape[0] // block, project, 0)
    up, down = lax.rem(me + 1, seq), lax.rem(me + seq - 1, seq)
    for n in range(groups):
        g = lax.rem(group + 2 * groups - 1 - n, groups)
        arrived = per if n < groups - 1 else per - 1
        wait_bytes(slots.at[1, pl.ds(0, arrived)], sem2.at[g])
        part = pl.ds(g * per, per)
        pltpu.make_async_remote_copy(
            slots.at[1, part], slots.at[0, part], sem3.at[0], sem3.at[1], device_id=at_seq(up), device_id_type=MESH
        ).start()
        pltpu.make_async_remote_copy(
            slots.at[1, part], slots.at[2, part], sem3.at[2], sem3.at[3], device_id=at_seq(down), device_id_type=MESH
        ).start()
    wait_bytes(first.at[pl.ds(0, seq - 1)], sem1.at[0])
    wait_bytes(order.at[pl.ds(0, seq - 1)], sem2s)
    for copy in og_copies:
        copy.wait_send()
    wait_bytes(slots.at[1], sem3.at[0])
    wait_bytes(slots.at[1], sem3.at[2])
    wait_bytes(slots.at[0], sem3.at[1])
    wait_bytes(slots.at[2], sem3.at[3])


def gather(owner, kv, og, w, seq, heads):
    vm = pl.BlockSpec(memory_space=pltpu.VMEM)
    hbm = pl.BlockSpec(memory_space=pltpu.HBM)
    pieces = kv.reshape(seq, -1, kv.shape[-1])
    rows, width = og.shape
    slots, ag = pl.pallas_call(
        functools.partial(gather_kernel, seq, heads),
        out_shape=(
            jax.ShapeDtypeStruct((3,) + pieces.shape, BF16),
            jax.ShapeDtypeStruct((rows, w.shape[0]), BF16),
        ),
        in_specs=[hbm, hbm, hbm, hbm],
        out_specs=(vm, vm),
        scratch_shapes=[
            pltpu.VMEM(pieces.shape, BF16),
            pltpu.VMEM(pieces.shape, BF16),
            pltpu.VMEM((heads, rows, width), BF16),
            pltpu.VMEM(w.shape, BF16),
            pltpu.SMEM(owner.shape, jnp.int32),
            pltpu.SemaphoreType.DMA((2,)),
            pltpu.SemaphoreType.DMA,
            pltpu.SemaphoreType.DMA((max(2, seq // 8),)),
            pltpu.SemaphoreType.DMA((4,)),
            pltpu.SemaphoreType.DMA((2, heads)),
            pltpu.SemaphoreType.DMA((4,)),
        ],
        compiler_params=pltpu.CompilerParams(
            collective_id=0, has_side_effects=True, vmem_limit_bytes=VMEM_LIMIT
        ),
        name="gather",
    )(*(in_hbm(x) for x in (owner, pieces, og, w)))
    return slots.reshape((3,) + kv.shape[1:]), ag


def scatter_kernel(
    seq, heads, owner_hbm, dslots, att, w_hbm, out, grad, near, summed, second, order, back, parts, got, w, own_part,
    owner, inverse_row, inverse, sem1s, sem1, sem2, sem3, sem4, local,
):
    me, mine = lax.axis_index("seq"), lax.axis_index("head")
    groups = max(2, seq // 8)
    per = seq // groups
    width = out.shape[1]
    load_owner = pltpu.make_async_copy(owner_hbm, owner, local.at[0])
    load_w = pltpu.make_async_copy(w_hbm, w, local.at[1])
    load_w.start()
    load_owner.start()
    greet(seq, heads)
    load_w.wait()

    def project(i):
        peer = lax.rem(mine + i, heads)
        return dot(att[...], w[:, pl.ds(pl.multiple_of(peer * width, width), width)], 1, 0)

    def send_part(i):
        copy = pltpu.make_async_remote_copy(
            parts.at[i], got.at[i], sem4.at[0, i], sem4.at[1, i],
            device_id=at_head(lax.rem(mine + i, heads)), device_id_type=MESH,
        )
        copy.start()
        return copy

    parts[1] = project(1).astype(BF16)
    all_in(seq, heads)
    up, down = lax.rem(me + 1, seq), lax.rem(me + seq - 1, seq)
    group = me // per
    for n in range(groups):
        g = lax.rem(group + n, groups)
        part = pl.ds(g * per, per)
        pltpu.make_async_remote_copy(
            dslots.at[2, part], near.at[0, part], sem1s.at[0], sem1.at[0, g], device_id=at_seq(up), device_id_type=MESH
        ).start()
        pltpu.make_async_remote_copy(
            dslots.at[0, part], near.at[1, part], sem1s.at[1], sem1.at[1, g], device_id=at_seq(down), device_id_type=MESH
        ).start()
    copies = [send_part(1)]
    for i in range(2, heads):
        parts[i] = project(i).astype(BF16)
        copies.append(send_part(i))
    at_start, at_end = me == 0, me == seq - 1
    for n in range(groups):
        g = lax.rem(group + n, groups)
        part = pl.ds(g * per, per)
        wait_bytes(near.at[0, part], sem1.at[0, g])
        wait_bytes(near.at[1, part], sem1.at[1, g])
        low = jnp.where(at_start, 0.0, near[0, part].astype(F32))
        high = jnp.where(at_end, 0.0, near[1, part].astype(F32))
        summed[part] = (dslots[1, part].astype(F32) + low + high).astype(BF16)
        for i in range(per):
            j = g * per + i

            @pl.when(j != me)
            def _():
                pltpu.make_async_remote_copy(
                    summed.at[j], second.at[me], sem2.at[0], sem2.at[1], device_id=at_seq(j), device_id_type=MESH
                ).start()

    second[me] = summed[me]
    load_owner.wait()
    lane = lax.broadcasted_iota(jnp.int32, inverse_row.shape, 1)
    row = jnp.zeros(inverse_row.shape, jnp.int32)
    for p in range(seq):
        row = jnp.where(lane == owner[p], p, row)
    inverse_row[...] = row
    to_scalars = pltpu.make_async_copy(inverse_row, inverse, local.at[2])
    to_scalars.start()
    own_part[...] = project(0)
    to_scalars.wait()
    wait_bytes(second.at[pl.ds(0, seq - 1)], sem2.at[1])

    def deliver(o):
        order[o] = second[inverse[0, o]]
        pltpu.make_async_remote_copy(
            order.at[o], back.at[me], sem3.at[0], sem3.at[1], device_id=at_seq(o), device_id_type=MESH
        ).start()

    each_peer(seq, deliver)
    back[me] = second[inverse[0, me]]
    for copy in copies:
        copy.wait_recv()
    total = own_part[...]
    for i in range(1, heads):
        total += got[i].astype(F32)
    out[...] = total.astype(BF16)
    for copy in copies:
        copy.wait_send()
    wait_bytes(near.at[0], sem1s.at[0])
    wait_bytes(near.at[1], sem1s.at[1])
    wait_bytes(second.at[pl.ds(0, seq - 1)], sem2.at[0])
    wait_bytes(order.at[pl.ds(0, seq - 1)], sem3.at[0])
    wait_bytes(back.at[pl.ds(0, seq - 1)], sem3.at[1])
    grad[...] = back[...].astype(F32)


def scatter(owner, dslots, att, w, seq, heads):
    vm = pl.BlockSpec(memory_space=pltpu.VMEM)
    hbm = pl.BlockSpec(memory_space=pltpu.HBM)
    pieces = dslots.reshape(3, seq, -1, dslots.shape[-1])
    shape = pieces.shape[1:]
    rows, width = att.shape[0], w.shape[1] // heads
    lanes = -(-seq // 128) * 128
    out, grad = pl.pallas_call(
        functools.partial(scatter_kernel, seq, heads),
        out_shape=(jax.ShapeDtypeStruct((rows, width), BF16), jax.ShapeDtypeStruct(shape, F32)),
        in_specs=[hbm, vm, vm, hbm],
        out_specs=(vm, vm),
        scratch_shapes=[
            pltpu.VMEM((2,) + shape, BF16),
            pltpu.VMEM(shape, BF16),
            pltpu.VMEM(shape, BF16),
            pltpu.VMEM(shape, BF16),
            pltpu.VMEM(shape, BF16),
            pltpu.VMEM((heads, rows, width), BF16),
            pltpu.VMEM((heads, rows, width), BF16),
            pltpu.VMEM(w.shape, BF16),
            pltpu.VMEM((rows, width), F32),
            pltpu.SMEM(owner.shape, jnp.int32),
            pltpu.VMEM((1, lanes), jnp.int32),
            pltpu.SMEM((1, lanes), jnp.int32),
            pltpu.SemaphoreType.DMA((2,)),
            pltpu.SemaphoreType.DMA((2, max(2, seq // 8))),
            pltpu.SemaphoreType.DMA((2,)),
            pltpu.SemaphoreType.DMA((2,)),
            pltpu.SemaphoreType.DMA((2, heads)),
            pltpu.SemaphoreType.DMA((3,)),
        ],
        compiler_params=pltpu.CompilerParams(
            collective_id=1, has_side_effects=True, vmem_limit_bytes=VMEM_LIMIT
        ),
        name="scatter",
    )(in_hbm(owner), pieces, att, in_hbm(w))
    return out, grad.reshape((1,) + dslots.shape[1:])


UNITS = 2

def attention_kernel(bounds, lanes, q_ref, g_ref, slots, rk, rv, att, dq, drk, drv, dslots, kt, vt, dk_acc, dv_acc, todo):
    heads = q_ref.shape[1] // 128
    plen = slots.shape[2]
    rows = rk.shape[0]
    scale = 128**-0.5
    c = scale * LOG2E
    tiles = q_ref.shape[0] // TILE
    width = TILE * heads
    for i in range(3):
        kt[i] = slots[i, 0].T
        vt[i] = slots[i, 1].T
    kt_r = rk[...].T
    vt_r = rv[...].T
    dk_acc[...] = jnp.zeros_like(dk_acc)
    dv_acc[...] = jnp.zeros_like(dv_acc)

    def list_tile(t, n):
        def list_pair(p, n):
            todo[0, n] = t
            todo[1, n] = p
            todo[2, n] = jnp.where(p == bounds[0, t], 1, 0)
            return n + 1

        return lax.fori_loop(bounds[0, t], bounds[1, t] + 1, list_pair, n)

    count = lax.fori_loop(0, tiles, list_tile, 0)
    for i in range(UNITS - 1):
        todo[0, count + i] = tiles - 1
        todo[1, count + i] = -1
        todo[2, count + i] = 0

    def load(n):
        t, p = todo[0, n], todo[1, n]
        t0 = pl.multiple_of(t * TILE, TILE)
        cut = [(pl.ds(t0, TILE), slice(h * 128, (h + 1) * 128)) for h in range(heads)]
        q = jnp.concatenate([q_ref[i] for i in cut], axis=0)
        g = jnp.concatenate([g_ref[i] for i in cut], axis=0)
        slot = jnp.maximum(p, 0)
        key_id = lax.broadcasted_iota(jnp.int32, (rows, width), 0)
        token = t0 + (lax.broadcasted_iota(jnp.int32, (1, width), 1) & (TILE - 1))
        visible = (key_id >= lanes[0, t]) & (key_id <= token)
        return dict(q=q, g=g, slot=slot, cut=cut, visible=visible, member=lanes[1, t] == p, first=todo[2, n] == 1)

    def scores(u):
        u["sp"] = dot(slots[u["slot"], 0], u["q"], 1, 1)
        u["sr"] = jnp.where(u["visible"], dot(rk[...], u["q"], 1, 1), -1e30)
        u["vp"] = dot(slots[u["slot"], 1], u["g"], 1, 1)
        u["vr"] = dot(rv[...], u["g"], 1, 1)

    def softmax(u):
        top = c * jnp.maximum(
            jnp.max(u["sp"], axis=0, keepdims=True), jnp.max(u["sr"], axis=0, keepdims=True)
        )
        ep = jnp.exp2(u["sp"] * c - top)
        er = jnp.exp2(u["sr"] * c - top)
        total = jnp.sum(ep, axis=0, keepdims=True) + jnp.sum(er, axis=0, keepdims=True)
        inverse = jnp.where(u["member"], 1.0 / total, 0.0)
        wp, wr = ep * inverse, er * inverse
        u["wpl"], u["wrl"] = wp.astype(BF16), wr.astype(BF16)
        dots = jnp.sum(wp * u["vp"], axis=0, keepdims=True) + jnp.sum(wr * u["vr"], axis=0, keepdims=True)
        u["gp"] = (wp * (u["vp"] - dots)).astype(BF16)
        u["gr"] = (wr * (u["vr"] - dots)).astype(BF16)

    def key_sums(u):
        pr = pl.multiple_of(u["slot"] * plen, plen)
        dv_acc[pl.ds(pr, plen)] += dot(u["wpl"], u["g"], 1, 0)
        dk_acc[pl.ds(pr, plen)] += dot(u["gp"], u["q"], 1, 0)
        dv_acc[3 * plen :] += dot(u["wrl"], u["g"], 1, 0)
        dk_acc[3 * plen :] += dot(u["gr"], u["q"], 1, 0)

    def row_sums(u):
        o = (dot(vt[u["slot"]], u["wpl"], 1, 0) + dot(vt_r, u["wrl"], 1, 0)).T.astype(BF16)
        d = ((dot(kt[u["slot"]], u["gp"], 1, 0) + dot(kt_r, u["gr"], 1, 0)) * scale).T.astype(BF16)
        for ref, val in ((att, o), (dq, d)):
            for h, i in enumerate(u["cut"]):
                new = val[h * TILE : (h + 1) * TILE]
                ref[i] = jnp.where(u["first"], new, ref[i] + new)

    def step(i, _):
        units = [load(UNITS * i + n) for n in range(UNITS)]
        for part in (scores, softmax, key_sums, row_sums):
            for u in units:
                part(u)
        return 0

    lax.fori_loop(0, (count + UNITS - 1) // UNITS, step, 0)
    for i in range(3):
        dslots[i, 0] = (dk_acc[i * plen : (i + 1) * plen] * scale).astype(BF16)
        dslots[i, 1] = dv_acc[i * plen : (i + 1) * plen].astype(BF16)
    drk[...] = (dk_acc[3 * plen :] * scale).astype(BF16)
    drv[...] = dv_acc[3 * plen :].astype(BF16)


def attention(tokens, k, q, g, slots, rk, rv):
    rows, feat = q.shape
    plen = slots.shape[2]
    heads = feat // 128
    tiles = rows // TILE
    start = jnp.sum((tokens[None, :] < tokens[:, None]).astype(jnp.int32), axis=1)
    slot = tokens // GROUP - (k - 1)
    lanes = jnp.stack([jnp.tile(x.reshape(tiles, 1, TILE), (1, 1, heads)) for x in (start, slot)])
    by_tile = slot.reshape(tiles, TILE)
    bounds = jnp.stack([by_tile[:, 0], by_tile[:, -1]])
    vm = pl.BlockSpec(memory_space=pltpu.VMEM)
    return pl.pallas_call(
        attention_kernel,
        out_shape=(
            jax.ShapeDtypeStruct(q.shape, BF16),
            jax.ShapeDtypeStruct(q.shape, BF16),
            jax.ShapeDtypeStruct(rk.shape, BF16),
            jax.ShapeDtypeStruct(rv.shape, BF16),
            jax.ShapeDtypeStruct(slots.shape, BF16),
        ),
        in_specs=[pl.BlockSpec(memory_space=pltpu.SMEM)] + [vm] * 6,
        out_specs=(vm,) * 5,
        scratch_shapes=[
            pltpu.VMEM((3, 128, plen), BF16),
            pltpu.VMEM((3, 128, plen), BF16),
            pltpu.VMEM((3 * plen + rows, 128), F32),
            pltpu.VMEM((3 * plen + rows, 128), F32),
            pltpu.SMEM((3, tiles + 2 + UNITS), jnp.int32),
        ],
        compiler_params=pltpu.CompilerParams(vmem_limit_bytes=40 * 2**20),
        name="attention",
    )(bounds, lanes, q, g, slots, rk, rv)


def per_device(
    token_response, prompt_owner, queries, resp_keys, resp_values, prompt_kv, out_weight, out_grad
):
    seq, heads = lax.axis_size("seq"), lax.axis_size("head")
    slots, attn_grad = gather(prompt_owner, prompt_kv, out_grad, out_weight, seq, heads)
    attended, query_grad, key_grad, value_grad, slot_grads = attention(
        token_response, lax.axis_index("seq"), queries, attn_grad, slots, resp_keys, resp_values
    )
    layer_out, prompt_kv_grad = scatter(prompt_owner, slot_grads, attended, out_weight, seq, heads)
    return (layer_out, query_grad, key_grad, value_grad, prompt_kv_grad)


def solution(mesh):
    placed = (
        P("seq"),
        P(),
        P("seq", "head"),
        P("seq", "head"),
        P("seq", "head"),
        P("seq", None, None, "head"),
        P("head", None),
        P("seq", "head"),
    )
    return jax.shard_map(
        per_device,
        mesh=mesh,
        in_specs=placed,
        out_specs=(
            P("seq", "head"),
            P("seq", "head"),
            P("seq", "head"),
            P("seq", "head"),
            P("seq", None, None, "head"),
        ),
        check_vma=False,
    )
```

```python
import functools

import jax
import jax.numpy as jnp
from jax import lax
from jax.experimental import pallas as pl
from jax.experimental.pallas import tpu as pltpu
from jax.sharding import PartitionSpec as P

GROUP = 16
TILE = 32
LOG2E = 1.4426950408889634
F32, BF16 = jnp.float32, jnp.bfloat16
MESH = pl.DeviceIdType.MESH
VMEM_LIMIT = 52 * 2**20


def dot(a, b, ca, cb):
    return lax.dot_general(a, b, (((ca,), (cb,)), ((), ())), preferred_element_type=F32)


def at_seq(j):
    return (j, lax.axis_index("head"))


def at_head(j):
    return (lax.axis_index("seq"), j)


def greet(seq, heads):
    me, mine = lax.axis_index("seq"), lax.axis_index("head")
    barrier = pltpu.get_barrier_semaphore()

    def tell(i, _):
        pl.semaphore_signal(barrier, inc=1, device_id=at_seq(lax.rem(me + i, seq)), device_id_type=MESH)
        return 0

    lax.fori_loop(1, seq, tell, 0)
    for i in range(1, heads):
        pl.semaphore_signal(barrier, inc=1, device_id=at_head(lax.rem(mine + i, heads)), device_id_type=MESH)


def all_in(seq, heads):
    pl.semaphore_wait(pltpu.get_barrier_semaphore(), seq - 1 + heads - 1)


def each_peer(seq, visit):
    me = lax.axis_index("seq")
    core, chip, chips = lax.rem(me, 2), me // 2, seq // 2
    visit(me + 1 - 2 * core)
    for c in range(2):

        def go(t, _):
            visit(2 * lax.rem(chip + t, chips) + c)
            return 0

        lax.fori_loop(1, chips, go, 0)


def in_hbm(x):
    return pltpu.with_memory_space_constraint(x, pltpu.HBM)


def wait_bytes(ref, sem):
    pltpu.make_async_copy(ref, ref, sem).wait()


def add_all(terms):
    return functools.reduce(lambda a, b: a + b, terms)


def count_if(condition):
    return jnp.where(condition, 1, 0)


def layer_kernel(
    seq, heads,
    tok_hbm, row_hbm, owner_hbm, q_hbm, rk_hbm, rv_hbm, kv, og, w_hbm,
    out, dq, drk, drv, grad,
    tok, owner, inverse, unit, tile_first, tile_count,
    row, q, rk, rv, w, ogs,
    first, order, slots, lanes, qp, gp, er, vr, rstat,
    weights, sgrads, ustat, dks, dvs,
    dslots, near, summed, second, back, inverse_row,
    kt, vt, ot, dqt, att, drk_acc, drv_acc, parts, got, own_part,
    sem_in1, sem_in2s, sem_in2, sem_near, sem_og, local, sem_back_s, sem_back, sem_out1, sem_out2, sem_parts,
):
    me, mine = lax.axis_index("seq"), lax.axis_index("head")
    groups = max(2, seq // 8)
    per = seq // groups
    group = me // per
    half = seq // 2
    rows, feat = q.shape
    plen = kt.shape[2]
    width = og.shape[1]
    tiles = rows // TILE
    per_group = feat // 128
    lanes_n = TILE * per_group
    units = tiles + 2
    scale = 128**-0.5
    c = scale * LOG2E
    up, down = lax.rem(me + 1, seq), lax.rem(me + seq - 1, seq)

    loads = {}
    for n, (name, src, dst) in enumerate(
        (
            ("tok", tok_hbm, tok),
            ("owner", owner_hbm, owner),
            ("piece", kv.at[me], first.at[me]),
            ("row", row_hbm, row),
            ("q", q_hbm, q),
            ("rk", rk_hbm, rk),
            ("rv", rv_hbm, rv),
            ("og", og, ogs.at[mine]),
            ("w", w_hbm, w),
        )
    ):
        loads[name] = pltpu.make_async_copy(src, dst, local.at[n])
        loads[name].start()
    greet(seq, heads)
    all_in(seq, heads)

    def spread(j):
        pltpu.make_async_remote_copy(
            kv.at[j], first.at[me], sem_in1.at[0], sem_in1.at[1], device_id=at_seq(j), device_id_type=MESH
        ).start()

    each_peer(seq, spread)
    og_copies = []
    for i in range(1, heads):
        copy = pltpu.make_async_remote_copy(
            og, ogs.at[mine], sem_og.at[0, i], sem_og.at[1, heads - i],
            device_id=at_head(lax.rem(mine + i, heads)), device_id_type=MESH,
        )
        copy.start()
        og_copies.append(copy)

    loads["tok"].wait()
    low = [lax.div(tok[t * TILE], GROUP) - (me - 1) for t in range(tiles)]
    high = [lax.div(tok[t * TILE + TILE - 1], GROUP) - (me - 1) for t in range(tiles)]
    offset = [jnp.int32(0)]
    for t in range(tiles):
        offset.append(offset[t] + high[t] - low[t] + 1)
        tile_first[t] = offset[t]
        tile_count[t] = high[t] - low[t] + 1
    slot_of_unit = []
    for n in range(units):
        t_n = add_all([count_if(offset[t] <= n) for t in range(1, tiles)])
        relative = low[0]
        for t in range(1, tiles):
            relative = jnp.where(offset[t] <= n, low[t] - offset[t], relative)
        p_n = relative + n
        s_n = jnp.clip(p_n, 0, 2)
        unit[0, n] = t_n
        unit[1, n] = p_n
        unit[2, n] = s_n
        unit[3, n] = count_if(s_n == slot_of_unit[-1]) if n else jnp.int32(0)
        slot_of_unit.append(s_n)
    slot_last = [add_all([count_if(s <= i) for s in slot_of_unit]) for i in range(3)]
    slot_used = [add_all([count_if(s == i) for s in slot_of_unit]) > 0 for i in range(3)]

    loads["row"].wait()
    row_f = row[...].astype(F32)
    column = jnp.broadcast_to(row_f, (128, rows)).T
    earlier = jnp.concatenate([column] * (-(-rows // 128)), axis=1)[:, :rows] < row_f
    start = jnp.sum(jnp.where(earlier, 1.0, 0.0), axis=0, keepdims=True)
    slot_row = (lax.div(row[...], GROUP) - (me - 1)).astype(F32)
    pick = lax.broadcasted_iota(jnp.int32, (16, rows), 0)
    facts = jnp.where(pick == 0, start, jnp.where(pick == 1, slot_row, 0.0)).astype(BF16)
    source = lax.broadcasted_iota(jnp.int32, (rows, lanes_n), 0)
    lane = lax.broadcasted_iota(jnp.int32, (rows, lanes_n), 1) & (TILE - 1)
    for t in range(tiles):
        chosen = jnp.where(source == lane + t * TILE, 1.0, 0.0).astype(BF16)
        lanes[t] = dot(facts, chosen, 1, 0)
    loads["q"].wait()
    for t in range(tiles):
        for h in range(per_group):
            qp[t, h * TILE : (h + 1) * TILE] = q[t * TILE : (t + 1) * TILE, h * 128 : (h + 1) * 128]

    spans = []
    for t in range(tiles):
        span = min(rows, -(-((t + 1) * TILE) // 128) * 128)
        if spans and spans[-1][2] == span:
            spans[-1][1] = t + 1
        else:
            spans.append([t, t + 1, span])

    def each_tile(step):
        for begin, end, span in spans:
            lax.fori_loop(begin, end, lambda t, _: (step(t, span), 0)[1], 0)

    def own_scores(t, span):
        key_id = lax.broadcasted_iota(jnp.int32, (span, lanes_n), 0)
        token = t * TILE + (lax.broadcasted_iota(jnp.int32, (1, lanes_n), 1) & (TILE - 1))
        visible = (key_id >= lanes[t, 0:1].astype(jnp.int32)) & (key_id <= token)
        s = jnp.where(visible, dot(rk[0:span], qp[t], 1, 1) * c, -1e30)
        top = jnp.max(s, axis=0, keepdims=True)
        e = jnp.exp2(s - top)
        er[t, 0:span] = e
        rstat[t, 0:1] = top
        rstat[t, 1:2] = jnp.sum(e, axis=0, keepdims=True)

    loads["rk"].wait()
    each_tile(own_scores)

    loads["owner"].wait()
    loads["piece"].wait()
    wait_bytes(first.at[pl.ds(0, seq - 1)], sem_in1.at[1])

    def deliver(p):
        order[p] = first[owner[p]]
        pltpu.make_async_remote_copy(
            order.at[p], slots.at[1, me], sem_in2s, sem_in2.at[group], device_id=at_seq(p), device_id_type=MESH
        ).start()

    each_peer(seq, deliver)
    slots[1, me] = first[owner[me]]

    loads["og"].wait()
    loads["w"].wait()
    for copy in og_copies:
        copy.wait_recv()
    block = 256

    def project(n, _):
        r = pl.multiple_of(n * block, block)
        total = dot(ogs[0], w[pl.ds(r, block), 0:width], 1, 1)
        for h in range(1, heads):
            total += dot(ogs[h], w[pl.ds(r, block), h * width : (h + 1) * width], 1, 1)
        total = total.astype(BF16)
        for t in range(tiles):
            for h in range(block // 128):
                at = pl.multiple_of((n * (block // 128) + h) * TILE, TILE)
                gp[t, pl.ds(at, TILE)] = total[t * TILE : (t + 1) * TILE, h * 128 : (h + 1) * 128]
        return 0

    lax.fori_loop(0, feat // block, project, 0)
    loads["rv"].wait()

    def own_dots(t, span):
        v = dot(rv[0:span], gp[t], 1, 1)
        vr[t, 0:span] = v
        rstat[t, 2:3] = jnp.sum(v * er[t, 0:span], axis=0, keepdims=True)

    each_tile(own_dots)
    dks[0] = jnp.zeros(dks.shape[1:], F32)
    dvs[0] = jnp.zeros(dvs.shape[1:], F32)
    for n in range(groups):
        g = lax.rem(group + 2 * groups - 1 - n, groups)
        arrived = per if n < groups - 1 else per - 1
        wait_bytes(slots.at[1, pl.ds(0, arrived)], sem_in2.at[g])
        part = pl.ds(g * per, per)
        pltpu.make_async_remote_copy(
            slots.at[1, part], slots.at[0, part], sem_near.at[0], sem_near.at[1],
            device_id=at_seq(up), device_id_type=MESH,
        ).start()
        pltpu.make_async_remote_copy(
            slots.at[1, part], slots.at[2, part], sem_near.at[2], sem_near.at[3],
            device_id=at_seq(down), device_id_type=MESH,
        ).start()
    wait_bytes(slots.at[0], sem_near.at[1])
    wait_bytes(slots.at[2], sem_near.at[3])

    def load_unit(n):
        t = unit[0, n]
        s = unit[2, n]
        member = lanes[t, 1:2].astype(jnp.int32) == unit[1, n]
        stat = rstat[t]
        return dict(
            n=n, s=s, q=qp[t], g=gp[t], member=member, same=unit[3, n] == 1,
            top=stat[0:1], total=stat[1:2], dots=stat[2:3],
        )

    def scores(u):
        k = slots[u["s"], 0:half].reshape(plen, 128)
        v = slots[u["s"], half:seq].reshape(plen, 128)
        u["sp"] = dot(k, u["q"], 1, 1)
        u["vp"] = dot(v, u["g"], 1, 1)

    def softmax(u):
        top = jnp.maximum(c * jnp.max(u["sp"], axis=0, keepdims=True), u["top"])
        e = jnp.exp2(u["sp"] * c - top)
        own = jnp.exp2(u["top"] - top)
        total = jnp.sum(e, axis=0, keepdims=True) + u["total"] * own
        inv = jnp.where(u["member"], 1.0 / total, 0.0)
        wp = e * inv
        dots = jnp.sum(wp * u["vp"], axis=0, keepdims=True) + u["dots"] * (own * inv)
        n = u["n"]
        u["wl"] = wp.astype(BF16)
        u["gl"] = (wp * (u["vp"] - dots)).astype(BF16)
        weights[n] = u["wl"]
        sgrads[n] = u["gl"]
        ustat[n, 0:1] = own * inv
        ustat[n, 1:2] = dots

    def key_sums(u):
        n = u["n"]
        dvs[n + 1] = jnp.where(u["same"], dvs[n], 0.0) + dot(u["wl"], u["g"], 1, 0)
        dks[n + 1] = jnp.where(u["same"], dks[n], 0.0) + dot(u["gl"], u["q"], 1, 0)

    def pair(i, _):
        two = [load_unit(2 * i), load_unit(2 * i + 1)]
        for stage in (scores, softmax, key_sums):
            for u in two:
                stage(u)
        return 0

    lax.fori_loop(0, units // 2, pair, 0)

    def place(i):
        dslots[i, 0:half] = jnp.where(slot_used[i], dks[slot_last[i]] * scale, 0.0).astype(BF16).reshape(
            half, -1, 128
        )
        dslots[i, half:seq] = jnp.where(slot_used[i], dvs[slot_last[i]], 0.0).astype(BF16).reshape(half, -1, 128)

    place(0)
    place(2)
    for n in range(groups):
        part = pl.ds(lax.rem(group + n, groups) * per, per)
        at = lax.rem(group + n, groups)
        pltpu.make_async_remote_copy(
            dslots.at[2, part], near.at[0, part], sem_back_s.at[0], sem_back.at[0, at],
            device_id=at_seq(up), device_id_type=MESH,
        ).start()
        pltpu.make_async_remote_copy(
            dslots.at[0, part], near.at[1, part], sem_back_s.at[1], sem_back.at[1, at],
            device_id=at_seq(down), device_id_type=MESH,
        ).start()
    place(1)

    spot = lax.broadcasted_iota(jnp.int32, inverse_row.shape, 1)
    found = jnp.zeros(inverse_row.shape, jnp.int32)
    for p in range(seq):
        found = jnp.where(spot == owner[p], p, found)
    inverse_row[...] = found
    to_scalars = pltpu.make_async_copy(inverse_row, inverse, local.at[len(loads)])
    to_scalars.start()
    for i in range(3):
        vt[i] = slots[i, half:seq].reshape(plen, 128).T

    def unit_rows(n, _):
        ot[n] = dot(vt[unit[2, n]], weights[n], 1, 0)
        return 0

    lax.fori_loop(0, units, unit_rows, 0)

    at_start, at_end = me == 0, me == seq - 1
    for n in range(groups):
        g = lax.rem(group + n, groups)
        part = pl.ds(g * per, per)
        wait_bytes(near.at[0, part], sem_back.at[0, g])
        wait_bytes(near.at[1, part], sem_back.at[1, g])
        below = jnp.where(at_start, 0.0, near[0, part].astype(F32))
        above = jnp.where(at_end, 0.0, near[1, part].astype(F32))
        summed[part] = (dslots[1, part].astype(F32) + below + above).astype(BF16)
        for i in range(per):
            j = g * per + i

            @pl.when(j != me)
            def _():
                pltpu.make_async_remote_copy(
                    summed.at[j], second.at[me], sem_out1.at[0], sem_out1.at[1],
                    device_id=at_seq(j), device_id_type=MESH,
                ).start()

    second[me] = summed[me]

    def of_tile(t, ref, row_slice=slice(None)):
        begin, many = tile_first[t], tile_count[t]
        total = ref[begin, row_slice]
        for j in range(1, 3):
            total += jnp.where(many > j, ref[jnp.minimum(begin + j, units - 1), row_slice], 0.0)
        return total

    def unit_facts(t):
        begin, many = tile_first[t], tile_count[t]
        slot = lanes[t, 1:2].astype(jnp.int32)
        factor, dots = 0.0, 0.0
        for j in range(3):
            n = jnp.minimum(begin + j, units - 1)
            member = (slot == unit[1, n]) & (many > j)
            factor += jnp.where(member, ustat[n, 0:1], 0.0)
            dots += jnp.where(member, ustat[n, 1:2], 0.0)
        return factor, dots

    rvt = rv[...].T

    def attend(t, span):
        factor, _ = unit_facts(t)
        o = of_tile(t, ot) + dot(rvt[:, 0:span], (er[t, 0:span] * factor).astype(BF16), 1, 0)
        o = o.T.astype(BF16)
        for h in range(per_group):
            att[pl.ds(pl.multiple_of(t * TILE, TILE), TILE), h * 128 : (h + 1) * 128] = o[h * TILE : (h + 1) * TILE]

    each_tile(attend)

    def share(i):
        peer = lax.rem(mine + i, heads)
        return dot(att[...], w[:, pl.ds(pl.multiple_of(peer * width, width), width)], 1, 0)

    part_copies = []
    for i in range(1, heads):
        parts[i] = share(i).astype(BF16)
        copy = pltpu.make_async_remote_copy(
            parts.at[i], got.at[i], sem_parts.at[0, i], sem_parts.at[1, i],
            device_id=at_head(lax.rem(mine + i, heads)), device_id_type=MESH,
        )
        copy.start()
        part_copies.append(copy)

    to_scalars.wait()
    wait_bytes(second.at[pl.ds(0, seq - 1)], sem_out1.at[1])
    wait_bytes(order.at[pl.ds(0, seq - 1)], sem_in2s)

    def give_back(o):
        order[o] = second[inverse[0, o]]
        pltpu.make_async_remote_copy(
            order.at[o], back.at[me], sem_out2.at[0], sem_out2.at[1], device_id=at_seq(o), device_id_type=MESH
        ).start()

    each_peer(seq, give_back)
    back[me] = second[inverse[0, me]]

    own_part[...] = share(0)
    for i in range(3):
        kt[i] = slots[i, 0:half].reshape(plen, 128).T

    def unit_query(n, _):
        dqt[n] = dot(kt[unit[2, n]], sgrads[n], 1, 0)
        return 0

    lax.fori_loop(0, units, unit_query, 0)
    rkt = rk[...].T
    drk_acc[...] = jnp.zeros_like(drk_acc)
    drv_acc[...] = jnp.zeros_like(drv_acc)

    def own_grads(t, span):
        factor, dots = unit_facts(t)
        wr = er[t, 0:span] * factor
        gr = (wr * (vr[t, 0:span] - dots)).astype(BF16)
        drv_acc[0:span] += dot(wr.astype(BF16), gp[t], 1, 0)
        drk_acc[0:span] += dot(gr, qp[t], 1, 0)
        d = ((of_tile(t, dqt) + dot(rkt[:, 0:span], gr, 1, 0)) * scale).T.astype(BF16)
        for h in range(per_group):
            dq[pl.ds(pl.multiple_of(t * TILE, TILE), TILE), h * 128 : (h + 1) * 128] = d[h * TILE : (h + 1) * TILE]

    each_tile(own_grads)
    drk[...] = (drk_acc[...] * scale).astype(BF16)
    drv[...] = drv_acc[...].astype(BF16)
    for copy in part_copies:
        copy.wait_recv()
    total = own_part[...]
    for i in range(1, heads):
        total += got[i].astype(F32)
    out[...] = total.astype(BF16)

    for copy in og_copies + part_copies:
        copy.wait_send()
    wait_bytes(first.at[pl.ds(0, seq - 1)], sem_in1.at[0])
    wait_bytes(slots.at[1], sem_near.at[0])
    wait_bytes(slots.at[1], sem_near.at[2])
    wait_bytes(near.at[0], sem_back_s.at[0])
    wait_bytes(near.at[1], sem_back_s.at[1])
    wait_bytes(second.at[pl.ds(0, seq - 1)], sem_out1.at[0])
    wait_bytes(order.at[pl.ds(0, seq - 1)], sem_out2.at[0])
    wait_bytes(back.at[pl.ds(0, seq - 1)], sem_out2.at[1])
    grad[...] = back[...].astype(F32)


def store_kernel(*refs):
    many = (len(refs) - 1) // 2
    copies = [pltpu.make_async_copy(refs[i], refs[many + i], refs[-1].at[i]) for i in range(many)]
    for copy in copies:
        copy.start()
    for copy in copies:
        copy.wait()


def per_device(
    token_response, prompt_owner, queries, resp_keys, resp_values, prompt_kv, out_weight, out_grad
):
    seq, heads = lax.axis_size("seq"), lax.axis_size("head")
    vm = pl.BlockSpec(memory_space=pltpu.VMEM)
    hbm = pl.BlockSpec(memory_space=pltpu.HBM)
    pieces = prompt_kv.reshape(seq, -1, 128)
    plen = prompt_kv.shape[2]
    rows, feat = queries.shape
    width = out_grad.shape[1]
    tiles = rows // TILE
    units = tiles + 2
    lanes = TILE * feat // 128
    wide = -(-seq // 128) * 128
    groups = max(2, seq // 8)
    dma = pltpu.SemaphoreType.DMA
    shapes = (
        jax.ShapeDtypeStruct((rows, width), BF16),
        jax.ShapeDtypeStruct(queries.shape, BF16),
        jax.ShapeDtypeStruct(resp_keys.shape, BF16),
        jax.ShapeDtypeStruct(resp_values.shape, BF16),
        jax.ShapeDtypeStruct(pieces.shape, F32),
    )
    operands = (
        token_response, token_response.reshape(1, rows), prompt_owner, queries, resp_keys, resp_values,
        pieces, out_grad, out_weight,
    )
    results = pl.pallas_call(
        functools.partial(layer_kernel, seq, heads),
        out_shape=shapes,
        in_specs=[hbm] * len(operands),
        out_specs=(vm,) * len(shapes),
        scratch_shapes=[
            pltpu.SMEM((rows,), jnp.int32),
            pltpu.SMEM((seq,), jnp.int32),
            pltpu.SMEM((1, wide), jnp.int32),
            pltpu.SMEM((4, units), jnp.int32),
            pltpu.SMEM((tiles,), jnp.int32),
            pltpu.SMEM((tiles,), jnp.int32),
            pltpu.VMEM((1, rows), jnp.int32),
            pltpu.VMEM(queries.shape, BF16),
            pltpu.VMEM(resp_keys.shape, BF16),
            pltpu.VMEM(resp_values.shape, BF16),
            pltpu.VMEM(out_weight.shape, BF16),
            pltpu.VMEM((heads, rows, width), BF16),
            pltpu.VMEM(pieces.shape, BF16),
            pltpu.VMEM(pieces.shape, BF16),
            pltpu.VMEM((3,) + pieces.shape, BF16),
            pltpu.VMEM((tiles, 16, lanes), F32),
            pltpu.VMEM((tiles, lanes, 128), BF16),
            pltpu.VMEM((tiles, lanes, 128), BF16),
            pltpu.VMEM((tiles, rows, lanes), F32),
            pltpu.VMEM((tiles, rows, lanes), F32),
            pltpu.VMEM((tiles, 8, lanes), F32),
            pltpu.VMEM((units, plen, lanes), BF16),
            pltpu.VMEM((units, plen, lanes), BF16),
            pltpu.VMEM((units, 8, lanes), F32),
            pltpu.VMEM((units + 1, plen, 128), F32),
            pltpu.VMEM((units + 1, plen, 128), F32),
            pltpu.VMEM((3,) + pieces.shape, BF16),
            pltpu.VMEM((2,) + pieces.shape, BF16),
            pltpu.VMEM(pieces.shape, BF16),
            pltpu.VMEM(pieces.shape, BF16),
            pltpu.VMEM(pieces.shape, BF16),
            pltpu.VMEM((1, wide), jnp.int32),
            pltpu.VMEM((3, 128, plen), BF16),
            pltpu.VMEM((3, 128, plen), BF16),
            pltpu.VMEM((units, 128, lanes), F32),
            pltpu.VMEM((units, 128, lanes), F32),
            pltpu.VMEM(queries.shape, BF16),
            pltpu.VMEM(resp_keys.shape, F32),
            pltpu.VMEM(resp_keys.shape, F32),
            pltpu.VMEM((heads, rows, width), BF16),
            pltpu.VMEM((heads, rows, width), BF16),
            pltpu.VMEM((rows, width), F32),
            dma((2,)),
            dma,
            dma((groups,)),
            dma((4,)),
            dma((2, heads)),
            dma((10,)),
            dma((2,)),
            dma((2, groups)),
            dma((2,)),
            dma((2,)),
            dma((2, heads)),
        ],
        compiler_params=pltpu.CompilerParams(
            collective_id=0, has_side_effects=True, vmem_limit_bytes=VMEM_LIMIT
        ),
        name="layer",
    )(*(in_hbm(x) for x in operands))
    layer_out, query_grad, key_grad, value_grad, prompt_grad = pl.pallas_call(
        store_kernel,
        out_shape=shapes,
        in_specs=[pl.BlockSpec(memory_space=pl.ANY)] * len(shapes),
        out_specs=(pl.BlockSpec(memory_space=pl.ANY),) * len(shapes),
        scratch_shapes=[dma((len(shapes),))],
        name="store",
    )(*results)
    return (layer_out, query_grad, key_grad, value_grad, prompt_grad.reshape(prompt_kv.shape))


def solution(mesh):
    placed = (
        P("seq"),
        P(),
        P("seq", "head"),
        P("seq", "head"),
        P("seq", "head"),
        P("seq", None, None, "head"),
        P("head", None),
        P("seq", "head"),
    )
    return jax.shard_map(
        per_device,
        mesh=mesh,
        in_specs=placed,
        out_specs=(
            P("seq", "head"),
            P("seq", "head"),
            P("seq", "head"),
            P("seq", "head"),
            P("seq", None, None, "head"),
        ),
        check_vma=False,
    )
```

```python
import functools

import jax
import jax.numpy as jnp
from jax import lax
from jax.experimental import pallas as pl
from jax.experimental.pallas import tpu as pltpu
from jax.sharding import PartitionSpec as P

GROUP = 16
TILE = 32
LOG2E = 1.4426950408889634
F32, BF16 = jnp.float32, jnp.bfloat16
MESH = pl.DeviceIdType.MESH
VMEM_LIMIT = 52 * 2**20


def dot(a, b, ca, cb):
    return lax.dot_general(a, b, (((ca,), (cb,)), ((), ())), preferred_element_type=F32)


def at_seq(j):
    return (j, lax.axis_index("head"))


def at_head(j):
    return (lax.axis_index("seq"), j)


def greet(seq, heads):
    me, mine = lax.axis_index("seq"), lax.axis_index("head")
    barrier = pltpu.get_barrier_semaphore()

    def tell(i, _):
        pl.semaphore_signal(barrier, inc=1, device_id=at_seq(lax.rem(me + i, seq)), device_id_type=MESH)
        return 0

    lax.fori_loop(1, seq, tell, 0)
    for i in range(1, heads):
        pl.semaphore_signal(barrier, inc=1, device_id=at_head(lax.rem(mine + i, heads)), device_id_type=MESH)


def all_in(seq, heads):
    pl.semaphore_wait(pltpu.get_barrier_semaphore(), seq - 1 + heads - 1)


def each_peer(seq, visit):
    me = lax.axis_index("seq")
    core, chip, chips = lax.rem(me, 2), me // 2, seq // 2
    visit(me + 1 - 2 * core)
    for c in range(2):

        def go(t, _):
            visit(2 * lax.rem(chip + t, chips) + c)
            return 0

        lax.fori_loop(1, chips, go, 0)


def in_hbm(x):
    return pltpu.with_memory_space_constraint(x, pltpu.HBM)


def wait_bytes(ref, sem):
    pltpu.make_async_copy(ref, ref, sem).wait()


def add_all(terms):
    return functools.reduce(lambda a, b: a + b, terms)


def count_if(condition):
    return jnp.where(condition, 1, 0)


def layer_kernel(
    seq, heads,
    tok_hbm, row_hbm, owner_hbm, q_hbm, rk_hbm, rv_hbm, kv, og, w_hbm,
    out, dq, drk, drv, grad,
    tok, owner, inverse, unit, tile_first, tile_count,
    row, q, rk, rv, w, ogs,
    first, order, slots, lanes, qp, gp, er, vr, rstat,
    weights, sgrads, ustat, dks, dvs,
    dslots, near, summed, second, back, inverse_row,
    kt, vt, ot, dqt, att, drk_acc, drv_acc, parts, got, own_part,
    sem_in1, sem_in2s, sem_in2, sem_near, sem_og, local, sem_back_s, sem_back, sem_out1, sem_out2, sem_parts,
):
    me, mine = lax.axis_index("seq"), lax.axis_index("head")
    groups = max(2, seq // 8)
    per = seq // groups
    group = me // per
    half = seq // 2
    rows, feat = q.shape
    plen = kt.shape[2]
    width = og.shape[1]
    tiles = rows // TILE
    per_group = feat // 128
    lanes_n = TILE * per_group
    units = tiles + 2
    scale = 128**-0.5
    c = scale * LOG2E
    up, down = lax.rem(me + 1, seq), lax.rem(me + seq - 1, seq)

    loads = {}
    for n, (name, src, dst) in enumerate(
        (
            ("tok", tok_hbm, tok),
            ("owner", owner_hbm, owner),
            ("piece", kv.at[me], first.at[me]),
            ("row", row_hbm, row),
            ("q", q_hbm, q),
            ("rk", rk_hbm, rk),
            ("rv", rv_hbm, rv),
            ("og", og, ogs.at[mine]),
            ("w", w_hbm, w),
        )
    ):
        loads[name] = pltpu.make_async_copy(src, dst, local.at[n])
        loads[name].start()
    greet(seq, heads)
    all_in(seq, heads)

    def spread(j):
        pltpu.make_async_remote_copy(
            kv.at[j], first.at[me], sem_in1.at[0], sem_in1.at[1], device_id=at_seq(j), device_id_type=MESH
        ).start()

    each_peer(seq, spread)
    og_copies = []
    for i in range(1, heads):
        copy = pltpu.make_async_remote_copy(
            og, ogs.at[mine], sem_og.at[0, i], sem_og.at[1, heads - i],
            device_id=at_head(lax.rem(mine + i, heads)), device_id_type=MESH,
        )
        copy.start()
        og_copies.append(copy)

    loads["tok"].wait()
    low = [lax.div(tok[t * TILE], GROUP) - (me - 1) for t in range(tiles)]
    high = [lax.div(tok[t * TILE + TILE - 1], GROUP) - (me - 1) for t in range(tiles)]
    offset = [jnp.int32(0)]
    for t in range(tiles):
        offset.append(offset[t] + high[t] - low[t] + 1)
        tile_first[t] = offset[t]
        tile_count[t] = high[t] - low[t] + 1
    slot_of_unit = []
    for n in range(units):
        t_n = add_all([count_if(offset[t] <= n) for t in range(1, tiles)])
        relative = low[0]
        for t in range(1, tiles):
            relative = jnp.where(offset[t] <= n, low[t] - offset[t], relative)
        p_n = relative + n
        s_n = jnp.clip(p_n, 0, 2)
        unit[0, n] = t_n
        unit[1, n] = p_n
        unit[2, n] = s_n
        unit[3, n] = count_if(s_n == slot_of_unit[-1]) if n else jnp.int32(0)
        slot_of_unit.append(s_n)
    slot_last = [add_all([count_if(s <= i) for s in slot_of_unit]) for i in range(3)]
    slot_used = [add_all([count_if(s == i) for s in slot_of_unit]) > 0 for i in range(3)]

    loads["row"].wait()
    row_f = row[...].astype(F32)
    column = jnp.broadcast_to(row_f, (128, rows)).T
    earlier = jnp.concatenate([column] * (-(-rows // 128)), axis=1)[:, :rows] < row_f
    start = jnp.sum(jnp.where(earlier, 1.0, 0.0), axis=0, keepdims=True)
    slot_row = (lax.div(row[...], GROUP) - (me - 1)).astype(F32)
    pick = lax.broadcasted_iota(jnp.int32, (16, rows), 0)
    facts = jnp.where(pick == 0, start, jnp.where(pick == 1, slot_row, 0.0)).astype(BF16)
    source = lax.broadcasted_iota(jnp.int32, (rows, lanes_n), 0)
    lane = lax.broadcasted_iota(jnp.int32, (rows, lanes_n), 1) & (TILE - 1)
    for t in range(tiles):
        chosen = jnp.where(source == lane + t * TILE, 1.0, 0.0).astype(BF16)
        lanes[t] = dot(facts, chosen, 1, 0)
    loads["q"].wait()
    for t in range(tiles):
        for h in range(per_group):
            qp[t, h * TILE : (h + 1) * TILE] = q[t * TILE : (t + 1) * TILE, h * 128 : (h + 1) * 128]

    spans = []
    for t in range(tiles):
        span = min(rows, -(-((t + 1) * TILE) // 128) * 128)
        if spans and spans[-1][2] == span:
            spans[-1][1] = t + 1
        else:
            spans.append([t, t + 1, span])

    def each_tile(step):
        for begin, end, span in spans:
            lax.fori_loop(begin, end, lambda t, _: (step(t, span), 0)[1], 0)

    def own_scores(t, span):
        key_id = lax.broadcasted_iota(jnp.int32, (span, lanes_n), 0)
        token = t * TILE + (lax.broadcasted_iota(jnp.int32, (1, lanes_n), 1) & (TILE - 1))
        visible = (key_id >= lanes[t, 0:1].astype(jnp.int32)) & (key_id <= token)
        s = jnp.where(visible, dot(rk[0:span], qp[t], 1, 1) * c, -1e30)
        top = jnp.max(s, axis=0, keepdims=True)
        e = jnp.exp2(s - top)
        er[t, 0:span] = e
        rstat[t, 0:1] = top
        rstat[t, 1:2] = jnp.sum(e, axis=0, keepdims=True)

    loads["rk"].wait()
    each_tile(own_scores)

    loads["owner"].wait()
    loads["piece"].wait()
    wait_bytes(first.at[pl.ds(0, seq - 1)], sem_in1.at[1])

    def deliver(p):
        order[p] = first[owner[p]]
        pltpu.make_async_remote_copy(
            order.at[p], slots.at[1, me], sem_in2s, sem_in2.at[group], device_id=at_seq(p), device_id_type=MESH
        ).start()

    each_peer(seq, deliver)
    slots[1, me] = first[owner[me]]

    loads["og"].wait()
    loads["w"].wait()
    for copy in og_copies:
        copy.wait_recv()
    block = 256

    def project(n, _):
        r = pl.multiple_of(n * block, block)
        total = dot(ogs[0], w[pl.ds(r, block), 0:width], 1, 1)
        for h in range(1, heads):
            total += dot(ogs[h], w[pl.ds(r, block), h * width : (h + 1) * width], 1, 1)
        total = total.astype(BF16)
        for t in range(tiles):
            for h in range(block // 128):
                at = pl.multiple_of((n * (block // 128) + h) * TILE, TILE)
                gp[t, pl.ds(at, TILE)] = total[t * TILE : (t + 1) * TILE, h * 128 : (h + 1) * 128]
        return 0

    lax.fori_loop(0, feat // block, project, 0)
    loads["rv"].wait()

    def own_dots(t, span):
        v = dot(rv[0:span], gp[t], 1, 1)
        vr[t, 0:span] = v
        rstat[t, 2:3] = jnp.sum(v * er[t, 0:span], axis=0, keepdims=True)

    each_tile(own_dots)
    dks[0] = jnp.zeros(dks.shape[1:], F32)
    dvs[0] = jnp.zeros(dvs.shape[1:], F32)
    for n in range(groups):
        g = lax.rem(group + 2 * groups - 1 - n, groups)
        arrived = per if n < groups - 1 else per - 1
        wait_bytes(slots.at[1, pl.ds(0, arrived)], sem_in2.at[g])
        part = pl.ds(g * per, per)
        pltpu.make_async_remote_copy(
            slots.at[1, part], slots.at[0, part], sem_near.at[0], sem_near.at[1],
            device_id=at_seq(up), device_id_type=MESH,
        ).start()
        pltpu.make_async_remote_copy(
            slots.at[1, part], slots.at[2, part], sem_near.at[2], sem_near.at[3],
            device_id=at_seq(down), device_id_type=MESH,
        ).start()
    wait_bytes(slots.at[0], sem_near.at[1])
    wait_bytes(slots.at[2], sem_near.at[3])

    def load_unit(n):
        t = unit[0, n]
        s = unit[2, n]
        member = lanes[t, 1:2].astype(jnp.int32) == unit[1, n]
        stat = rstat[t]
        return dict(
            n=n, s=s, q=qp[t], g=gp[t], member=member, same=unit[3, n] == 1,
            top=stat[0:1], total=stat[1:2], dots=stat[2:3],
        )

    def scores(u):
        k = slots[u["s"], 0:half].reshape(plen, 128)
        v = slots[u["s"], half:seq].reshape(plen, 128)
        u["sp"] = dot(k, u["q"], 1, 1)
        u["vp"] = dot(v, u["g"], 1, 1)

    def softmax(u):
        top = jnp.maximum(c * jnp.max(u["sp"], axis=0, keepdims=True), u["top"])
        e = jnp.exp2(u["sp"] * c - top)
        own = jnp.exp2(u["top"] - top)
        total = jnp.sum(e, axis=0, keepdims=True) + u["total"] * own
        inv = jnp.where(u["member"], 1.0 / total, 0.0)
        wp = e * inv
        dots = jnp.sum(wp * u["vp"], axis=0, keepdims=True) + u["dots"] * (own * inv)
        n = u["n"]
        u["wl"] = wp.astype(BF16)
        u["gl"] = (wp * (u["vp"] - dots)).astype(BF16)
        weights[n] = u["wl"]
        sgrads[n] = u["gl"]
        ustat[n, 0:1] = own * inv
        ustat[n, 1:2] = dots

    def key_sums(u):
        n = u["n"]
        dvs[n + 1] = jnp.where(u["same"], dvs[n], 0.0) + dot(u["wl"], u["g"], 1, 0)
        dks[n + 1] = jnp.where(u["same"], dks[n], 0.0) + dot(u["gl"], u["q"], 1, 0)

    def pair(i, _):
        two = [load_unit(2 * i), load_unit(2 * i + 1)]
        for stage in (scores, softmax, key_sums):
            for u in two:
                stage(u)
        return 0

    lax.fori_loop(0, units // 2, pair, 0)

    def place(i):
        dslots[i, 0:half] = jnp.where(slot_used[i], dks[slot_last[i]] * scale, 0.0).astype(BF16).reshape(
            half, -1, 128
        )
        dslots[i, half:seq] = jnp.where(slot_used[i], dvs[slot_last[i]], 0.0).astype(BF16).reshape(half, -1, 128)

    place(0)
    place(2)
    for n in range(groups):
        part = pl.ds(lax.rem(group + n, groups) * per, per)
        at = lax.rem(group + n, groups)
        pltpu.make_async_remote_copy(
            dslots.at[2, part], near.at[0, part], sem_back_s.at[0], sem_back.at[0, at],
            device_id=at_seq(up), device_id_type=MESH,
        ).start()
        pltpu.make_async_remote_copy(
            dslots.at[0, part], near.at[1, part], sem_back_s.at[1], sem_back.at[1, at],
            device_id=at_seq(down), device_id_type=MESH,
        ).start()
    place(1)

    spot = lax.broadcasted_iota(jnp.int32, inverse_row.shape, 1)
    found = jnp.zeros(inverse_row.shape, jnp.int32)
    for p in range(seq):
        found = jnp.where(spot == owner[p], p, found)
    inverse_row[...] = found
    to_scalars = pltpu.make_async_copy(inverse_row, inverse, local.at[len(loads)])
    to_scalars.start()
    for i in range(3):
        vt[i] = slots[i, half:seq].reshape(plen, 128).T

    def unit_rows(n, _):
        ot[n] = dot(vt[unit[2, n]], weights[n], 1, 0)
        return 0

    lax.fori_loop(0, units, unit_rows, 0)

    at_start, at_end = me == 0, me == seq - 1
    for n in range(groups):
        g = lax.rem(group + n, groups)
        part = pl.ds(g * per, per)
        wait_bytes(near.at[0, part], sem_back.at[0, g])
        wait_bytes(near.at[1, part], sem_back.at[1, g])
        below = jnp.where(at_start, 0.0, near[0, part].astype(F32))
        above = jnp.where(at_end, 0.0, near[1, part].astype(F32))
        summed[part] = (dslots[1, part].astype(F32) + below + above).astype(BF16)
        for i in range(per):
            j = g * per + i

            @pl.when(j != me)
            def _():
                pltpu.make_async_remote_copy(
                    summed.at[j], second.at[me], sem_out1.at[0], sem_out1.at[1],
                    device_id=at_seq(j), device_id_type=MESH,
                ).start()

    second[me] = summed[me]

    def of_tile(t, ref, row_slice=slice(None)):
        begin, many = tile_first[t], tile_count[t]
        total = ref[begin, row_slice]
        for j in range(1, 3):
            total += jnp.where(many > j, ref[jnp.minimum(begin + j, units - 1), row_slice], 0.0)
        return total

    def unit_facts(t):
        begin, many = tile_first[t], tile_count[t]
        slot = lanes[t, 1:2].astype(jnp.int32)
        factor, dots = 0.0, 0.0
        for j in range(3):
            n = jnp.minimum(begin + j, units - 1)
            member = (slot == unit[1, n]) & (many > j)
            factor += jnp.where(member, ustat[n, 0:1], 0.0)
            dots += jnp.where(member, ustat[n, 1:2], 0.0)
        return factor, dots

    rvt = rv[...].T

    def attend(t, span):
        factor, _ = unit_facts(t)
        o = of_tile(t, ot) + dot(rvt[:, 0:span], (er[t, 0:span] * factor).astype(BF16), 1, 0)
        o = o.T.astype(BF16)
        for h in range(per_group):
            att[pl.ds(pl.multiple_of(t * TILE, TILE), TILE), h * 128 : (h + 1) * 128] = o[h * TILE : (h + 1) * TILE]

    each_tile(attend)

    def share(i):
        peer = lax.rem(mine + i, heads)
        return dot(att[...], w[:, pl.ds(pl.multiple_of(peer * width, width), width)], 1, 0)

    part_copies = []
    for i in range(1, heads):
        parts[i] = share(i).astype(BF16)
        copy = pltpu.make_async_remote_copy(
            parts.at[i], got.at[i], sem_parts.at[0, i], sem_parts.at[1, i],
            device_id=at_head(lax.rem(mine + i, heads)), device_id_type=MESH,
        )
        copy.start()
        part_copies.append(copy)

    to_scalars.wait()
    wait_bytes(second.at[pl.ds(0, seq - 1)], sem_out1.at[1])
    wait_bytes(order.at[pl.ds(0, seq - 1)], sem_in2s)

    def give_back(o):
        order[o] = second[inverse[0, o]]
        pltpu.make_async_remote_copy(
            order.at[o], back.at[me], sem_out2.at[0], sem_out2.at[1], device_id=at_seq(o), device_id_type=MESH
        ).start()

    each_peer(seq, give_back)
    back[me] = second[inverse[0, me]]

    own_part[...] = share(0)
    for i in range(3):
        kt[i] = slots[i, 0:half].reshape(plen, 128).T

    def unit_query(n, _):
        dqt[n] = dot(kt[unit[2, n]], sgrads[n], 1, 0)
        return 0

    lax.fori_loop(0, units, unit_query, 0)
    rkt = rk[...].T
    drk_acc[...] = jnp.zeros_like(drk_acc)
    drv_acc[...] = jnp.zeros_like(drv_acc)

    def own_grads(t, span):
        factor, dots = unit_facts(t)
        wr = er[t, 0:span] * factor
        gr = (wr * (vr[t, 0:span] - dots)).astype(BF16)
        drv_acc[0:span] += dot(wr.astype(BF16), gp[t], 1, 0)
        drk_acc[0:span] += dot(gr, qp[t], 1, 0)
        d = ((of_tile(t, dqt) + dot(rkt[:, 0:span], gr, 1, 0)) * scale).T.astype(BF16)
        for h in range(per_group):
            dq[pl.ds(pl.multiple_of(t * TILE, TILE), TILE), h * 128 : (h + 1) * 128] = d[h * TILE : (h + 1) * TILE]

    each_tile(own_grads)
    drk[...] = (drk_acc[...] * scale).astype(BF16)
    drv[...] = drv_acc[...].astype(BF16)
    for copy in part_copies:
        copy.wait_recv()
    total = own_part[...]
    for i in range(1, heads):
        total += got[i].astype(F32)
    out[...] = total.astype(BF16)

    for copy in og_copies + part_copies:
        copy.wait_send()
    wait_bytes(first.at[pl.ds(0, seq - 1)], sem_in1.at[0])
    wait_bytes(slots.at[1], sem_near.at[0])
    wait_bytes(slots.at[1], sem_near.at[2])
    wait_bytes(near.at[0], sem_back_s.at[0])
    wait_bytes(near.at[1], sem_back_s.at[1])
    wait_bytes(second.at[pl.ds(0, seq - 1)], sem_out1.at[0])
    wait_bytes(order.at[pl.ds(0, seq - 1)], sem_out2.at[0])
    wait_bytes(back.at[pl.ds(0, seq - 1)], sem_out2.at[1])
    grad[...] = back[...].astype(F32)


def store_kernel(*refs):
    many = (len(refs) - 1) // 2
    copies = [pltpu.make_async_copy(refs[i], refs[many + i], refs[-1].at[i]) for i in range(many)]
    for copy in copies:
        copy.start()
    for copy in copies:
        copy.wait()


def per_device(
    token_response, prompt_owner, queries, resp_keys, resp_values, prompt_kv, out_weight, out_grad
):
    seq, heads = lax.axis_size("seq"), lax.axis_size("head")
    vm = pl.BlockSpec(memory_space=pltpu.VMEM)
    hbm = pl.BlockSpec(memory_space=pltpu.HBM)
    pieces = prompt_kv.reshape(seq, -1, 128)
    plen = prompt_kv.shape[2]
    rows, feat = queries.shape
    width = out_grad.shape[1]
    tiles = rows // TILE
    units = tiles + 2
    lanes = TILE * feat // 128
    wide = -(-seq // 128) * 128
    groups = max(2, seq // 8)
    dma = pltpu.SemaphoreType.DMA
    shapes = (
        jax.ShapeDtypeStruct((rows, width), BF16),
        jax.ShapeDtypeStruct(queries.shape, BF16),
        jax.ShapeDtypeStruct(resp_keys.shape, BF16),
        jax.ShapeDtypeStruct(resp_values.shape, BF16),
        jax.ShapeDtypeStruct(pieces.shape, F32),
    )
    operands = (
        token_response, token_response.reshape(1, rows), prompt_owner, queries, resp_keys, resp_values,
        pieces, out_grad, out_weight,
    )
    results = pl.pallas_call(
        functools.partial(layer_kernel, seq, heads),
        out_shape=shapes,
        in_specs=[hbm] * len(operands),
        out_specs=(vm,) * len(shapes),
        scratch_shapes=[
            pltpu.SMEM((rows,), jnp.int32),
            pltpu.SMEM((seq,), jnp.int32),
            pltpu.SMEM((1, wide), jnp.int32),
            pltpu.SMEM((4, units), jnp.int32),
            pltpu.SMEM((tiles,), jnp.int32),
            pltpu.SMEM((tiles,), jnp.int32),
            pltpu.VMEM((1, rows), jnp.int32),
            pltpu.VMEM(queries.shape, BF16),
            pltpu.VMEM(resp_keys.shape, BF16),
            pltpu.VMEM(resp_values.shape, BF16),
            pltpu.VMEM(out_weight.shape, BF16),
            pltpu.VMEM((heads, rows, width), BF16),
            pltpu.VMEM(pieces.shape, BF16),
            pltpu.VMEM(pieces.shape, BF16),
            pltpu.VMEM((3,) + pieces.shape, BF16),
            pltpu.VMEM((tiles, 16, lanes), F32),
            pltpu.VMEM((tiles, lanes, 128), BF16),
            pltpu.VMEM((tiles, lanes, 128), BF16),
            pltpu.VMEM((tiles, rows, lanes), F32),
            pltpu.VMEM((tiles, rows, lanes), F32),
            pltpu.VMEM((tiles, 8, lanes), F32),
            pltpu.VMEM((units, plen, lanes), BF16),
            pltpu.VMEM((units, plen, lanes), BF16),
            pltpu.VMEM((units, 8, lanes), F32),
            pltpu.VMEM((units + 1, plen, 128), F32),
            pltpu.VMEM((units + 1, plen, 128), F32),
            pltpu.VMEM((3,) + pieces.shape, BF16),
            pltpu.VMEM((2,) + pieces.shape, BF16),
            pltpu.VMEM(pieces.shape, BF16),
            pltpu.VMEM(pieces.shape, BF16),
            pltpu.VMEM(pieces.shape, BF16),
            pltpu.VMEM((1, wide), jnp.int32),
            pltpu.VMEM((3, 128, plen), BF16),
            pltpu.VMEM((3, 128, plen), BF16),
            pltpu.VMEM((units, 128, lanes), F32),
            pltpu.VMEM((units, 128, lanes), F32),
            pltpu.VMEM(queries.shape, BF16),
            pltpu.VMEM(resp_keys.shape, F32),
            pltpu.VMEM(resp_keys.shape, F32),
            pltpu.VMEM((heads, rows, width), BF16),
            pltpu.VMEM((heads, rows, width), BF16),
            pltpu.VMEM((rows, width), F32),
            dma((2,)),
            dma,
            dma((groups,)),
            dma((4,)),
            dma((2, heads)),
            dma((10,)),
            dma((2,)),
            dma((2, groups)),
            dma((2,)),
            dma((2,)),
            dma((2, heads)),
        ],
        compiler_params=pltpu.CompilerParams(
            collective_id=0, has_side_effects=True, vmem_limit_bytes=VMEM_LIMIT
        ),
        name="layer",
    )(*(in_hbm(x) for x in operands))
    layer_out, query_grad, key_grad, value_grad, prompt_grad = pl.pallas_call(
        store_kernel,
        out_shape=shapes,
        in_specs=[vm] * len(shapes),
        out_specs=(hbm,) * len(shapes),
        scratch_shapes=[dma((len(shapes),))],
        name="store",
    )(*results)
    return (layer_out, query_grad, key_grad, value_grad, prompt_grad.reshape(prompt_kv.shape))


def solution(mesh):
    placed = (
        P("seq"),
        P(),
        P("seq", "head"),
        P("seq", "head"),
        P("seq", "head"),
        P("seq", None, None, "head"),
        P("head", None),
        P("seq", "head"),
    )
    return jax.shard_map(
        per_device,
        mesh=mesh,
        in_specs=placed,
        out_specs=(
            P("seq", "head"),
            P("seq", "head"),
            P("seq", "head"),
            P("seq", "head"),
            P("seq", None, None, "head"),
        ),
        check_vma=False,
    )
```

```python
import functools

import jax
import jax.numpy as jnp
from jax import lax
from jax.experimental import pallas as pl
from jax.experimental.pallas import tpu as pltpu
from jax.sharding import PartitionSpec as P

GROUP = 16
TILE = 32
LOG2E = 1.4426950408889634
F32, BF16 = jnp.float32, jnp.bfloat16
MESH = pl.DeviceIdType.MESH
VMEM_LIMIT = 52 * 2**20


def dot(a, b, ca, cb):
    return lax.dot_general(a, b, (((ca,), (cb,)), ((), ())), preferred_element_type=F32)


def at_seq(j):
    return (j, lax.axis_index("head"))


def at_head(j):
    return (lax.axis_index("seq"), j)


def greet(seq, heads):
    me, mine = lax.axis_index("seq"), lax.axis_index("head")
    barrier = pltpu.get_barrier_semaphore()

    def tell(i, _):
        pl.semaphore_signal(barrier, inc=1, device_id=at_seq(lax.rem(me + i, seq)), device_id_type=MESH)
        return 0

    lax.fori_loop(1, seq, tell, 0)
    for i in range(1, heads):
        pl.semaphore_signal(barrier, inc=1, device_id=at_head(lax.rem(mine + i, heads)), device_id_type=MESH)


def all_in(seq, heads):
    pl.semaphore_wait(pltpu.get_barrier_semaphore(), seq - 1 + heads - 1)


def each_peer(seq, visit):
    me = lax.axis_index("seq")
    core, chip, chips = lax.rem(me, 2), me // 2, seq // 2
    visit(me + 1 - 2 * core)
    for c in range(2):

        def go(t, _):
            visit(2 * lax.rem(chip + t, chips) + c)
            return 0

        lax.fori_loop(1, chips, go, 0)


def in_hbm(x):
    return pltpu.with_memory_space_constraint(x, pltpu.HBM)


def wait_bytes(ref, sem):
    pltpu.make_async_copy(ref, ref, sem).wait()


def add_all(terms):
    return functools.reduce(lambda a, b: a + b, terms)


def count_if(condition):
    return jnp.where(condition, 1, 0)


def layer_kernel(
    seq, heads,
    tok_hbm, row_hbm, owner_hbm, q_hbm, rk_hbm, rv_hbm, kv, og, w_hbm,
    out, dq, drk, drv, grad,
    tok, owner, inverse, unit, tile_first, tile_count,
    row, q, rk, rv, w, ogs,
    first, order, slots, lanes, qp, gp, er, vr, rstat,
    weights, sgrads, ustat, dks, dvs,
    dslots, near, summed, second, back, inverse_row,
    kt, vt, ot, dqt, att, drk_acc, drv_acc, parts, got, own_part,
    sem_in1, sem_in2s, sem_in2, sem_near, sem_og, local, sem_back_s, sem_back, sem_out1, sem_out2, sem_parts,
):
    me, mine = lax.axis_index("seq"), lax.axis_index("head")
    groups = max(2, seq // 8)
    per = seq // groups
    group = me // per
    half = seq // 2
    rows, feat = q.shape
    plen = kt.shape[2]
    width = og.shape[1]
    tiles = rows // TILE
    per_group = feat // 128
    lanes_n = TILE * per_group
    units = tiles + 2
    scale = 128**-0.5
    c = scale * LOG2E
    up, down = lax.rem(me + 1, seq), lax.rem(me + seq - 1, seq)

    loads = {}
    for n, (name, src, dst) in enumerate(
        (
            ("tok", tok_hbm, tok),
            ("owner", owner_hbm, owner),
            ("piece", kv.at[me], first.at[me]),
            ("row", row_hbm, row),
            ("q", q_hbm, q),
            ("rk", rk_hbm, rk),
            ("rv", rv_hbm, rv),
            ("og", og, ogs.at[mine]),
            ("w", w_hbm, w),
        )
    ):
        loads[name] = pltpu.make_async_copy(src, dst, local.at[n])
        loads[name].start()
    greet(seq, heads)
    all_in(seq, heads)

    def spread(j):
        pltpu.make_async_remote_copy(
            kv.at[j], first.at[me], sem_in1.at[0], sem_in1.at[1], device_id=at_seq(j), device_id_type=MESH
        ).start()

    each_peer(seq, spread)
    og_copies = []
    for i in range(1, heads):
        copy = pltpu.make_async_remote_copy(
            og, ogs.at[mine], sem_og.at[0, i], sem_og.at[1, heads - i],
            device_id=at_head(lax.rem(mine + i, heads)), device_id_type=MESH,
        )
        copy.start()
        og_copies.append(copy)

    loads["tok"].wait()
    low = [lax.div(tok[t * TILE], GROUP) - (me - 1) for t in range(tiles)]
    high = [lax.div(tok[t * TILE + TILE - 1], GROUP) - (me - 1) for t in range(tiles)]
    offset = [jnp.int32(0)]
    for t in range(tiles):
        offset.append(offset[t] + high[t] - low[t] + 1)
        tile_first[t] = offset[t]
        tile_count[t] = high[t] - low[t] + 1
    slot_of_unit = []
    for n in range(units):
        t_n = add_all([count_if(offset[t] <= n) for t in range(1, tiles)])
        relative = low[0]
        for t in range(1, tiles):
            relative = jnp.where(offset[t] <= n, low[t] - offset[t], relative)
        p_n = relative + n
        s_n = jnp.clip(p_n, 0, 2)
        unit[0, n] = t_n
        unit[1, n] = p_n
        unit[2, n] = s_n
        unit[3, n] = count_if(s_n == slot_of_unit[-1]) if n else jnp.int32(0)
        slot_of_unit.append(s_n)
    slot_last = [add_all([count_if(s <= i) for s in slot_of_unit]) for i in range(3)]
    slot_used = [add_all([count_if(s == i) for s in slot_of_unit]) > 0 for i in range(3)]

    loads["row"].wait()
    row_f = row[...].astype(F32)
    column = jnp.broadcast_to(row_f, (128, rows)).T
    earlier = jnp.concatenate([column] * (-(-rows // 128)), axis=1)[:, :rows] < row_f
    start = jnp.sum(jnp.where(earlier, 1.0, 0.0), axis=0, keepdims=True)
    slot_row = (lax.div(row[...], GROUP) - (me - 1)).astype(F32)
    pick = lax.broadcasted_iota(jnp.int32, (16, rows), 0)
    facts = jnp.where(pick == 0, start, jnp.where(pick == 1, slot_row, 0.0)).astype(BF16)
    source = lax.broadcasted_iota(jnp.int32, (rows, lanes_n), 0)
    lane = lax.broadcasted_iota(jnp.int32, (rows, lanes_n), 1) & (TILE - 1)
    for t in range(tiles):
        chosen = jnp.where(source == lane + t * TILE, 1.0, 0.0).astype(BF16)
        lanes[t] = dot(facts, chosen, 1, 0)
    loads["q"].wait()
    for t in range(tiles):
        for h in range(per_group):
            qp[t, h * TILE : (h + 1) * TILE] = q[t * TILE : (t + 1) * TILE, h * 128 : (h + 1) * 128]

    spans = []
    for t in range(tiles):
        span = min(rows, -(-((t + 1) * TILE) // 128) * 128)
        if spans and spans[-1][2] == span:
            spans[-1][1] = t + 1
        else:
            spans.append([t, t + 1, span])

    def each_tile(step):
        for begin, end, span in spans:
            lax.fori_loop(begin, end, lambda t, _: (step(t, span), 0)[1], 0)

    def own_scores(t, span):
        key_id = lax.broadcasted_iota(jnp.int32, (span, lanes_n), 0)
        token = t * TILE + (lax.broadcasted_iota(jnp.int32, (1, lanes_n), 1) & (TILE - 1))
        visible = (key_id >= lanes[t, 0:1].astype(jnp.int32)) & (key_id <= token)
        s = jnp.where(visible, dot(rk[0:span], qp[t], 1, 1) * c, -1e30)
        top = jnp.max(s, axis=0, keepdims=True)
        e = jnp.exp2(s - top)
        er[t, 0:span] = e
        rstat[t, 0:1] = top
        rstat[t, 1:2] = jnp.sum(e, axis=0, keepdims=True)

    loads["rk"].wait()
    each_tile(own_scores)

    loads["owner"].wait()
    loads["piece"].wait()
    wait_bytes(first.at[pl.ds(0, seq - 1)], sem_in1.at[1])

    def deliver(p):
        order[p] = first[owner[p]]
        pltpu.make_async_remote_copy(
            order.at[p], slots.at[1, me], sem_in2s, sem_in2.at[group], device_id=at_seq(p), device_id_type=MESH
        ).start()

    each_peer(seq, deliver)
    slots[1, me] = first[owner[me]]

    loads["og"].wait()
    loads["w"].wait()
    for copy in og_copies:
        copy.wait_recv()
    block = 256

    def project(n, _):
        r = pl.multiple_of(n * block, block)
        total = dot(ogs[0], w[pl.ds(r, block), 0:width], 1, 1)
        for h in range(1, heads):
            total += dot(ogs[h], w[pl.ds(r, block), h * width : (h + 1) * width], 1, 1)
        total = total.astype(BF16)
        for t in range(tiles):
            for h in range(block // 128):
                at = pl.multiple_of((n * (block // 128) + h) * TILE, TILE)
                gp[t, pl.ds(at, TILE)] = total[t * TILE : (t + 1) * TILE, h * 128 : (h + 1) * 128]
        return 0

    lax.fori_loop(0, feat // block, project, 0)
    loads["rv"].wait()

    def own_dots(t, span):
        v = dot(rv[0:span], gp[t], 1, 1)
        vr[t, 0:span] = v
        rstat[t, 2:3] = jnp.sum(v * er[t, 0:span], axis=0, keepdims=True)

    each_tile(own_dots)
    dks[0] = jnp.zeros(dks.shape[1:], F32)
    dvs[0] = jnp.zeros(dvs.shape[1:], F32)
    for n in range(groups):
        g = lax.rem(group + 2 * groups - 1 - n, groups)
        arrived = per if n < groups - 1 else per - 1
        wait_bytes(slots.at[1, pl.ds(0, arrived)], sem_in2.at[g])
        part = pl.ds(g * per, per)
        pltpu.make_async_remote_copy(
            slots.at[1, part], slots.at[0, part], sem_near.at[0], sem_near.at[1],
            device_id=at_seq(up), device_id_type=MESH,
        ).start()
        pltpu.make_async_remote_copy(
            slots.at[1, part], slots.at[2, part], sem_near.at[2], sem_near.at[3],
            device_id=at_seq(down), device_id_type=MESH,
        ).start()
    wait_bytes(slots.at[0], sem_near.at[1])
    wait_bytes(slots.at[2], sem_near.at[3])

    def load_unit(n):
        t = unit[0, n]
        s = unit[2, n]
        member = lanes[t, 1:2].astype(jnp.int32) == unit[1, n]
        stat = rstat[t]
        return dict(
            n=n, s=s, q=qp[t], g=gp[t], member=member, same=unit[3, n] == 1,
            top=stat[0:1], total=stat[1:2], dots=stat[2:3],
        )

    def scores(u):
        k = slots[u["s"], 0:half].reshape(plen, 128)
        v = slots[u["s"], half:seq].reshape(plen, 128)
        u["sp"] = dot(k, u["q"], 1, 1)
        u["vp"] = dot(v, u["g"], 1, 1)

    def softmax(u):
        top = jnp.maximum(c * jnp.max(u["sp"], axis=0, keepdims=True), u["top"])
        e = jnp.exp2(u["sp"] * c - top)
        own = jnp.exp2(u["top"] - top)
        total = jnp.sum(e, axis=0, keepdims=True) + u["total"] * own
        inv = jnp.where(u["member"], 1.0 / total, 0.0)
        wp = e * inv
        dots = jnp.sum(wp * u["vp"], axis=0, keepdims=True) + u["dots"] * (own * inv)
        n = u["n"]
        u["wl"] = wp.astype(BF16)
        u["gl"] = (wp * (u["vp"] - dots)).astype(BF16)
        weights[n] = u["wl"]
        sgrads[n] = u["gl"]
        ustat[n, 0:1] = own * inv
        ustat[n, 1:2] = dots

    def key_sums(u):
        n = u["n"]
        dvs[n + 1] = jnp.where(u["same"], dvs[n], 0.0) + dot(u["wl"], u["g"], 1, 0)
        dks[n + 1] = jnp.where(u["same"], dks[n], 0.0) + dot(u["gl"], u["q"], 1, 0)

    def pair(i, _):
        two = [load_unit(2 * i), load_unit(2 * i + 1)]
        for stage in (scores, softmax, key_sums):
            for u in two:
                stage(u)
        return 0

    lax.fori_loop(0, units // 2, pair, 0)

    def place(i):
        dslots[i, 0:half] = jnp.where(slot_used[i], dks[slot_last[i]] * scale, 0.0).astype(BF16).reshape(
            half, -1, 128
        )
        dslots[i, half:seq] = jnp.where(slot_used[i], dvs[slot_last[i]], 0.0).astype(BF16).reshape(half, -1, 128)

    place(0)
    place(2)
    for n in range(groups):
        part = pl.ds(lax.rem(group + n, groups) * per, per)
        at = lax.rem(group + n, groups)
        pltpu.make_async_remote_copy(
            dslots.at[2, part], near.at[0, part], sem_back_s.at[0], sem_back.at[0, at],
            device_id=at_seq(up), device_id_type=MESH,
        ).start()
        pltpu.make_async_remote_copy(
            dslots.at[0, part], near.at[1, part], sem_back_s.at[1], sem_back.at[1, at],
            device_id=at_seq(down), device_id_type=MESH,
        ).start()
    place(1)

    spot = lax.broadcasted_iota(jnp.int32, inverse_row.shape, 1)
    found = jnp.zeros(inverse_row.shape, jnp.int32)
    for p in range(seq):
        found = jnp.where(spot == owner[p], p, found)
    inverse_row[...] = found
    to_scalars = pltpu.make_async_copy(inverse_row, inverse, local.at[len(loads)])
    to_scalars.start()
    for i in range(3):
        vt[i] = slots[i, half:seq].reshape(plen, 128).T

    def unit_rows(n, _):
        ot[n] = dot(vt[unit[2, n]], weights[n], 1, 0)
        return 0

    lax.fori_loop(0, units, unit_rows, 0)

    at_start, at_end = me == 0, me == seq - 1
    for n in range(groups):
        g = lax.rem(group + n, groups)
        part = pl.ds(g * per, per)
        wait_bytes(near.at[0, part], sem_back.at[0, g])
        wait_bytes(near.at[1, part], sem_back.at[1, g])
        below = jnp.where(at_start, 0.0, near[0, part].astype(F32))
        above = jnp.where(at_end, 0.0, near[1, part].astype(F32))
        summed[part] = (dslots[1, part].astype(F32) + below + above).astype(BF16)
        for i in range(per):
            j = g * per + i

            @pl.when(j != me)
            def _():
                pltpu.make_async_remote_copy(
                    summed.at[j], second.at[me], sem_out1.at[0], sem_out1.at[1],
                    device_id=at_seq(j), device_id_type=MESH,
                ).start()

    second[me] = summed[me]

    def of_tile(t, ref, row_slice=slice(None)):
        begin, many = tile_first[t], tile_count[t]
        total = ref[begin, row_slice]
        for j in range(1, 3):
            total += jnp.where(many > j, ref[jnp.minimum(begin + j, units - 1), row_slice], 0.0)
        return total

    def unit_facts(t):
        begin, many = tile_first[t], tile_count[t]
        slot = lanes[t, 1:2].astype(jnp.int32)
        factor, dots = 0.0, 0.0
        for j in range(3):
            n = jnp.minimum(begin + j, units - 1)
            member = (slot == unit[1, n]) & (many > j)
            factor += jnp.where(member, ustat[n, 0:1], 0.0)
            dots += jnp.where(member, ustat[n, 1:2], 0.0)
        return factor, dots

    rvt = rv[...].T

    def attend(t, span):
        factor, _ = unit_facts(t)
        o = of_tile(t, ot) + dot(rvt[:, 0:span], (er[t, 0:span] * factor).astype(BF16), 1, 0)
        o = o.T.astype(BF16)
        for h in range(per_group):
            att[pl.ds(pl.multiple_of(t * TILE, TILE), TILE), h * 128 : (h + 1) * 128] = o[h * TILE : (h + 1) * TILE]

    each_tile(attend)

    def share(i):
        peer = lax.rem(mine + i, heads)
        return dot(att[...], w[:, pl.ds(pl.multiple_of(peer * width, width), width)], 1, 0)

    part_copies = []
    for i in range(1, heads):
        parts[i] = share(i).astype(BF16)
        copy = pltpu.make_async_remote_copy(
            parts.at[i], got.at[i], sem_parts.at[0, i], sem_parts.at[1, i],
            device_id=at_head(lax.rem(mine + i, heads)), device_id_type=MESH,
        )
        copy.start()
        part_copies.append(copy)

    to_scalars.wait()
    wait_bytes(second.at[pl.ds(0, seq - 1)], sem_out1.at[1])
    wait_bytes(order.at[pl.ds(0, seq - 1)], sem_in2s)

    def give_back(o):
        order[o] = second[inverse[0, o]]
        pltpu.make_async_remote_copy(
            order.at[o], back.at[me], sem_out2.at[0], sem_out2.at[1], device_id=at_seq(o), device_id_type=MESH
        ).start()

    each_peer(seq, give_back)
    back[me] = second[inverse[0, me]]

    own_part[...] = share(0)
    for i in range(3):
        kt[i] = slots[i, 0:half].reshape(plen, 128).T

    def unit_query(n, _):
        dqt[n] = dot(kt[unit[2, n]], sgrads[n], 1, 0)
        return 0

    lax.fori_loop(0, units, unit_query, 0)
    rkt = rk[...].T
    drk_acc[...] = jnp.zeros_like(drk_acc)
    drv_acc[...] = jnp.zeros_like(drv_acc)

    def own_grads(t, span):
        factor, dots = unit_facts(t)
        wr = er[t, 0:span] * factor
        gr = (wr * (vr[t, 0:span] - dots)).astype(BF16)
        drv_acc[0:span] += dot(wr.astype(BF16), gp[t], 1, 0)
        drk_acc[0:span] += dot(gr, qp[t], 1, 0)
        d = ((of_tile(t, dqt) + dot(rkt[:, 0:span], gr, 1, 0)) * scale).T.astype(BF16)
        for h in range(per_group):
            dq[pl.ds(pl.multiple_of(t * TILE, TILE), TILE), h * 128 : (h + 1) * 128] = d[h * TILE : (h + 1) * TILE]

    each_tile(own_grads)
    drk[...] = (drk_acc[...] * scale).astype(BF16)
    drv[...] = drv_acc[...].astype(BF16)
    for copy in part_copies:
        copy.wait_recv()
    total = own_part[...]
    for i in range(1, heads):
        total += got[i].astype(F32)
    out[...] = total.astype(BF16)

    for copy in og_copies + part_copies:
        copy.wait_send()
    wait_bytes(first.at[pl.ds(0, seq - 1)], sem_in1.at[0])
    wait_bytes(slots.at[1], sem_near.at[0])
    wait_bytes(slots.at[1], sem_near.at[2])
    wait_bytes(near.at[0], sem_back_s.at[0])
    wait_bytes(near.at[1], sem_back_s.at[1])
    wait_bytes(second.at[pl.ds(0, seq - 1)], sem_out1.at[0])
    wait_bytes(order.at[pl.ds(0, seq - 1)], sem_out2.at[0])
    wait_bytes(back.at[pl.ds(0, seq - 1)], sem_out2.at[1])
    grad[...] = back[...].astype(F32)


def store_kernel(*refs):
    many = (len(refs) - 1) // 2
    copies = [pltpu.make_async_copy(refs[i], refs[many + i], refs[-1].at[i]) for i in range(many)]
    for copy in copies:
        copy.start()
    for copy in copies:
        copy.wait()


def per_device(
    token_response, prompt_owner, queries, resp_keys, resp_values, prompt_kv, out_weight, out_grad
):
    seq, heads = lax.axis_size("seq"), lax.axis_size("head")
    vm = pl.BlockSpec(memory_space=pltpu.VMEM)
    hbm = pl.BlockSpec(memory_space=pltpu.HBM)
    pieces = prompt_kv.reshape(seq, -1, 128)
    plen = prompt_kv.shape[2]
    rows, feat = queries.shape
    width = out_grad.shape[1]
    tiles = rows // TILE
    units = tiles + 2
    lanes = TILE * feat // 128
    wide = -(-seq // 128) * 128
    groups = max(2, seq // 8)
    dma = pltpu.SemaphoreType.DMA
    shapes = (
        jax.ShapeDtypeStruct((rows, width), BF16),
        jax.ShapeDtypeStruct(queries.shape, BF16),
        jax.ShapeDtypeStruct(resp_keys.shape, BF16),
        jax.ShapeDtypeStruct(resp_values.shape, BF16),
        jax.ShapeDtypeStruct(pieces.shape, F32),
    )
    operands = (
        token_response, token_response.reshape(1, rows), prompt_owner, queries, resp_keys, resp_values,
        pieces, out_grad, out_weight,
    )
    results = pl.pallas_call(
        functools.partial(layer_kernel, seq, heads),
        out_shape=shapes,
        in_specs=[hbm] * len(operands),
        out_specs=(vm,) * len(shapes),
        scratch_shapes=[
            pltpu.SMEM((rows,), jnp.int32),
            pltpu.SMEM((seq,), jnp.int32),
            pltpu.SMEM((1, wide), jnp.int32),
            pltpu.SMEM((4, units), jnp.int32),
            pltpu.SMEM((tiles,), jnp.int32),
            pltpu.SMEM((tiles,), jnp.int32),
            pltpu.VMEM((1, rows), jnp.int32),
            pltpu.VMEM(queries.shape, BF16),
            pltpu.VMEM(resp_keys.shape, BF16),
            pltpu.VMEM(resp_values.shape, BF16),
            pltpu.VMEM(out_weight.shape, BF16),
            pltpu.VMEM((heads, rows, width), BF16),
            pltpu.VMEM(pieces.shape, BF16),
            pltpu.VMEM(pieces.shape, BF16),
            pltpu.VMEM((3,) + pieces.shape, BF16),
            pltpu.VMEM((tiles, 16, lanes), F32),
            pltpu.VMEM((tiles, lanes, 128), BF16),
            pltpu.VMEM((tiles, lanes, 128), BF16),
            pltpu.VMEM((tiles, rows, lanes), F32),
            pltpu.VMEM((tiles, rows, lanes), F32),
            pltpu.VMEM((tiles, 8, lanes), F32),
            pltpu.VMEM((units, plen, lanes), BF16),
            pltpu.VMEM((units, plen, lanes), BF16),
            pltpu.VMEM((units, 8, lanes), F32),
            pltpu.VMEM((units + 1, plen, 128), F32),
            pltpu.VMEM((units + 1, plen, 128), F32),
            pltpu.VMEM((3,) + pieces.shape, BF16),
            pltpu.VMEM((2,) + pieces.shape, BF16),
            pltpu.VMEM(pieces.shape, BF16),
            pltpu.VMEM(pieces.shape, BF16),
            pltpu.VMEM(pieces.shape, BF16),
            pltpu.VMEM((1, wide), jnp.int32),
            pltpu.VMEM((3, 128, plen), BF16),
            pltpu.VMEM((3, 128, plen), BF16),
            pltpu.VMEM((units, 128, lanes), F32),
            pltpu.VMEM((units, 128, lanes), F32),
            pltpu.VMEM(queries.shape, BF16),
            pltpu.VMEM(resp_keys.shape, F32),
            pltpu.VMEM(resp_keys.shape, F32),
            pltpu.VMEM((heads, rows, width), BF16),
            pltpu.VMEM((heads, rows, width), BF16),
            pltpu.VMEM((rows, width), F32),
            dma((2,)),
            dma,
            dma((groups,)),
            dma((4,)),
            dma((2, heads)),
            dma((10,)),
            dma((2,)),
            dma((2, groups)),
            dma((2,)),
            dma((2,)),
            dma((2, heads)),
        ],
        compiler_params=pltpu.CompilerParams(
            collective_id=0, has_side_effects=True, vmem_limit_bytes=VMEM_LIMIT
        ),
        name="layer",
    )(*(in_hbm(x) for x in operands))
    layer_out, query_grad, key_grad, value_grad, prompt_grad = pl.pallas_call(
        store_kernel,
        out_shape=shapes,
        in_specs=[vm] * len(shapes),
        out_specs=(hbm,) * len(shapes),
        scratch_shapes=[dma((len(shapes),))],
        compiler_params=pltpu.CompilerParams(vmem_limit_bytes=4 * 2**20),
        name="store",
    )(*results)
    return (layer_out, query_grad, key_grad, value_grad, prompt_grad.reshape(prompt_kv.shape))


def solution(mesh):
    placed = (
        P("seq"),
        P(),
        P("seq", "head"),
        P("seq", "head"),
        P("seq", "head"),
        P("seq", None, None, "head"),
        P("head", None),
        P("seq", "head"),
    )
    return jax.shard_map(
        per_device,
        mesh=mesh,
        in_specs=placed,
        out_specs=(
            P("seq", "head"),
            P("seq", "head"),
            P("seq", "head"),
            P("seq", "head"),
            P("seq", None, None, "head"),
        ),
        check_vma=False,
    )
```

```python
import functools

import jax
import jax.numpy as jnp
from jax import lax
from jax.experimental import pallas as pl
from jax.experimental.pallas import tpu as pltpu
from jax.sharding import PartitionSpec as P

GROUP = 16
TILE = 32
LOG2E = 1.4426950408889634
F32, BF16 = jnp.float32, jnp.bfloat16
MESH = pl.DeviceIdType.MESH
VMEM_LIMIT = 52 * 2**20


def dot(a, b, ca, cb):
    return lax.dot_general(a, b, (((ca,), (cb,)), ((), ())), preferred_element_type=F32)


def at_seq(j):
    return (j, lax.axis_index("head"))


def at_head(j):
    return (lax.axis_index("seq"), j)


def greet(seq, heads):
    me, mine = lax.axis_index("seq"), lax.axis_index("head")
    barrier = pltpu.get_barrier_semaphore()

    def tell(i, _):
        pl.semaphore_signal(barrier, inc=1, device_id=at_seq(lax.rem(me + i, seq)), device_id_type=MESH)
        return 0

    lax.fori_loop(1, seq, tell, 0)
    for i in range(1, heads):
        pl.semaphore_signal(barrier, inc=1, device_id=at_head(lax.rem(mine + i, heads)), device_id_type=MESH)


def all_in(seq, heads):
    pl.semaphore_wait(pltpu.get_barrier_semaphore(), seq - 1 + heads - 1)


def each_peer(seq, visit):
    me = lax.axis_index("seq")
    core, chip, chips = lax.rem(me, 2), me // 2, seq // 2
    visit(me + 1 - 2 * core)
    for c in range(2):

        def go(t, _):
            visit(2 * lax.rem(chip + t, chips) + c)
            return 0

        lax.fori_loop(1, chips, go, 0)


def place_of(j, seq):
    return lax.rem(j, 2) * (seq // 2) + j // 2


def in_hbm(x):
    return pltpu.with_memory_space_constraint(x, pltpu.HBM)


def wait_bytes(ref, sem):
    pltpu.make_async_copy(ref, ref, sem).wait()


def add_all(terms):
    return functools.reduce(lambda a, b: a + b, terms)


def count_if(condition):
    return jnp.where(condition, 1, 0)


def layer_kernel(
    seq, heads,
    tok_hbm, row_hbm, owner_hbm, q_hbm, rk_hbm, rv_hbm, kv, og, w_hbm,
    out, dq, drk, drv, grad,
    tok, owner, inverse, unit, tile_first, tile_count,
    row, q, rk, rv, w, ogs,
    first, order, slots_k, slots_v, lanes, ag, qp, gp, er, vr, rstat,
    weights, sgrads, ustat, dks, dvs,
    dslots, near, summed, second, back, inverse_row,
    kt, vt, ot, dqt, att, drk_acc, drv_acc, parts, got, own_part,
    sem_in1, sem_in2s, sem_in2, sem_near, sem_og, local, sem_back_s, sem_back, sem_out1, sem_out2, sem_parts,
):
    me, mine = lax.axis_index("seq"), lax.axis_index("head")
    groups = max(2, seq // 8)
    per = seq // groups
    half = seq // 2
    mine_at = place_of(me, seq)
    group = mine_at // per
    of_kind = groups // 2
    chip_group = (me // 2) // per
    rows, feat = q.shape
    plen = kt.shape[2]
    width = og.shape[1]
    tiles = rows // TILE
    per_group = feat // 128
    lanes_n = TILE * per_group
    units = tiles + 2
    scale = 128**-0.5
    c = scale * LOG2E
    up, down = lax.rem(me + 1, seq), lax.rem(me + seq - 1, seq)
    slots = (slots_k, slots_v)

    loads = {}
    for n, (name, src, dst) in enumerate(
        (
            ("tok", tok_hbm, tok),
            ("owner", owner_hbm, owner),
            ("piece", kv.at[mine_at], first.at[me]),
            ("row", row_hbm, row),
            ("q", q_hbm, q),
            ("rk", rk_hbm, rk),
            ("rv", rv_hbm, rv),
            ("og", og, ogs.at[mine]),
            ("w", w_hbm, w),
        )
    ):
        loads[name] = pltpu.make_async_copy(src, dst, local.at[n])
        loads[name].start()
    greet(seq, heads)
    all_in(seq, heads)

    def spread(j):
        pltpu.make_async_remote_copy(
            kv.at[place_of(j, seq)], first.at[me], sem_in1.at[0], sem_in1.at[1], device_id=at_seq(j), device_id_type=MESH
        ).start()

    each_peer(seq, spread)
    right, left = lax.rem(mine + 1, heads), lax.rem(mine + heads - 1, heads)
    top_half, low_half = pl.ds(0, rows // 2), pl.ds(rows // 2, rows // 2)

    def send_og(n, src, at, part, peer):
        copy = pltpu.make_async_remote_copy(
            src.at[part], ogs.at[at, part], sem_og.at[0, n], sem_og.at[1, n],
            device_id=at_head(peer), device_id_type=MESH,
        )
        copy.start()
        return copy

    og_copies = [
        send_og(0, og, mine, top_half, right),
        send_og(1, og, mine, low_half, left),
        send_og(2, og, mine, low_half, right),
        send_og(3, og, mine, top_half, left),
    ]

    loads["tok"].wait()
    low = [lax.div(tok[t * TILE], GROUP) - (me - 1) for t in range(tiles)]
    high = [lax.div(tok[t * TILE + TILE - 1], GROUP) - (me - 1) for t in range(tiles)]
    offset = [jnp.int32(0)]
    for t in range(tiles):
        offset.append(offset[t] + high[t] - low[t] + 1)
        tile_first[t] = offset[t]
        tile_count[t] = high[t] - low[t] + 1
    slot_of_unit = []
    for n in range(units):
        t_n = add_all([count_if(offset[t] <= n) for t in range(1, tiles)])
        relative = low[0]
        for t in range(1, tiles):
            relative = jnp.where(offset[t] <= n, low[t] - offset[t], relative)
        p_n = relative + n
        s_n = jnp.clip(p_n, 0, 2)
        unit[0, n] = t_n
        unit[1, n] = p_n
        unit[2, n] = s_n
        unit[3, n] = count_if(s_n == slot_of_unit[-1]) if n else jnp.int32(0)
        slot_of_unit.append(s_n)
    slot_last = [add_all([count_if(s <= i) for s in slot_of_unit]) for i in range(3)]
    slot_used = [add_all([count_if(s == i) for s in slot_of_unit]) > 0 for i in range(3)]

    loads["row"].wait()
    row_f = row[...].astype(F32)
    column = jnp.broadcast_to(row_f, (128, rows)).T
    earlier = jnp.concatenate([column] * (-(-rows // 128)), axis=1)[:, :rows] < row_f
    start = jnp.sum(jnp.where(earlier, 1.0, 0.0), axis=0, keepdims=True)
    slot_row = (lax.div(row[...], GROUP) - (me - 1)).astype(F32)
    pick = lax.broadcasted_iota(jnp.int32, (16, rows), 0)
    facts = jnp.where(pick == 0, start, jnp.where(pick == 1, slot_row, 0.0)).astype(BF16)
    source = lax.broadcasted_iota(jnp.int32, (rows, lanes_n), 0)
    lane = lax.broadcasted_iota(jnp.int32, (rows, lanes_n), 1) & (TILE - 1)
    for t in range(tiles):
        chosen = jnp.where(source == lane + t * TILE, 1.0, 0.0).astype(BF16)
        lanes[t] = dot(facts, chosen, 1, 0)
    loads["q"].wait()
    for t in range(tiles):
        for h in range(per_group):
            qp[t, h * TILE : (h + 1) * TILE] = q[t * TILE : (t + 1) * TILE, h * 128 : (h + 1) * 128]

    spans = []
    for t in range(tiles):
        span = min(rows, -(-((t + 1) * TILE) // 128) * 128)
        if spans and spans[-1][2] == span:
            spans[-1][1] = t + 1
        else:
            spans.append([t, t + 1, span])

    def each_tile(step):
        for begin, end, span in spans:
            lax.fori_loop(begin, end, lambda t, _: (step(t, span), 0)[1], 0)

    def own_scores(t, span):
        key_id = lax.broadcasted_iota(jnp.int32, (span, lanes_n), 0)
        token = t * TILE + (lax.broadcasted_iota(jnp.int32, (1, lanes_n), 1) & (TILE - 1))
        visible = (key_id >= lanes[t, 0:1].astype(jnp.int32)) & (key_id <= token)
        s = jnp.where(visible, dot(rk[0:span], qp[t], 1, 1) * c, -1e30)
        top = jnp.max(s, axis=0, keepdims=True)
        e = jnp.exp2(s - top)
        er[t, 0:span] = e
        rstat[t, 0:1] = top
        rstat[t, 1:2] = jnp.sum(e, axis=0, keepdims=True)

    loads["rk"].wait()
    each_tile(own_scores)
    og_copies[0].wait_recv()
    og_copies.append(send_og(4, ogs.at[left], left, top_half, right))
    og_copies[1].wait_recv()
    og_copies.append(send_og(5, ogs.at[right], right, low_half, left))

    loads["owner"].wait()
    loads["piece"].wait()
    wait_bytes(first.at[pl.ds(0, seq - 1)], sem_in1.at[1])

    core, chip = lax.rem(me, 2), me // 2
    for kind in range(2):

        @pl.when(core == kind)
        def _():
            def deliver(p):
                order[p] = first[owner[p]]
                pltpu.make_async_remote_copy(
                    order.at[p], slots[kind].at[1, chip], sem_in2s, sem_in2.at[group],
                    device_id=at_seq(p), device_id_type=MESH,
                ).start()

            each_peer(seq, deliver)
            slots[kind][1, chip] = first[owner[me]]

    loads["og"].wait()
    loads["w"].wait()
    og_copies[2].wait_recv()
    og_copies[3].wait_recv()
    block = 256

    def w_columns(h, r):
        return w[pl.ds(r, block), pl.ds(pl.multiple_of(h * width, width), width)]

    def project_near(n, _):
        r = pl.multiple_of(n * block, block)
        total = dot(ogs[mine], w_columns(mine, r), 1, 1)
        for h in (right, left):
            total += dot(ogs[h], w_columns(h, r), 1, 1)
        ag[:, pl.ds(r, block)] = total
        return 0

    lax.fori_loop(0, feat // block, project_near, 0)

    def forward(n, kind):
        at = lax.rem(chip_group + 2 * of_kind - 1 - n, of_kind)
        g = kind * of_kind + at
        ref = slots[kind]

        @pl.when(g == group)
        def _():
            wait_bytes(ref.at[1, pl.ds(0, per - 1)], sem_in2.at[g])

        @pl.when(g != group)
        def _():
            wait_bytes(ref.at[1, pl.ds(0, per)], sem_in2.at[g])

        part = pl.ds(at * per, per)
        pltpu.make_async_remote_copy(
            ref.at[1, part], ref.at[0, part], sem_near.at[0, kind], sem_near.at[1, kind],
            device_id=at_seq(up), device_id_type=MESH,
        ).start()
        pltpu.make_async_remote_copy(
            ref.at[1, part], ref.at[2, part], sem_near.at[2, kind], sem_near.at[3, kind],
            device_id=at_seq(down), device_id_type=MESH,
        ).start()

    for n in range(of_kind):
        forward(n, 0)
    opposite = lax.rem(mine + 2, heads)
    og_copies[4].wait_recv()
    og_copies[5].wait_recv()

    def project_far(n, _):
        r = pl.multiple_of(n * block, block)
        total = (ag[:, pl.ds(r, block)] + dot(ogs[opposite], w_columns(opposite, r), 1, 1)).astype(BF16)
        for t in range(tiles):
            for h in range(block // 128):
                at = pl.multiple_of((n * (block // 128) + h) * TILE, TILE)
                gp[t, pl.ds(at, TILE)] = total[t * TILE : (t + 1) * TILE, h * 128 : (h + 1) * 128]
        return 0

    lax.fori_loop(0, feat // block, project_far, 0)
    dks[0] = jnp.zeros(dks.shape[1:], F32)
    dvs[0] = jnp.zeros(dvs.shape[1:], F32)
    for n in range(of_kind):
        forward(n, 1)
    wait_bytes(slots_k.at[0], sem_near.at[1, 0])
    wait_bytes(slots_k.at[2], sem_near.at[3, 0])

    def load_unit(n):
        t = unit[0, n]
        member = lanes[t, 1:2].astype(jnp.int32) == unit[1, n]
        stat = rstat[t]
        return dict(
            n=n, s=unit[2, n], q=qp[t], g=gp[t], member=member, same=unit[3, n] == 1,
            top=stat[0:1], total=stat[1:2], dots=stat[2:3],
        )

    def scores(u):
        u["sp"] = dot(slots_k[u["s"]].reshape(plen, 128), u["q"], 1, 1)

    def softmax(u):
        top = jnp.maximum(c * jnp.max(u["sp"], axis=0, keepdims=True), u["top"])
        e = jnp.exp2(u["sp"] * c - top)
        own = jnp.exp2(u["top"] - top)
        total = jnp.sum(e, axis=0, keepdims=True) + u["total"] * own
        inv = jnp.where(u["member"], 1.0 / total, 0.0)
        u["w"] = e * inv
        weights[u["n"]] = u["w"]
        ustat[u["n"], 0:1] = own * inv

    def value_sums(u):
        n = u["n"]
        dvs[n + 1] = jnp.where(u["same"], dvs[n], 0.0) + dot(u["w"].astype(BF16), u["g"], 1, 0)

    def value_dots(u):
        u["vp"] = dot(slots_v[u["s"]].reshape(plen, 128), u["g"], 1, 1)

    def score_grads(u):
        n = u["n"]
        wp = weights[n]
        dots = jnp.sum(wp * u["vp"], axis=0, keepdims=True) + u["dots"] * ustat[n, 0:1]
        u["gl"] = (wp * (u["vp"] - dots)).astype(BF16)
        sgrads[n] = u["gl"]
        ustat[n, 1:2] = dots

    def key_sums(u):
        n = u["n"]
        dks[n + 1] = jnp.where(u["same"], dks[n], 0.0) + dot(u["gl"], u["q"], 1, 0)

    def each_unit(*stages):
        def pair(i, _):
            two = [load_unit(2 * i), load_unit(2 * i + 1)]
            for stage in stages:
                for u in two:
                    stage(u)
            return 0

        lax.fori_loop(0, units // 2, pair, 0)

    def put_keys(i):
        x = jnp.where(slot_used[i], dks[slot_last[i]] * scale, 0.0)
        dslots[i, 0:half] = x.astype(BF16).reshape(half, -1, 128)

    def put_values(i):
        x = jnp.where(slot_used[i], dvs[slot_last[i]], 0.0)
        dslots[i, half:seq] = x.astype(BF16).reshape(half, -1, 128)

    def back_groups(kind):
        return [kind * of_kind + lax.rem(chip_group + n, of_kind) for n in range(of_kind)]

    def send_back(kind):
        for g in back_groups(kind):
            part = pl.ds(g * per, per)
            pltpu.make_async_remote_copy(
                dslots.at[2, part], near.at[0, part], sem_back_s.at[0], sem_back.at[0, g],
                device_id=at_seq(up), device_id_type=MESH,
            ).start()
            pltpu.make_async_remote_copy(
                dslots.at[0, part], near.at[1, part], sem_back_s.at[1], sem_back.at[1, g],
                device_id=at_seq(down), device_id_type=MESH,
            ).start()

    at_start, at_end = me == 0, me == seq - 1

    def sum_and_spread(kind):
        for g in back_groups(kind):
            part = pl.ds(g * per, per)
            wait_bytes(near.at[0, part], sem_back.at[0, g])
            wait_bytes(near.at[1, part], sem_back.at[1, g])
            below = jnp.where(at_start, 0.0, near[0, part].astype(F32))
            above = jnp.where(at_end, 0.0, near[1, part].astype(F32))
            summed[part] = (dslots[1, part].astype(F32) + below + above).astype(BF16)
            for i in range(per):
                piece = g * per + i
                j = 2 * (piece - kind * half) + kind

                @pl.when(j != me)
                def _():
                    pltpu.make_async_remote_copy(
                        summed.at[piece], second.at[me], sem_out1.at[0], sem_out1.at[1],
                        device_id=at_seq(j), device_id_type=MESH,
                    ).start()

    each_unit(scores, softmax, value_sums)

    put_values(0)
    put_values(2)
    send_back(1)
    put_values(1)
    loads["rv"].wait()

    def own_dots(t, span):
        v = dot(rv[0:span], gp[t], 1, 1)
        vr[t, 0:span] = v
        rstat[t, 2:3] = jnp.sum(v * er[t, 0:span], axis=0, keepdims=True)

    each_tile(own_dots)
    wait_bytes(slots_v.at[0], sem_near.at[1, 1])
    wait_bytes(slots_v.at[2], sem_near.at[3, 1])
    each_unit(value_dots, score_grads, key_sums)
    put_keys(0)
    put_keys(2)
    send_back(0)
    put_keys(1)
    sum_and_spread(1)

    spot = lax.broadcasted_iota(jnp.int32, inverse_row.shape, 1)
    found = jnp.zeros(inverse_row.shape, jnp.int32)
    for p in range(seq):
        found = jnp.where(spot == owner[p], p, found)
    inverse_row[...] = found
    to_scalars = pltpu.make_async_copy(inverse_row, inverse, local.at[len(loads)])
    to_scalars.start()
    for i in range(3):
        vt[i] = slots_v[i].reshape(plen, 128).T

    def unit_rows(n, _):
        ot[n] = dot(vt[unit[2, n]], weights[n].astype(BF16), 1, 0)
        return 0

    lax.fori_loop(0, units, unit_rows, 0)

    def of_tile(t, ref, row_slice=slice(None)):
        begin, many = tile_first[t], tile_count[t]
        total = ref[begin, row_slice]
        for j in range(1, 3):
            total += jnp.where(many > j, ref[jnp.minimum(begin + j, units - 1), row_slice], 0.0)
        return total

    def unit_facts(t):
        begin, many = tile_first[t], tile_count[t]
        slot = lanes[t, 1:2].astype(jnp.int32)
        factor, dots = 0.0, 0.0
        for j in range(3):
            n = jnp.minimum(begin + j, units - 1)
            member = (slot == unit[1, n]) & (many > j)
            factor += jnp.where(member, ustat[n, 0:1], 0.0)
            dots += jnp.where(member, ustat[n, 1:2], 0.0)
        return factor, dots

    rvt = rv[...].T

    def attend(t, span):
        factor, _ = unit_facts(t)
        o = of_tile(t, ot) + dot(rvt[:, 0:span], (er[t, 0:span] * factor).astype(BF16), 1, 0)
        o = o.T.astype(BF16)
        for h in range(per_group):
            att[pl.ds(pl.multiple_of(t * TILE, TILE), TILE), h * 128 : (h + 1) * 128] = o[h * TILE : (h + 1) * TILE]

    each_tile(attend)
    sum_and_spread(0)
    second[me] = summed[mine_at]

    def share(i):
        peer = lax.rem(mine + i, heads)
        return dot(att[...], w[:, pl.ds(pl.multiple_of(peer * width, width), width)], 1, 0)

    part_copies = []
    for i in range(1, heads):
        parts[i] = share(i).astype(BF16)
        copy = pltpu.make_async_remote_copy(
            parts.at[i], got.at[i], sem_parts.at[0, i], sem_parts.at[1, i],
            device_id=at_head(lax.rem(mine + i, heads)), device_id_type=MESH,
        )
        copy.start()
        part_copies.append(copy)

    to_scalars.wait()
    wait_bytes(second.at[pl.ds(0, seq - 1)], sem_out1.at[1])
    wait_bytes(order.at[pl.ds(0, seq - 1)], sem_in2s)

    def give_back(o):
        order[o] = second[inverse[0, o]]
        pltpu.make_async_remote_copy(
            order.at[o], back.at[mine_at], sem_out2.at[0], sem_out2.at[1], device_id=at_seq(o), device_id_type=MESH
        ).start()

    each_peer(seq, give_back)
    back[mine_at] = second[inverse[0, me]]

    own_part[...] = share(0)
    for i in range(3):
        kt[i] = slots_k[i].reshape(plen, 128).T

    def unit_query(n, _):
        dqt[n] = dot(kt[unit[2, n]], sgrads[n], 1, 0)
        return 0

    lax.fori_loop(0, units, unit_query, 0)
    rkt = rk[...].T
    drk_acc[...] = jnp.zeros_like(drk_acc)
    drv_acc[...] = jnp.zeros_like(drv_acc)

    def own_grads(t, span):
        factor, dots = unit_facts(t)
        wr = er[t, 0:span] * factor
        gr = (wr * (vr[t, 0:span] - dots)).astype(BF16)
        drv_acc[0:span] += dot(wr.astype(BF16), gp[t], 1, 0)
        drk_acc[0:span] += dot(gr, qp[t], 1, 0)
        d = ((of_tile(t, dqt) + dot(rkt[:, 0:span], gr, 1, 0)) * scale).T.astype(BF16)
        for h in range(per_group):
            dq[pl.ds(pl.multiple_of(t * TILE, TILE), TILE), h * 128 : (h + 1) * 128] = d[h * TILE : (h + 1) * TILE]

    each_tile(own_grads)
    drk[...] = (drk_acc[...] * scale).astype(BF16)
    drv[...] = drv_acc[...].astype(BF16)
    for copy in part_copies:
        copy.wait_recv()
    total = own_part[...]
    for i in range(1, heads):
        total += got[i].astype(F32)
    out[...] = total.astype(BF16)

    for copy in og_copies + part_copies:
        copy.wait_send()
    wait_bytes(first.at[pl.ds(0, seq - 1)], sem_in1.at[0])
    for side in (0, 2):
        wait_bytes(slots_k.at[1], sem_near.at[side, 0])
        wait_bytes(slots_v.at[1], sem_near.at[side, 1])
    wait_bytes(near.at[0], sem_back_s.at[0])
    wait_bytes(near.at[1], sem_back_s.at[1])
    wait_bytes(second.at[pl.ds(0, seq - 1)], sem_out1.at[0])
    wait_bytes(order.at[pl.ds(0, seq - 1)], sem_out2.at[0])
    wait_bytes(back.at[pl.ds(0, seq - 1)], sem_out2.at[1])
    grad[...] = back[...].astype(F32)


def store_kernel(*refs):
    many = (len(refs) - 1) // 2
    copies = [pltpu.make_async_copy(refs[i], refs[many + i], refs[-1].at[i]) for i in range(many)]
    for copy in copies:
        copy.start()
    for copy in copies:
        copy.wait()


def per_device(
    token_response, prompt_owner, queries, resp_keys, resp_values, prompt_kv, out_weight, out_grad
):
    seq, heads = lax.axis_size("seq"), lax.axis_size("head")
    vm = pl.BlockSpec(memory_space=pltpu.VMEM)
    hbm = pl.BlockSpec(memory_space=pltpu.HBM)
    pieces = prompt_kv.reshape(seq, -1, 128)
    plen = prompt_kv.shape[2]
    rows, feat = queries.shape
    width = out_grad.shape[1]
    tiles = rows // TILE
    units = tiles + 2
    lanes = TILE * feat // 128
    wide = -(-seq // 128) * 128
    groups = max(2, seq // 8)
    dma = pltpu.SemaphoreType.DMA
    shapes = (
        jax.ShapeDtypeStruct((rows, width), BF16),
        jax.ShapeDtypeStruct(queries.shape, BF16),
        jax.ShapeDtypeStruct(resp_keys.shape, BF16),
        jax.ShapeDtypeStruct(resp_values.shape, BF16),
        jax.ShapeDtypeStruct(pieces.shape, F32),
    )
    operands = (
        token_response, token_response.reshape(1, rows), prompt_owner, queries, resp_keys, resp_values,
        pieces, out_grad, out_weight,
    )
    results = pl.pallas_call(
        functools.partial(layer_kernel, seq, heads),
        out_shape=shapes,
        in_specs=[hbm] * len(operands),
        out_specs=(vm,) * len(shapes),
        scratch_shapes=[
            pltpu.SMEM((rows,), jnp.int32),
            pltpu.SMEM((seq,), jnp.int32),
            pltpu.SMEM((1, wide), jnp.int32),
            pltpu.SMEM((4, units), jnp.int32),
            pltpu.SMEM((tiles,), jnp.int32),
            pltpu.SMEM((tiles,), jnp.int32),
            pltpu.VMEM((1, rows), jnp.int32),
            pltpu.VMEM(queries.shape, BF16),
            pltpu.VMEM(resp_keys.shape, BF16),
            pltpu.VMEM(resp_values.shape, BF16),
            pltpu.VMEM(out_weight.shape, BF16),
            pltpu.VMEM((heads, rows, width), BF16),
            pltpu.VMEM(pieces.shape, BF16),
            pltpu.VMEM(pieces.shape, BF16),
            pltpu.VMEM((3, seq // 2) + pieces.shape[1:], BF16),
            pltpu.VMEM((3, seq // 2) + pieces.shape[1:], BF16),
            pltpu.VMEM((tiles, 16, lanes), F32),
            pltpu.VMEM(queries.shape, F32),
            pltpu.VMEM((tiles, lanes, 128), BF16),
            pltpu.VMEM((tiles, lanes, 128), BF16),
            pltpu.VMEM((tiles, rows, lanes), F32),
            pltpu.VMEM((tiles, rows, lanes), F32),
            pltpu.VMEM((tiles, 8, lanes), F32),
            pltpu.VMEM((units, plen, lanes), F32),
            pltpu.VMEM((units, plen, lanes), BF16),
            pltpu.VMEM((units, 8, lanes), F32),
            pltpu.VMEM((units + 1, plen, 128), F32),
            pltpu.VMEM((units + 1, plen, 128), F32),
            pltpu.VMEM((3,) + pieces.shape, BF16),
            pltpu.VMEM((2,) + pieces.shape, BF16),
            pltpu.VMEM(pieces.shape, BF16),
            pltpu.VMEM(pieces.shape, BF16),
            pltpu.VMEM(pieces.shape, BF16),
            pltpu.VMEM((1, wide), jnp.int32),
            pltpu.VMEM((3, 128, plen), BF16),
            pltpu.VMEM((3, 128, plen), BF16),
            pltpu.VMEM((units, 128, lanes), F32),
            pltpu.VMEM((units, 128, lanes), F32),
            pltpu.VMEM(queries.shape, BF16),
            pltpu.VMEM(resp_keys.shape, F32),
            pltpu.VMEM(resp_keys.shape, F32),
            pltpu.VMEM((heads, rows, width), BF16),
            pltpu.VMEM((heads, rows, width), BF16),
            pltpu.VMEM((rows, width), F32),
            dma((2,)),
            dma,
            dma((groups,)),
            dma((4, 2)),
            dma((2, 6)),
            dma((10,)),
            dma((2,)),
            dma((2, groups)),
            dma((2,)),
            dma((2,)),
            dma((2, heads)),
        ],
        compiler_params=pltpu.CompilerParams(
            collective_id=0, has_side_effects=True, vmem_limit_bytes=VMEM_LIMIT
        ),
        name="layer",
    )(*(in_hbm(x) for x in operands))
    layer_out, query_grad, key_grad, value_grad, prompt_grad = pl.pallas_call(
        store_kernel,
        out_shape=shapes,
        in_specs=[vm] * len(shapes),
        out_specs=(hbm,) * len(shapes),
        scratch_shapes=[dma((len(shapes),))],
        compiler_params=pltpu.CompilerParams(vmem_limit_bytes=4 * 2**20),
        name="store",
    )(*results)
    return (layer_out, query_grad, key_grad, value_grad, prompt_grad.reshape(prompt_kv.shape))


def solution(mesh):
    placed = (
        P("seq"),
        P(),
        P("seq", "head"),
        P("seq", "head"),
        P("seq", "head"),
        P("seq", None, None, "head"),
        P("head", None),
        P("seq", "head"),
    )
    return jax.shard_map(
        per_device,
        mesh=mesh,
        in_specs=placed,
        out_specs=(
            P("seq", "head"),
            P("seq", "head"),
            P("seq", "head"),
            P("seq", "head"),
            P("seq", None, None, "head"),
        ),
        check_vma=False,
    )
```

```python
import functools

import jax
import jax.numpy as jnp
from jax import lax
from jax.experimental import pallas as pl
from jax.experimental.pallas import tpu as pltpu
from jax.sharding import PartitionSpec as P

GROUP = 16
TILE = 32
LOG2E = 1.4426950408889634
F32, BF16 = jnp.float32, jnp.bfloat16
MESH = pl.DeviceIdType.MESH
VMEM_LIMIT = 52 * 2**20


def dot(a, b, ca, cb):
    return lax.dot_general(a, b, (((ca,), (cb,)), ((), ())), preferred_element_type=F32)


def at_seq(j):
    return (j, lax.axis_index("head"))


def at_head(j):
    return (lax.axis_index("seq"), j)


def greet(seq, heads):
    me, mine = lax.axis_index("seq"), lax.axis_index("head")
    barrier = pltpu.get_barrier_semaphore()

    def tell(i, _):
        pl.semaphore_signal(barrier, inc=1, device_id=at_seq(lax.rem(me + i, seq)), device_id_type=MESH)
        return 0

    lax.fori_loop(1, seq, tell, 0)
    for i in range(1, heads):
        pl.semaphore_signal(barrier, inc=1, device_id=at_head(lax.rem(mine + i, heads)), device_id_type=MESH)


def all_in(seq, heads):
    pl.semaphore_wait(pltpu.get_barrier_semaphore(), seq - 1 + heads - 1)


def each_peer(seq, visit, kinds=(0, 1)):
    me = lax.axis_index("seq")
    core, chip, chips = lax.rem(me, 2), me // 2, seq // 2
    for c in kinds:

        @pl.when(core != c)
        def _():
            visit(2 * chip + c)

        def go(t, _):
            visit(2 * lax.rem(chip + t, chips) + c)
            return 0

        lax.fori_loop(1, chips, go, 0)


def place_of(j, seq):
    return lax.rem(j, 2) * (seq // 2) + j // 2


def in_hbm(x):
    return pltpu.with_memory_space_constraint(x, pltpu.HBM)


def wait_bytes(ref, sem):
    pltpu.make_async_copy(ref, ref, sem).wait()


def add_all(terms):
    return functools.reduce(lambda a, b: a + b, terms)


def count_if(condition):
    return jnp.where(condition, 1, 0)


def layer_kernel(
    seq, heads,
    tok_hbm, row_hbm, owner_hbm, q_hbm, rk_hbm, rv_hbm, kv, og, w_hbm,
    out, dq, drk, drv, grad,
    tok, owner, inverse, unit, tile_first, tile_count,
    row, q, rk, rv, w, ogs,
    first, order, slots_k, slots_v, lanes, ag, qp, gp, er, vr, rstat,
    weights, sgrads, ustat, dks, dvs,
    dslots, near, summed, second, back, inverse_row,
    kt, vt, ot, dqt, att, drk_acc, drv_acc, parts, got, own_part,
    sem_in1, sem_in2s, sem_in2, sem_near, sem_og, local, sem_back_s, sem_back, sem_out1, sem_out2, sem_parts,
):
    me, mine = lax.axis_index("seq"), lax.axis_index("head")
    groups = max(2, seq // 8)
    per = seq // groups
    half = seq // 2
    mine_at = place_of(me, seq)
    group = mine_at // per
    of_kind = groups // 2
    chip_group = (me // 2) // per
    rows, feat = q.shape
    plen = kt.shape[2]
    width = og.shape[1]
    tiles = rows // TILE
    per_group = feat // 128
    lanes_n = TILE * per_group
    units = tiles + 2
    scale = 128**-0.5
    c = scale * LOG2E
    up, down = lax.rem(me + 1, seq), lax.rem(me + seq - 1, seq)
    slots = (slots_k, slots_v)

    loads = {}
    for n, (name, src, dst) in enumerate(
        (
            ("tok", tok_hbm, tok),
            ("owner", owner_hbm, owner),
            ("piece", kv.at[mine_at], first.at[me]),
            ("row", row_hbm, row),
            ("q", q_hbm, q),
            ("rk", rk_hbm, rk),
            ("rv", rv_hbm, rv),
            ("og", og, ogs.at[mine]),
            ("w", w_hbm, w),
        )
    ):
        loads[name] = pltpu.make_async_copy(src, dst, local.at[n])
        loads[name].start()
    greet(seq, heads)
    all_in(seq, heads)

    right, left = lax.rem(mine + 1, heads), lax.rem(mine + heads - 1, heads)
    top_half, low_half = pl.ds(0, rows // 2), pl.ds(rows // 2, rows // 2)

    def send_og(n, src, at, part, peer):
        copy = pltpu.make_async_remote_copy(
            src.at[part], ogs.at[at, part], sem_og.at[0, n], sem_og.at[1, n],
            device_id=at_head(peer), device_id_type=MESH,
        )
        copy.start()
        return copy

    og_copies = [
        send_og(0, og, mine, top_half, right),
        send_og(1, og, mine, low_half, left),
        send_og(2, og, mine, low_half, right),
        send_og(3, og, mine, top_half, left),
    ]

    def spread(j):
        pltpu.make_async_remote_copy(
            kv.at[place_of(j, seq)], first.at[me], sem_in1.at[0], sem_in1.at[1], device_id=at_seq(j), device_id_type=MESH
        ).start()

    each_peer(seq, spread, (0,))
    loads["tok"].wait()
    low = [lax.div(tok[t * TILE], GROUP) - (me - 1) for t in range(tiles)]
    high = [lax.div(tok[t * TILE + TILE - 1], GROUP) - (me - 1) for t in range(tiles)]
    offset = [jnp.int32(0)]
    for t in range(tiles):
        offset.append(offset[t] + high[t] - low[t] + 1)
        tile_first[t] = offset[t]
        tile_count[t] = high[t] - low[t] + 1
    slot_of_unit = []
    for n in range(units):
        t_n = add_all([count_if(offset[t] <= n) for t in range(1, tiles)])
        relative = low[0]
        for t in range(1, tiles):
            relative = jnp.where(offset[t] <= n, low[t] - offset[t], relative)
        p_n = relative + n
        s_n = jnp.clip(p_n, 0, 2)
        unit[0, n] = t_n
        unit[1, n] = p_n
        unit[2, n] = s_n
        unit[3, n] = count_if(s_n == slot_of_unit[-1]) if n else jnp.int32(0)
        slot_of_unit.append(s_n)
    slot_last = [add_all([count_if(s <= i) for s in slot_of_unit]) for i in range(3)]
    slot_used = [add_all([count_if(s == i) for s in slot_of_unit]) > 0 for i in range(3)]

    loads["row"].wait()
    row_f = row[...].astype(F32)
    column = jnp.broadcast_to(row_f, (128, rows)).T
    earlier = jnp.concatenate([column] * (-(-rows // 128)), axis=1)[:, :rows] < row_f
    start = jnp.sum(jnp.where(earlier, 1.0, 0.0), axis=0, keepdims=True)
    slot_row = (lax.div(row[...], GROUP) - (me - 1)).astype(F32)
    pick = lax.broadcasted_iota(jnp.int32, (16, rows), 0)
    facts = jnp.where(pick == 0, start, jnp.where(pick == 1, slot_row, 0.0)).astype(BF16)
    source = lax.broadcasted_iota(jnp.int32, (rows, lanes_n), 0)
    lane = lax.broadcasted_iota(jnp.int32, (rows, lanes_n), 1) & (TILE - 1)
    for t in range(tiles):
        chosen = jnp.where(source == lane + t * TILE, 1.0, 0.0).astype(BF16)
        lanes[t] = dot(facts, chosen, 1, 0)
    loads["q"].wait()
    for t in range(tiles):
        for h in range(per_group):
            qp[t, h * TILE : (h + 1) * TILE] = q[t * TILE : (t + 1) * TILE, h * 128 : (h + 1) * 128]

    spans = []
    for t in range(tiles):
        span = min(rows, -(-((t + 1) * TILE) // 128) * 128)
        if spans and spans[-1][2] == span:
            spans[-1][1] = t + 1
        else:
            spans.append([t, t + 1, span])

    def each_tile(step):
        for begin, end, span in spans:
            lax.fori_loop(begin, end, lambda t, _: (step(t, span), 0)[1], 0)

    def own_scores(t, span):
        key_id = lax.broadcasted_iota(jnp.int32, (span, lanes_n), 0)
        token = t * TILE + (lax.broadcasted_iota(jnp.int32, (1, lanes_n), 1) & (TILE - 1))
        visible = (key_id >= lanes[t, 0:1].astype(jnp.int32)) & (key_id <= token)
        s = jnp.where(visible, dot(rk[0:span], qp[t], 1, 1) * c, -1e30)
        top = jnp.max(s, axis=0, keepdims=True)
        e = jnp.exp2(s - top)
        er[t, 0:span] = e
        rstat[t, 0:1] = top
        rstat[t, 1:2] = jnp.sum(e, axis=0, keepdims=True)

    loads["rk"].wait()
    each_tile(own_scores)
    each_peer(seq, spread, (1,))
    og_copies[0].wait_recv()
    og_copies.append(send_og(4, ogs.at[left], left, top_half, right))
    og_copies[1].wait_recv()
    og_copies.append(send_og(5, ogs.at[right], right, low_half, left))

    loads["owner"].wait()
    loads["piece"].wait()
    wait_bytes(first.at[pl.ds(0, seq - 1)], sem_in1.at[1])

    core, chip = lax.rem(me, 2), me // 2
    for kind in range(2):

        @pl.when(core == kind)
        def _():
            def deliver(p):
                order[p] = first[owner[p]]
                pltpu.make_async_remote_copy(
                    order.at[p], slots[kind].at[1, chip], sem_in2s, sem_in2.at[group],
                    device_id=at_seq(p), device_id_type=MESH,
                ).start()

            each_peer(seq, deliver)
            slots[kind][1, chip] = first[owner[me]]

    loads["og"].wait()
    loads["w"].wait()
    og_copies[2].wait_recv()
    og_copies[3].wait_recv()
    block = 256

    def w_columns(h, r):
        return w[pl.ds(r, block), pl.ds(pl.multiple_of(h * width, width), width)]

    def project_near(n, _):
        r = pl.multiple_of(n * block, block)
        total = dot(ogs[mine], w_columns(mine, r), 1, 1)
        for h in (right, left):
            total += dot(ogs[h], w_columns(h, r), 1, 1)
        ag[:, pl.ds(r, block)] = total
        return 0

    lax.fori_loop(0, feat // block, project_near, 0)

    def forward(n, kind):
        at = lax.rem(chip_group + 2 * of_kind - 1 - n, of_kind)
        g = kind * of_kind + at
        ref = slots[kind]

        @pl.when(g == group)
        def _():
            wait_bytes(ref.at[1, pl.ds(0, per - 1)], sem_in2.at[g])

        @pl.when(g != group)
        def _():
            wait_bytes(ref.at[1, pl.ds(0, per)], sem_in2.at[g])

        part = pl.ds(at * per, per)
        pltpu.make_async_remote_copy(
            ref.at[1, part], ref.at[0, part], sem_near.at[0, kind], sem_near.at[1, kind],
            device_id=at_seq(up), device_id_type=MESH,
        ).start()
        pltpu.make_async_remote_copy(
            ref.at[1, part], ref.at[2, part], sem_near.at[2, kind], sem_near.at[3, kind],
            device_id=at_seq(down), device_id_type=MESH,
        ).start()

    for n in range(of_kind):
        forward(n, 0)
    opposite = lax.rem(mine + 2, heads)
    og_copies[4].wait_recv()
    og_copies[5].wait_recv()

    def project_far(n, _):
        r = pl.multiple_of(n * block, block)
        total = (ag[:, pl.ds(r, block)] + dot(ogs[opposite], w_columns(opposite, r), 1, 1)).astype(BF16)
        for t in range(tiles):
            for h in range(block // 128):
                at = pl.multiple_of((n * (block // 128) + h) * TILE, TILE)
                gp[t, pl.ds(at, TILE)] = total[t * TILE : (t + 1) * TILE, h * 128 : (h + 1) * 128]
        return 0

    lax.fori_loop(0, feat // block, project_far, 0)
    dks[0] = jnp.zeros(dks.shape[1:], F32)
    dvs[0] = jnp.zeros(dvs.shape[1:], F32)
    for n in range(of_kind):
        forward(n, 1)
    wait_bytes(slots_k.at[0], sem_near.at[1, 0])
    wait_bytes(slots_k.at[2], sem_near.at[3, 0])

    def load_unit(n):
        t = unit[0, n]
        member = lanes[t, 1:2].astype(jnp.int32) == unit[1, n]
        stat = rstat[t]
        return dict(
            n=n, s=unit[2, n], q=qp[t], g=gp[t], member=member, same=unit[3, n] == 1,
            top=stat[0:1], total=stat[1:2], dots=stat[2:3],
        )

    def scores(u):
        u["sp"] = dot(slots_k[u["s"]].reshape(plen, 128), u["q"], 1, 1)

    def softmax(u):
        top = jnp.maximum(c * jnp.max(u["sp"], axis=0, keepdims=True), u["top"])
        e = jnp.exp2(u["sp"] * c - top)
        own = jnp.exp2(u["top"] - top)
        total = jnp.sum(e, axis=0, keepdims=True) + u["total"] * own
        inv = jnp.where(u["member"], 1.0 / total, 0.0)
        u["w"] = e * inv
        weights[u["n"]] = u["w"]
        ustat[u["n"], 0:1] = own * inv

    def value_sums(u):
        n = u["n"]
        dvs[n + 1] = jnp.where(u["same"], dvs[n], 0.0) + dot(u["w"].astype(BF16), u["g"], 1, 0)

    def value_dots(u):
        u["vp"] = dot(slots_v[u["s"]].reshape(plen, 128), u["g"], 1, 1)

    def score_grads(u):
        n = u["n"]
        wp = weights[n]
        dots = jnp.sum(wp * u["vp"], axis=0, keepdims=True) + u["dots"] * ustat[n, 0:1]
        u["gl"] = (wp * (u["vp"] - dots)).astype(BF16)
        sgrads[n] = u["gl"]
        ustat[n, 1:2] = dots

    def key_sums(u):
        n = u["n"]
        dks[n + 1] = jnp.where(u["same"], dks[n], 0.0) + dot(u["gl"], u["q"], 1, 0)

    def each_unit(*stages):
        def pair(i, _):
            two = [load_unit(2 * i), load_unit(2 * i + 1)]
            for stage in stages:
                for u in two:
                    stage(u)
            return 0

        lax.fori_loop(0, units // 2, pair, 0)

    def put_keys(i):
        x = jnp.where(slot_used[i], dks[slot_last[i]] * scale, 0.0)
        dslots[i, 0:half] = x.astype(BF16).reshape(half, -1, 128)

    def put_values(i):
        x = jnp.where(slot_used[i], dvs[slot_last[i]], 0.0)
        dslots[i, half:seq] = x.astype(BF16).reshape(half, -1, 128)

    def back_groups(kind):
        return [kind * of_kind + lax.rem(chip_group + n, of_kind) for n in range(of_kind)]

    def send_back(kind):
        for g in back_groups(kind):
            part = pl.ds(g * per, per)
            pltpu.make_async_remote_copy(
                dslots.at[2, part], near.at[0, part], sem_back_s.at[0], sem_back.at[0, g],
                device_id=at_seq(up), device_id_type=MESH,
            ).start()
            pltpu.make_async_remote_copy(
                dslots.at[0, part], near.at[1, part], sem_back_s.at[1], sem_back.at[1, g],
                device_id=at_seq(down), device_id_type=MESH,
            ).start()

    at_start, at_end = me == 0, me == seq - 1

    def sum_and_spread(kind):
        for g in back_groups(kind):
            part = pl.ds(g * per, per)
            wait_bytes(near.at[0, part], sem_back.at[0, g])
            wait_bytes(near.at[1, part], sem_back.at[1, g])
            below = jnp.where(at_start, 0.0, near[0, part].astype(F32))
            above = jnp.where(at_end, 0.0, near[1, part].astype(F32))
            summed[part] = (dslots[1, part].astype(F32) + below + above).astype(BF16)
            for i in range(per):
                piece = g * per + i
                j = 2 * (piece - kind * half) + kind

                @pl.when(j != me)
                def _():
                    pltpu.make_async_remote_copy(
                        summed.at[piece], second.at[me], sem_out1.at[0], sem_out1.at[1],
                        device_id=at_seq(j), device_id_type=MESH,
                    ).start()

    each_unit(scores, softmax, value_sums)

    put_values(0)
    put_values(2)
    send_back(1)
    put_values(1)
    loads["rv"].wait()

    def own_dots(t, span):
        v = dot(rv[0:span], gp[t], 1, 1)
        vr[t, 0:span] = v
        rstat[t, 2:3] = jnp.sum(v * er[t, 0:span], axis=0, keepdims=True)

    each_tile(own_dots)
    wait_bytes(slots_v.at[0], sem_near.at[1, 1])
    wait_bytes(slots_v.at[2], sem_near.at[3, 1])
    each_unit(value_dots, score_grads, key_sums)
    put_keys(0)
    put_keys(2)
    send_back(0)
    put_keys(1)
    sum_and_spread(1)

    spot = lax.broadcasted_iota(jnp.int32, inverse_row.shape, 1)
    found = jnp.zeros(inverse_row.shape, jnp.int32)
    for p in range(seq):
        found = jnp.where(spot == owner[p], p, found)
    inverse_row[...] = found
    to_scalars = pltpu.make_async_copy(inverse_row, inverse, local.at[len(loads)])
    to_scalars.start()
    for i in range(3):
        vt[i] = slots_v[i].reshape(plen, 128).T

    def unit_rows(n, _):
        ot[n] = dot(vt[unit[2, n]], weights[n].astype(BF16), 1, 0)
        return 0

    lax.fori_loop(0, units, unit_rows, 0)

    def of_tile(t, ref, row_slice=slice(None)):
        begin, many = tile_first[t], tile_count[t]
        total = ref[begin, row_slice]
        for j in range(1, 3):
            total += jnp.where(many > j, ref[jnp.minimum(begin + j, units - 1), row_slice], 0.0)
        return total

    def unit_facts(t):
        begin, many = tile_first[t], tile_count[t]
        slot = lanes[t, 1:2].astype(jnp.int32)
        factor, dots = 0.0, 0.0
        for j in range(3):
            n = jnp.minimum(begin + j, units - 1)
            member = (slot == unit[1, n]) & (many > j)
            factor += jnp.where(member, ustat[n, 0:1], 0.0)
            dots += jnp.where(member, ustat[n, 1:2], 0.0)
        return factor, dots

    rvt = rv[...].T

    def attend(t, span):
        factor, _ = unit_facts(t)
        o = of_tile(t, ot) + dot(rvt[:, 0:span], (er[t, 0:span] * factor).astype(BF16), 1, 0)
        o = o.T.astype(BF16)
        for h in range(per_group):
            att[pl.ds(pl.multiple_of(t * TILE, TILE), TILE), h * 128 : (h + 1) * 128] = o[h * TILE : (h + 1) * TILE]

    each_tile(attend)
    sum_and_spread(0)
    second[me] = summed[mine_at]

    def share(i):
        peer = lax.rem(mine + i, heads)
        return dot(att[...], w[:, pl.ds(pl.multiple_of(peer * width, width), width)], 1, 0)

    part_copies = []
    for i in range(1, heads):
        parts[i] = share(i).astype(BF16)
        copy = pltpu.make_async_remote_copy(
            parts.at[i], got.at[i], sem_parts.at[0, i], sem_parts.at[1, i],
            device_id=at_head(lax.rem(mine + i, heads)), device_id_type=MESH,
        )
        copy.start()
        part_copies.append(copy)

    to_scalars.wait()
    wait_bytes(second.at[pl.ds(0, seq - 1)], sem_out1.at[1])
    wait_bytes(order.at[pl.ds(0, seq - 1)], sem_in2s)

    def give_back(o):
        order[o] = second[inverse[0, o]]
        pltpu.make_async_remote_copy(
            order.at[o], back.at[mine_at], sem_out2.at[0], sem_out2.at[1], device_id=at_seq(o), device_id_type=MESH
        ).start()

    each_peer(seq, give_back)
    back[mine_at] = second[inverse[0, me]]

    own_part[...] = share(0)
    for i in range(3):
        kt[i] = slots_k[i].reshape(plen, 128).T

    def unit_query(n, _):
        dqt[n] = dot(kt[unit[2, n]], sgrads[n], 1, 0)
        return 0

    lax.fori_loop(0, units, unit_query, 0)
    rkt = rk[...].T
    drk_acc[...] = jnp.zeros_like(drk_acc)
    drv_acc[...] = jnp.zeros_like(drv_acc)

    def own_grads(t, span):
        factor, dots = unit_facts(t)
        wr = er[t, 0:span] * factor
        gr = (wr * (vr[t, 0:span] - dots)).astype(BF16)
        drv_acc[0:span] += dot(wr.astype(BF16), gp[t], 1, 0)
        drk_acc[0:span] += dot(gr, qp[t], 1, 0)
        d = ((of_tile(t, dqt) + dot(rkt[:, 0:span], gr, 1, 0)) * scale).T.astype(BF16)
        for h in range(per_group):
            dq[pl.ds(pl.multiple_of(t * TILE, TILE), TILE), h * 128 : (h + 1) * 128] = d[h * TILE : (h + 1) * TILE]

    each_tile(own_grads)
    drk[...] = (drk_acc[...] * scale).astype(BF16)
    drv[...] = drv_acc[...].astype(BF16)
    for copy in part_copies:
        copy.wait_recv()
    total = own_part[...]
    for i in range(1, heads):
        total += got[i].astype(F32)
    out[...] = total.astype(BF16)

    for copy in og_copies + part_copies:
        copy.wait_send()
    wait_bytes(first.at[pl.ds(0, seq - 1)], sem_in1.at[0])
    for side in (0, 2):
        wait_bytes(slots_k.at[1], sem_near.at[side, 0])
        wait_bytes(slots_v.at[1], sem_near.at[side, 1])
    wait_bytes(near.at[0], sem_back_s.at[0])
    wait_bytes(near.at[1], sem_back_s.at[1])
    wait_bytes(second.at[pl.ds(0, seq - 1)], sem_out1.at[0])
    wait_bytes(order.at[pl.ds(0, seq - 1)], sem_out2.at[0])
    wait_bytes(back.at[pl.ds(0, seq - 1)], sem_out2.at[1])
    grad[...] = back[...].astype(F32)


def store_kernel(*refs):
    many = (len(refs) - 1) // 2
    copies = [pltpu.make_async_copy(refs[i], refs[many + i], refs[-1].at[i]) for i in range(many)]
    for copy in copies:
        copy.start()
    for copy in copies:
        copy.wait()


def per_device(
    token_response, prompt_owner, queries, resp_keys, resp_values, prompt_kv, out_weight, out_grad
):
    seq, heads = lax.axis_size("seq"), lax.axis_size("head")
    vm = pl.BlockSpec(memory_space=pltpu.VMEM)
    hbm = pl.BlockSpec(memory_space=pltpu.HBM)
    pieces = prompt_kv.reshape(seq, -1, 128)
    plen = prompt_kv.shape[2]
    rows, feat = queries.shape
    width = out_grad.shape[1]
    tiles = rows // TILE
    units = tiles + 2
    lanes = TILE * feat // 128
    wide = -(-seq // 128) * 128
    groups = max(2, seq // 8)
    dma = pltpu.SemaphoreType.DMA
    shapes = (
        jax.ShapeDtypeStruct((rows, width), BF16),
        jax.ShapeDtypeStruct(queries.shape, BF16),
        jax.ShapeDtypeStruct(resp_keys.shape, BF16),
        jax.ShapeDtypeStruct(resp_values.shape, BF16),
        jax.ShapeDtypeStruct(pieces.shape, F32),
    )
    operands = (
        token_response, token_response.reshape(1, rows), prompt_owner, queries, resp_keys, resp_values,
        pieces, out_grad, out_weight,
    )
    results = pl.pallas_call(
        functools.partial(layer_kernel, seq, heads),
        out_shape=shapes,
        in_specs=[hbm] * len(operands),
        out_specs=(vm,) * len(shapes),
        scratch_shapes=[
            pltpu.SMEM((rows,), jnp.int32),
            pltpu.SMEM((seq,), jnp.int32),
            pltpu.SMEM((1, wide), jnp.int32),
            pltpu.SMEM((4, units), jnp.int32),
            pltpu.SMEM((tiles,), jnp.int32),
            pltpu.SMEM((tiles,), jnp.int32),
            pltpu.VMEM((1, rows), jnp.int32),
            pltpu.VMEM(queries.shape, BF16),
            pltpu.VMEM(resp_keys.shape, BF16),
            pltpu.VMEM(resp_values.shape, BF16),
            pltpu.VMEM(out_weight.shape, BF16),
            pltpu.VMEM((heads, rows, width), BF16),
            pltpu.VMEM(pieces.shape, BF16),
            pltpu.VMEM(pieces.shape, BF16),
            pltpu.VMEM((3, seq // 2) + pieces.shape[1:], BF16),
            pltpu.VMEM((3, seq // 2) + pieces.shape[1:], BF16),
            pltpu.VMEM((tiles, 16, lanes), F32),
            pltpu.VMEM(queries.shape, F32),
            pltpu.VMEM((tiles, lanes, 128), BF16),
            pltpu.VMEM((tiles, lanes, 128), BF16),
            pltpu.VMEM((tiles, rows, lanes), F32),
            pltpu.VMEM((tiles, rows, lanes), F32),
            pltpu.VMEM((tiles, 8, lanes), F32),
            pltpu.VMEM((units, plen, lanes), F32),
            pltpu.VMEM((units, plen, lanes), BF16),
            pltpu.VMEM((units, 8, lanes), F32),
            pltpu.VMEM((units + 1, plen, 128), F32),
            pltpu.VMEM((units + 1, plen, 128), F32),
            pltpu.VMEM((3,) + pieces.shape, BF16),
            pltpu.VMEM((2,) + pieces.shape, BF16),
            pltpu.VMEM(pieces.shape, BF16),
            pltpu.VMEM(pieces.shape, BF16),
            pltpu.VMEM(pieces.shape, BF16),
            pltpu.VMEM((1, wide), jnp.int32),
            pltpu.VMEM((3, 128, plen), BF16),
            pltpu.VMEM((3, 128, plen), BF16),
            pltpu.VMEM((units, 128, lanes), F32),
            pltpu.VMEM((units, 128, lanes), F32),
            pltpu.VMEM(queries.shape, BF16),
            pltpu.VMEM(resp_keys.shape, F32),
            pltpu.VMEM(resp_keys.shape, F32),
            pltpu.VMEM((heads, rows, width), BF16),
            pltpu.VMEM((heads, rows, width), BF16),
            pltpu.VMEM((rows, width), F32),
            dma((2,)),
            dma,
            dma((groups,)),
            dma((4, 2)),
            dma((2, 6)),
            dma((10,)),
            dma((2,)),
            dma((2, groups)),
            dma((2,)),
            dma((2,)),
            dma((2, heads)),
        ],
        compiler_params=pltpu.CompilerParams(
            collective_id=0, has_side_effects=True, vmem_limit_bytes=VMEM_LIMIT
        ),
        name="layer",
    )(*(in_hbm(x) for x in operands))
    layer_out, query_grad, key_grad, value_grad, prompt_grad = pl.pallas_call(
        store_kernel,
        out_shape=shapes,
        in_specs=[vm] * len(shapes),
        out_specs=(hbm,) * len(shapes),
        scratch_shapes=[dma((len(shapes),))],
        compiler_params=pltpu.CompilerParams(vmem_limit_bytes=4 * 2**20),
        name="store",
    )(*results)
    return (layer_out, query_grad, key_grad, value_grad, prompt_grad.reshape(prompt_kv.shape))


def solution(mesh):
    placed = (
        P("seq"),
        P(),
        P("seq", "head"),
        P("seq", "head"),
        P("seq", "head"),
        P("seq", None, None, "head"),
        P("head", None),
        P("seq", "head"),
    )
    return jax.shard_map(
        per_device,
        mesh=mesh,
        in_specs=placed,
        out_specs=(
            P("seq", "head"),
            P("seq", "head"),
            P("seq", "head"),
            P("seq", "head"),
            P("seq", None, None, "head"),
        ),
        check_vma=False,
    )
```

```python
import functools

import jax
import jax.numpy as jnp
from jax import lax
from jax.experimental import pallas as pl
from jax.experimental.pallas import tpu as pltpu
from jax.sharding import PartitionSpec as P

GROUP = 16
TILE = 32
LOG2E = 1.4426950408889634
F32, BF16 = jnp.float32, jnp.bfloat16
MESH = pl.DeviceIdType.MESH
VMEM_LIMIT = 52 * 2**20


def dot(a, b, ca, cb):
    return lax.dot_general(a, b, (((ca,), (cb,)), ((), ())), preferred_element_type=F32)


def at_seq(j):
    return (j, lax.axis_index("head"))


def at_head(j):
    return (lax.axis_index("seq"), j)


def greet(seq, heads):
    me, mine = lax.axis_index("seq"), lax.axis_index("head")
    barrier = pltpu.get_barrier_semaphore()

    def tell(i, _):
        pl.semaphore_signal(barrier, inc=1, device_id=at_seq(lax.rem(me + i, seq)), device_id_type=MESH)
        return 0

    lax.fori_loop(1, seq, tell, 0)
    for i in range(1, heads):
        pl.semaphore_signal(barrier, inc=1, device_id=at_head(lax.rem(mine + i, heads)), device_id_type=MESH)


def all_in(seq, heads):
    pl.semaphore_wait(pltpu.get_barrier_semaphore(), seq - 1 + heads - 1)


def each_peer(seq, visit, kinds=(0, 1)):
    me = lax.axis_index("seq")
    core, chip, chips = lax.rem(me, 2), me // 2, seq // 2
    for c in kinds:

        @pl.when(core != c)
        def _():
            visit(2 * chip + c)

        def go(t, _):
            visit(2 * lax.rem(chip + t, chips) + c)
            return 0

        lax.fori_loop(1, chips, go, 0)


def place_of(j, seq):
    return lax.rem(j, 2) * (seq // 2) + j // 2


def in_hbm(x):
    return pltpu.with_memory_space_constraint(x, pltpu.HBM)


def wait_bytes(ref, sem):
    pltpu.make_async_copy(ref, ref, sem).wait()


def add_all(terms):
    return functools.reduce(lambda a, b: a + b, terms)


def count_if(condition):
    return jnp.where(condition, 1, 0)


def layer_kernel(
    seq, heads,
    tok_hbm, row_hbm, owner_hbm, q_hbm, rk_hbm, rv_hbm, kv, og, w_hbm,
    out, dq, drk, drv, grad,
    tok, owner, inverse, unit, tile_first, tile_count,
    row, q, rk, rv, w, ogs,
    first, order, slots_k, slots_v, lanes, ag, qp, gp, er, vr, rstat,
    weights, sgrads, ustat, dks, dvs,
    dslots, near, summed, second, back, inverse_row,
    kt, vt, ot, dqt, att, drk_acc, drv_acc, parts, got, own_part,
    sem_in1, sem_in2s, sem_in2, sem_near, sem_og, local, sem_back_s, sem_back, sem_out1, sem_out2, sem_parts,
):
    me, mine = lax.axis_index("seq"), lax.axis_index("head")
    groups = max(2, seq // 8)
    per = seq // groups
    half = seq // 2
    mine_at = place_of(me, seq)
    group = mine_at // per
    of_kind = groups // 2
    chip_group = (me // 2) // per
    rows, feat = q.shape
    plen = kt.shape[2]
    width = og.shape[1]
    tiles = rows // TILE
    per_group = feat // 128
    lanes_n = TILE * per_group
    units = tiles + 2
    scale = 128**-0.5
    c = scale * LOG2E
    up, down = lax.rem(me + 1, seq), lax.rem(me + seq - 1, seq)
    slots = (slots_k, slots_v)

    loads = {}
    for n, (name, src, dst) in enumerate(
        (
            ("tok", tok_hbm, tok),
            ("owner", owner_hbm, owner),
            ("piece", kv.at[mine_at], first.at[me]),
            ("row", row_hbm, row),
            ("q", q_hbm, q),
            ("rk", rk_hbm, rk),
            ("rv", rv_hbm, rv),
            ("og", og, ogs.at[mine]),
            ("w", w_hbm, w),
        )
    ):
        loads[name] = pltpu.make_async_copy(src, dst, local.at[n])
        loads[name].start()
    greet(seq, heads)
    all_in(seq, heads)

    right, left = lax.rem(mine + 1, heads), lax.rem(mine + heads - 1, heads)
    top_half, low_half = pl.ds(0, rows // 2), pl.ds(rows // 2, rows // 2)

    def send_og(n, src, at, part, peer):
        copy = pltpu.make_async_remote_copy(
            src.at[part], ogs.at[at, part], sem_og.at[0, n], sem_og.at[1, n],
            device_id=at_head(peer), device_id_type=MESH,
        )
        copy.start()
        return copy

    og_copies = [
        send_og(0, og, mine, top_half, right),
        send_og(1, og, mine, low_half, left),
        send_og(2, og, mine, low_half, right),
        send_og(3, og, mine, top_half, left),
    ]

    def spread(j):
        pltpu.make_async_remote_copy(
            kv.at[place_of(j, seq)], first.at[me], sem_in1.at[0], sem_in1.at[1], device_id=at_seq(j), device_id_type=MESH
        ).start()

    each_peer(seq, spread, (0,))
    loads["tok"].wait()
    low = [lax.div(tok[t * TILE], GROUP) - (me - 1) for t in range(tiles)]
    high = [lax.div(tok[t * TILE + TILE - 1], GROUP) - (me - 1) for t in range(tiles)]
    offset = [jnp.int32(0)]
    for t in range(tiles):
        offset.append(offset[t] + high[t] - low[t] + 1)
        tile_first[t] = offset[t]
        tile_count[t] = high[t] - low[t] + 1
    slot_of_unit = []
    for n in range(units):
        t_n = add_all([count_if(offset[t] <= n) for t in range(1, tiles)])
        relative = low[0]
        for t in range(1, tiles):
            relative = jnp.where(offset[t] <= n, low[t] - offset[t], relative)
        p_n = relative + n
        s_n = jnp.clip(p_n, 0, 2)
        unit[0, n] = t_n
        unit[1, n] = p_n
        unit[2, n] = s_n
        unit[3, n] = count_if(s_n == slot_of_unit[-1]) if n else jnp.int32(0)
        slot_of_unit.append(s_n)
    slot_last = [add_all([count_if(s <= i) for s in slot_of_unit]) for i in range(3)]
    slot_used = [add_all([count_if(s == i) for s in slot_of_unit]) > 0 for i in range(3)]

    loads["row"].wait()
    row_f = row[...].astype(F32)
    column = jnp.broadcast_to(row_f, (128, rows)).T
    earlier = jnp.concatenate([column] * (-(-rows // 128)), axis=1)[:, :rows] < row_f
    start = jnp.sum(jnp.where(earlier, 1.0, 0.0), axis=0, keepdims=True)
    slot_row = (lax.div(row[...], GROUP) - (me - 1)).astype(F32)
    pick = lax.broadcasted_iota(jnp.int32, (16, rows), 0)
    facts = jnp.where(pick == 0, start, jnp.where(pick == 1, slot_row, 0.0)).astype(BF16)
    source = lax.broadcasted_iota(jnp.int32, (rows, lanes_n), 0)
    lane = lax.broadcasted_iota(jnp.int32, (rows, lanes_n), 1) & (TILE - 1)
    for t in range(tiles):
        chosen = jnp.where(source == lane + t * TILE, 1.0, 0.0).astype(BF16)
        lanes[t] = dot(facts, chosen, 1, 0)
    loads["q"].wait()
    for t in range(tiles):
        for h in range(per_group):
            qp[t, h * TILE : (h + 1) * TILE] = q[t * TILE : (t + 1) * TILE, h * 128 : (h + 1) * 128]

    spans = []
    for t in range(tiles):
        span = min(rows, -(-((t + 1) * TILE) // 128) * 128)
        if spans and spans[-1][2] == span:
            spans[-1][1] = t + 1
        else:
            spans.append([t, t + 1, span])

    def each_tile(step):
        for begin, end, span in spans:
            lax.fori_loop(begin, end, lambda t, _: (step(t, span), 0)[1], 0)

    def own_scores(t, span):
        key_id = lax.broadcasted_iota(jnp.int32, (span, lanes_n), 0)
        token = t * TILE + (lax.broadcasted_iota(jnp.int32, (1, lanes_n), 1) & (TILE - 1))
        visible = (key_id >= lanes[t, 0:1].astype(jnp.int32)) & (key_id <= token)
        s = jnp.where(visible, dot(rk[0:span], qp[t], 1, 1) * c, -1e30)
        top = jnp.max(s, axis=0, keepdims=True)
        e = jnp.exp2(s - top)
        er[t, 0:span] = e
        rstat[t, 0:1] = top
        rstat[t, 1:2] = jnp.sum(e, axis=0, keepdims=True)

    loads["rk"].wait()
    each_tile(own_scores)
    each_peer(seq, spread, (1,))
    og_copies[0].wait_recv()
    og_copies.append(send_og(4, ogs.at[left], left, top_half, right))
    og_copies[1].wait_recv()
    og_copies.append(send_og(5, ogs.at[right], right, low_half, left))

    loads["owner"].wait()
    loads["piece"].wait()
    wait_bytes(first.at[pl.ds(0, seq - 1)], sem_in1.at[1])

    core, chip = lax.rem(me, 2), me // 2
    for kind in range(2):

        @pl.when(core == kind)
        def _():
            def deliver(p):
                order[p] = first[owner[p]]
                pltpu.make_async_remote_copy(
                    order.at[p], slots[kind].at[1, chip], sem_in2s, sem_in2.at[group],
                    device_id=at_seq(p), device_id_type=MESH,
                ).start()

            each_peer(seq, deliver)
            slots[kind][1, chip] = first[owner[me]]

    loads["og"].wait()
    loads["w"].wait()
    og_copies[2].wait_recv()
    og_copies[3].wait_recv()
    block = 256

    def w_columns(h, r):
        return w[pl.ds(r, block), pl.ds(pl.multiple_of(h * width, width), width)]

    def project_near(n, _):
        r = pl.multiple_of(n * block, block)
        total = dot(ogs[mine], w_columns(mine, r), 1, 1)
        for h in (right, left):
            total += dot(ogs[h], w_columns(h, r), 1, 1)
        ag[:, pl.ds(r, block)] = total
        return 0

    lax.fori_loop(0, feat // block, project_near, 0)

    def forward(n, kind):
        at = lax.rem(chip_group + 2 * of_kind - 1 - n, of_kind)
        g = kind * of_kind + at
        ref = slots[kind]

        @pl.when(g == group)
        def _():
            wait_bytes(ref.at[1, pl.ds(0, per - 1)], sem_in2.at[g])

        @pl.when(g != group)
        def _():
            wait_bytes(ref.at[1, pl.ds(0, per)], sem_in2.at[g])

        part = pl.ds(at * per, per)
        pltpu.make_async_remote_copy(
            ref.at[1, part], ref.at[0, part], sem_near.at[0, kind], sem_near.at[1, kind],
            device_id=at_seq(up), device_id_type=MESH,
        ).start()
        pltpu.make_async_remote_copy(
            ref.at[1, part], ref.at[2, part], sem_near.at[2, kind], sem_near.at[3, kind],
            device_id=at_seq(down), device_id_type=MESH,
        ).start()

    for n in range(of_kind):
        forward(n, 0)
    opposite = lax.rem(mine + 2, heads)
    og_copies[4].wait_recv()
    og_copies[5].wait_recv()

    def project_far(n, _):
        r = pl.multiple_of(n * block, block)
        total = (ag[:, pl.ds(r, block)] + dot(ogs[opposite], w_columns(opposite, r), 1, 1)).astype(BF16)
        for t in range(tiles):
            for h in range(block // 128):
                at = pl.multiple_of((n * (block // 128) + h) * TILE, TILE)
                gp[t, pl.ds(at, TILE)] = total[t * TILE : (t + 1) * TILE, h * 128 : (h + 1) * 128]
        return 0

    lax.fori_loop(0, feat // block, project_far, 0)
    dks[0] = jnp.zeros(dks.shape[1:], F32)
    dvs[0] = jnp.zeros(dvs.shape[1:], F32)
    for n in range(of_kind):
        forward(n, 1)
    wait_bytes(slots_k.at[0], sem_near.at[1, 0])
    wait_bytes(slots_k.at[2], sem_near.at[3, 0])

    def load_unit(n):
        t = unit[0, n]
        member = lanes[t, 1:2].astype(jnp.int32) == unit[1, n]
        stat = rstat[t]
        return dict(
            n=n, s=unit[2, n], q=qp[t], g=gp[t], member=member, same=unit[3, n] == 1,
            top=stat[0:1], total=stat[1:2], dots=stat[2:3],
        )

    def scores(u):
        u["sp"] = dot(slots_k[u["s"]].reshape(plen, 128), u["q"], 1, 1)

    def softmax(u):
        top = jnp.maximum(c * jnp.max(u["sp"], axis=0, keepdims=True), u["top"])
        e = jnp.exp2(u["sp"] * c - top)
        own = jnp.exp2(u["top"] - top)
        total = jnp.sum(e, axis=0, keepdims=True) + u["total"] * own
        inv = jnp.where(u["member"], 1.0 / total, 0.0)
        u["w"] = e * inv
        weights[u["n"]] = u["w"]
        ustat[u["n"], 0:1] = own * inv

    def value_sums(u):
        n = u["n"]
        dvs[n + 1] = jnp.where(u["same"], dvs[n], 0.0) + dot(u["w"].astype(BF16), u["g"], 1, 0)

    def value_dots(u):
        u["vp"] = dot(slots_v[u["s"]].reshape(plen, 128), u["g"], 1, 1)

    def score_grads(u):
        n = u["n"]
        wp = weights[n]
        dots = jnp.sum(wp * u["vp"], axis=0, keepdims=True) + u["dots"] * ustat[n, 0:1]
        u["gl"] = (wp * (u["vp"] - dots)).astype(BF16)
        sgrads[n] = u["gl"]
        ustat[n, 1:2] = dots

    def key_sums(u):
        n = u["n"]
        dks[n + 1] = jnp.where(u["same"], dks[n], 0.0) + dot(u["gl"], u["q"], 1, 0)

    together = 5 if units % 5 == 0 else 2

    def each_unit(*stages):
        def batch(i, _):
            some = [load_unit(together * i + n) for n in range(together)]
            for stage in stages:
                for u in some:
                    stage(u)
            return 0

        lax.fori_loop(0, units // together, batch, 0)

    def put_keys(i):
        x = jnp.where(slot_used[i], dks[slot_last[i]] * scale, 0.0)
        dslots[i, 0:half] = x.astype(BF16).reshape(half, -1, 128)

    def put_values(i):
        x = jnp.where(slot_used[i], dvs[slot_last[i]], 0.0)
        dslots[i, half:seq] = x.astype(BF16).reshape(half, -1, 128)

    def back_groups(kind):
        return [kind * of_kind + lax.rem(chip_group + n, of_kind) for n in range(of_kind)]

    def send_back(kind):
        for g in back_groups(kind):
            part = pl.ds(g * per, per)
            pltpu.make_async_remote_copy(
                dslots.at[2, part], near.at[0, part], sem_back_s.at[0], sem_back.at[0, g],
                device_id=at_seq(up), device_id_type=MESH,
            ).start()
            pltpu.make_async_remote_copy(
                dslots.at[0, part], near.at[1, part], sem_back_s.at[1], sem_back.at[1, g],
                device_id=at_seq(down), device_id_type=MESH,
            ).start()

    at_start, at_end = me == 0, me == seq - 1

    def sum_and_spread(kind):
        for g in back_groups(kind):
            part = pl.ds(g * per, per)
            wait_bytes(near.at[0, part], sem_back.at[0, g])
            wait_bytes(near.at[1, part], sem_back.at[1, g])
            below = jnp.where(at_start, 0.0, near[0, part].astype(F32))
            above = jnp.where(at_end, 0.0, near[1, part].astype(F32))
            summed[part] = (dslots[1, part].astype(F32) + below + above).astype(BF16)
            for i in range(per):
                piece = g * per + i
                j = 2 * (piece - kind * half) + kind

                @pl.when(j != me)
                def _():
                    pltpu.make_async_remote_copy(
                        summed.at[piece], second.at[me], sem_out1.at[0], sem_out1.at[1],
                        device_id=at_seq(j), device_id_type=MESH,
                    ).start()

    each_unit(scores, softmax, value_sums)

    put_values(0)
    put_values(2)
    send_back(1)
    put_values(1)
    loads["rv"].wait()

    def own_dots(t, span):
        v = dot(rv[0:span], gp[t], 1, 1)
        vr[t, 0:span] = v
        rstat[t, 2:3] = jnp.sum(v * er[t, 0:span], axis=0, keepdims=True)

    each_tile(own_dots)
    wait_bytes(slots_v.at[0], sem_near.at[1, 1])
    wait_bytes(slots_v.at[2], sem_near.at[3, 1])
    each_unit(value_dots, score_grads, key_sums)
    put_keys(0)
    put_keys(2)
    send_back(0)
    put_keys(1)
    sum_and_spread(1)

    spot = lax.broadcasted_iota(jnp.int32, inverse_row.shape, 1)
    found = jnp.zeros(inverse_row.shape, jnp.int32)
    for p in range(seq):
        found = jnp.where(spot == owner[p], p, found)
    inverse_row[...] = found
    to_scalars = pltpu.make_async_copy(inverse_row, inverse, local.at[len(loads)])
    to_scalars.start()
    for i in range(3):
        vt[i] = slots_v[i].reshape(plen, 128).T

    def unit_rows(n, _):
        ot[n] = dot(vt[unit[2, n]], weights[n].astype(BF16), 1, 0)
        return 0

    lax.fori_loop(0, units, unit_rows, 0)

    def of_tile(t, ref, row_slice=slice(None)):
        begin, many = tile_first[t], tile_count[t]
        total = ref[begin, row_slice]
        for j in range(1, 3):
            total += jnp.where(many > j, ref[jnp.minimum(begin + j, units - 1), row_slice], 0.0)
        return total

    def unit_facts(t):
        begin, many = tile_first[t], tile_count[t]
        slot = lanes[t, 1:2].astype(jnp.int32)
        factor, dots = 0.0, 0.0
        for j in range(3):
            n = jnp.minimum(begin + j, units - 1)
            member = (slot == unit[1, n]) & (many > j)
            factor += jnp.where(member, ustat[n, 0:1], 0.0)
            dots += jnp.where(member, ustat[n, 1:2], 0.0)
        return factor, dots

    rvt = rv[...].T

    def attend(t, span):
        factor, _ = unit_facts(t)
        o = of_tile(t, ot) + dot(rvt[:, 0:span], (er[t, 0:span] * factor).astype(BF16), 1, 0)
        o = o.T.astype(BF16)
        for h in range(per_group):
            att[pl.ds(pl.multiple_of(t * TILE, TILE), TILE), h * 128 : (h + 1) * 128] = o[h * TILE : (h + 1) * TILE]

    each_tile(attend)
    sum_and_spread(0)
    second[me] = summed[mine_at]

    def share(i):
        peer = lax.rem(mine + i, heads)
        return dot(att[...], w[:, pl.ds(pl.multiple_of(peer * width, width), width)], 1, 0)

    part_copies = []
    for i in range(1, heads):
        parts[i] = share(i).astype(BF16)
        copy = pltpu.make_async_remote_copy(
            parts.at[i], got.at[i], sem_parts.at[0, i], sem_parts.at[1, i],
            device_id=at_head(lax.rem(mine + i, heads)), device_id_type=MESH,
        )
        copy.start()
        part_copies.append(copy)

    to_scalars.wait()
    wait_bytes(second.at[pl.ds(0, seq - 1)], sem_out1.at[1])
    wait_bytes(order.at[pl.ds(0, seq - 1)], sem_in2s)

    def give_back(o):
        order[o] = second[inverse[0, o]]
        pltpu.make_async_remote_copy(
            order.at[o], back.at[mine_at], sem_out2.at[0], sem_out2.at[1], device_id=at_seq(o), device_id_type=MESH
        ).start()

    each_peer(seq, give_back)
    back[mine_at] = second[inverse[0, me]]

    own_part[...] = share(0)
    for i in range(3):
        kt[i] = slots_k[i].reshape(plen, 128).T

    def unit_query(n, _):
        dqt[n] = dot(kt[unit[2, n]], sgrads[n], 1, 0)
        return 0

    lax.fori_loop(0, units, unit_query, 0)
    rkt = rk[...].T
    drk_acc[...] = jnp.zeros_like(drk_acc)
    drv_acc[...] = jnp.zeros_like(drv_acc)

    def own_grads(t, span):
        factor, dots = unit_facts(t)
        wr = er[t, 0:span] * factor
        gr = (wr * (vr[t, 0:span] - dots)).astype(BF16)
        drv_acc[0:span] += dot(wr.astype(BF16), gp[t], 1, 0)
        drk_acc[0:span] += dot(gr, qp[t], 1, 0)
        d = ((of_tile(t, dqt) + dot(rkt[:, 0:span], gr, 1, 0)) * scale).T.astype(BF16)
        for h in range(per_group):
            dq[pl.ds(pl.multiple_of(t * TILE, TILE), TILE), h * 128 : (h + 1) * 128] = d[h * TILE : (h + 1) * TILE]

    each_tile(own_grads)
    drk[...] = (drk_acc[...] * scale).astype(BF16)
    drv[...] = drv_acc[...].astype(BF16)
    for copy in part_copies:
        copy.wait_recv()
    total = own_part[...]
    for i in range(1, heads):
        total += got[i].astype(F32)
    out[...] = total.astype(BF16)

    for copy in og_copies + part_copies:
        copy.wait_send()
    wait_bytes(first.at[pl.ds(0, seq - 1)], sem_in1.at[0])
    for side in (0, 2):
        wait_bytes(slots_k.at[1], sem_near.at[side, 0])
        wait_bytes(slots_v.at[1], sem_near.at[side, 1])
    wait_bytes(near.at[0], sem_back_s.at[0])
    wait_bytes(near.at[1], sem_back_s.at[1])
    wait_bytes(second.at[pl.ds(0, seq - 1)], sem_out1.at[0])
    wait_bytes(order.at[pl.ds(0, seq - 1)], sem_out2.at[0])
    wait_bytes(back.at[pl.ds(0, seq - 1)], sem_out2.at[1])
    grad[...] = back[...].astype(F32)


def store_kernel(*refs):
    many = (len(refs) - 1) // 2
    copies = [pltpu.make_async_copy(refs[i], refs[many + i], refs[-1].at[i]) for i in range(many)]
    for copy in copies:
        copy.start()
    for copy in copies:
        copy.wait()


def per_device(
    token_response, prompt_owner, queries, resp_keys, resp_values, prompt_kv, out_weight, out_grad
):
    seq, heads = lax.axis_size("seq"), lax.axis_size("head")
    vm = pl.BlockSpec(memory_space=pltpu.VMEM)
    hbm = pl.BlockSpec(memory_space=pltpu.HBM)
    pieces = prompt_kv.reshape(seq, -1, 128)
    plen = prompt_kv.shape[2]
    rows, feat = queries.shape
    width = out_grad.shape[1]
    tiles = rows // TILE
    units = tiles + 2
    lanes = TILE * feat // 128
    wide = -(-seq // 128) * 128
    groups = max(2, seq // 8)
    dma = pltpu.SemaphoreType.DMA
    shapes = (
        jax.ShapeDtypeStruct((rows, width), BF16),
        jax.ShapeDtypeStruct(queries.shape, BF16),
        jax.ShapeDtypeStruct(resp_keys.shape, BF16),
        jax.ShapeDtypeStruct(resp_values.shape, BF16),
        jax.ShapeDtypeStruct(pieces.shape, F32),
    )
    operands = (
        token_response, token_response.reshape(1, rows), prompt_owner, queries, resp_keys, resp_values,
        pieces, out_grad, out_weight,
    )
    results = pl.pallas_call(
        functools.partial(layer_kernel, seq, heads),
        out_shape=shapes,
        in_specs=[hbm] * len(operands),
        out_specs=(vm,) * len(shapes),
        scratch_shapes=[
            pltpu.SMEM((rows,), jnp.int32),
            pltpu.SMEM((seq,), jnp.int32),
            pltpu.SMEM((1, wide), jnp.int32),
            pltpu.SMEM((4, units), jnp.int32),
            pltpu.SMEM((tiles,), jnp.int32),
            pltpu.SMEM((tiles,), jnp.int32),
            pltpu.VMEM((1, rows), jnp.int32),
            pltpu.VMEM(queries.shape, BF16),
            pltpu.VMEM(resp_keys.shape, BF16),
            pltpu.VMEM(resp_values.shape, BF16),
            pltpu.VMEM(out_weight.shape, BF16),
            pltpu.VMEM((heads, rows, width), BF16),
            pltpu.VMEM(pieces.shape, BF16),
            pltpu.VMEM(pieces.shape, BF16),
            pltpu.VMEM((3, seq // 2) + pieces.shape[1:], BF16),
            pltpu.VMEM((3, seq // 2) + pieces.shape[1:], BF16),
            pltpu.VMEM((tiles, 16, lanes), F32),
            pltpu.VMEM(queries.shape, F32),
            pltpu.VMEM((tiles, lanes, 128), BF16),
            pltpu.VMEM((tiles, lanes, 128), BF16),
            pltpu.VMEM((tiles, rows, lanes), F32),
            pltpu.VMEM((tiles, rows, lanes), F32),
            pltpu.VMEM((tiles, 8, lanes), F32),
            pltpu.VMEM((units, plen, lanes), F32),
            pltpu.VMEM((units, plen, lanes), BF16),
            pltpu.VMEM((units, 8, lanes), F32),
            pltpu.VMEM((units + 1, plen, 128), F32),
            pltpu.VMEM((units + 1, plen, 128), F32),
            pltpu.VMEM((3,) + pieces.shape, BF16),
            pltpu.VMEM((2,) + pieces.shape, BF16),
            pltpu.VMEM(pieces.shape, BF16),
            pltpu.VMEM(pieces.shape, BF16),
            pltpu.VMEM(pieces.shape, BF16),
            pltpu.VMEM((1, wide), jnp.int32),
            pltpu.VMEM((3, 128, plen), BF16),
            pltpu.VMEM((3, 128, plen), BF16),
            pltpu.VMEM((units, 128, lanes), F32),
            pltpu.VMEM((units, 128, lanes), F32),
            pltpu.VMEM(queries.shape, BF16),
            pltpu.VMEM(resp_keys.shape, F32),
            pltpu.VMEM(resp_keys.shape, F32),
            pltpu.VMEM((heads, rows, width), BF16),
            pltpu.VMEM((heads, rows, width), BF16),
            pltpu.VMEM((rows, width), F32),
            dma((2,)),
            dma,
            dma((groups,)),
            dma((4, 2)),
            dma((2, 6)),
            dma((10,)),
            dma((2,)),
            dma((2, groups)),
            dma((2,)),
            dma((2,)),
            dma((2, heads)),
        ],
        compiler_params=pltpu.CompilerParams(
            collective_id=0, has_side_effects=True, vmem_limit_bytes=VMEM_LIMIT
        ),
        name="layer",
    )(*(in_hbm(x) for x in operands))
    layer_out, query_grad, key_grad, value_grad, prompt_grad = pl.pallas_call(
        store_kernel,
        out_shape=shapes,
        in_specs=[vm] * len(shapes),
        out_specs=(hbm,) * len(shapes),
        scratch_shapes=[dma((len(shapes),))],
        compiler_params=pltpu.CompilerParams(vmem_limit_bytes=4 * 2**20),
        name="store",
    )(*results)
    return (layer_out, query_grad, key_grad, value_grad, prompt_grad.reshape(prompt_kv.shape))


def solution(mesh):
    placed = (
        P("seq"),
        P(),
        P("seq", "head"),
        P("seq", "head"),
        P("seq", "head"),
        P("seq", None, None, "head"),
        P("head", None),
        P("seq", "head"),
    )
    return jax.shard_map(
        per_device,
        mesh=mesh,
        in_specs=placed,
        out_specs=(
            P("seq", "head"),
            P("seq", "head"),
            P("seq", "head"),
            P("seq", "head"),
            P("seq", None, None, "head"),
        ),
        check_vma=False,
    )
```
